32 devices in a mesh: seq: 16 (over z, x, core), fsdp: 2 (over y).
Axes of the slice: x: 2, y: 2, z: 4, core: 2. Of those that a mesh axis runs over, the one named last changes fastest.
Arguments:
- tokens: bfloat16 [16, 2048, 768], P('fsdp', 'seq'), may hold values from -6 to 6
- positions: int32 [16, 2048], P('fsdp'), may hold values from 0 to 2047, as said below
- qkv_weight: bfloat16 [768, 2304], P('fsdp'), may hold values from -0.3125 to 0.3125
- out_weight: bfloat16 [768, 768], P('fsdp'), may hold values from -1.75 to 1.75
- in_weight: bfloat16 [768, 2304], P('fsdp'), may hold values from -0.21875 to 0.21875
- down_weight: bfloat16 [1152, 768], P('fsdp'), may hold values from -0.3125 to 0.3125
- norm_gains: bfloat16 [2, 768], P(None, 'fsdp'), may hold values from 0.5 to 1.5
- cotangent: bfloat16 [16, 2048, 768], P('fsdp', 'seq'), may hold values from -6 to 6
Outputs:
- layer_out: bfloat16 [16, 2048, 768], P('fsdp', 'seq')
- grad_tokens: bfloat16 [16, 2048, 768], P('fsdp', 'seq')
- grad_qkv: float32 [768, 2304], P('fsdp')
- grad_out: float32 [768, 768], P('fsdp')
- grad_in: float32 [768, 2304], P('fsdp')
- grad_down: float32 [1152, 768], P('fsdp')
- grad_gains: float32 [2, 768], P(None, 'fsdp')
The draws below stay inside these ranges and needn't reach their ends.
Inputs may be any that keep to these rules, and one draw needn't show every extreme that they name: In each row, positions count up by one from token to token and fall back to 0 where a document begins; every row starts at 0. Of each aligned block of 8 rows, one row is a single document.
All inputs are finite; a program needn't handle non-finite values.
Results may differ from the reference program's by a relative error of at most 0.015.
The reference program's roundings to bfloat16 on the way count: a program that leaves them out, or rounds other values in their place, can miss the bound.
Values may be sent and summed in bfloat16 or wider, within the bound.
No kernel may reach another device: no remote copies, remote signals or barrier semaphores. Data moves between devices by JAX's collectives and lax.ppermute only.
A program may use at most 192 MiB of HBM per device.

```python
from functools import partial
import jax
import jax.numpy as jnp
from jax import lax

HEADS = 12
HEAD_DIM = 64
FF = 1152
HALF_WINDOW = 64
BLK = 128
SEQ_DEV = 8
D = 768
LENGTH = 2048
SEQS = 16


def draw_positions(key, part):
    key = jax.random.fold_in(key, 11)
    flag_key, whole_key = jax.random.split(key)
    spacing = max(2, BLK * 4)
    starts = jax.random.randint(flag_key, (SEQS, LENGTH), 0, spacing) == 0
    chosen = jax.random.randint(whole_key, (SEQS // SEQ_DEV,), 0, SEQ_DEV)
    row_ids = jnp.arange(SEQS, dtype=jnp.int32)
    single = row_ids % SEQ_DEV == chosen[row_ids // SEQ_DEV]
    column = jnp.arange(LENGTH, dtype=jnp.int32)
    starts = starts & jnp.logical_not(single)[:, None] | (column[None, :] == 0)
    marks = jnp.where(starts, column[None, :], 0)
    return (column[None, :] - lax.cummax(marks, axis=1)).astype(jnp.int32)


def block_levels(rng, shape, cuts, low, high):
    level = 1.0
    for position, shards_of in cuts:
        draws = jax.random.uniform(jax.random.fold_in(jax.random.fold_in(rng, 6), position), (shards_of,), jnp.float32, low / len(cuts), high / len(cuts))
        level = level * jnp.repeat(jnp.exp(draws), shape[position] // shards_of).reshape((-1,) + (1,) * (len(shape) - 1 - position))
    return level


def noise(rng, extent, width, bound, cuts=(), kind=jnp.bfloat16):
    array = jax.random.normal(rng, extent, jnp.float32) * width
    if len(cuts) > 0:
        array = block_levels(rng, extent, cuts, -0.22, 0.18) * array
    return jnp.clip(array, min=-bound, max=bound).astype(kind)


def setup_inputs(seed: int = 0) -> dict:
    arg_keys = jax.random.split(jax.random.key(seed), 9)
    return {
        "tokens": noise(arg_keys[0], (SEQS, LENGTH, D), 1.0, 6.0, ((0, 2), (1, 16))),
        "positions": draw_positions(jax.random.fold_in(arg_keys[8], 71), 0),
        "qkv_weight": noise(arg_keys[2], (D, 3 * D), (D // 2) ** -0.5, 0.3125, ((0, 2),)),
        "out_weight": noise(arg_keys[3], (D, D), (max(1, D // 64)) ** -0.5, 1.75, ((0, 2),)),
        "in_weight": noise(arg_keys[4], (D, 2 * FF), D ** -0.5, 0.21875, ((0, 2),)),
        "down_weight": noise(arg_keys[5], (FF, D), (FF // 3) ** -0.5, 0.3125, ((0, 2),)),
        "norm_gains": jnp.clip(1.0 + 0.1 * jax.random.normal(arg_keys[6], (2, D), jnp.float32), 0.5, 1.5).astype(jnp.bfloat16),
        "cotangent": noise(arg_keys[7], (SEQS, LENGTH, D), 1.0, 6.0, ((0, 2), (1, 16))),
    }


@jax.custom_vjp
def low(v):
    return lax.optimization_barrier(v.astype(jnp.bfloat16)).astype(jnp.float32)

@jax.custom_vjp
def low_back(v):
    return v

def low_keep(v):
    return (low(v), None)

def low_pass(kept, grad):
    return (grad,)

def back_keep(v):
    return (v, None)

def back_low(kept, grad):
    return (low(grad),)
low.defvjp(low_keep, low_pass)
low_back.defvjp(back_keep, back_low)
masked_score = -1000000000.0
norm_epsilon = 1e-05
highest = lax.Precision.HIGHEST

def layer_norm(values, gain):
    center = values - lax.optimization_barrier(jnp.mean(values, -1, keepdims=True))
    return center * lax.rsqrt(lax.optimization_barrier(jnp.mean(center * center, -1, keepdims=True)) + norm_epsilon) * gain

def rotary_tables(pos, head_width):
    half = head_width // 2
    freqs = 10000.0 ** (-(jnp.arange(half, dtype=jnp.float32) * 2.0 / head_width))
    angle = pos.astype(jnp.float32)[..., None] * freqs
    return (jnp.cos(angle)[..., None, :], jnp.sin(angle)[..., None, :])

def rotate_heads(values, cosine, sine):
    half = values.shape[-1] // 2
    first = values[..., :half]
    second = values[..., half:]
    return jnp.concatenate([first * cosine - second * sine, second * cosine + first * sine], -1)

def window_mask(query_pos, key_pos, rows, half_span):
    offsets = jnp.arange(rows + 2 * half_span, dtype=jnp.int32)[None, :] - half_span - jnp.arange(rows, dtype=jnp.int32)[:, None]
    query_col = query_pos[..., :, None]
    key_row = key_pos[..., None, :]
    return (jnp.abs(offsets) <= half_span) & (key_row >= 0) & ((offsets > 0) | (query_col >= -offsets)) & ((offsets <= 0) | (key_row >= offsets))

def attention(query, keys, values, pos):
    length = query.shape[0]
    rows = 512 if length % 512 == 0 else length
    count = length // rows
    span = rows + 2 * HALF_WINDOW
    keys_pad = jnp.pad(keys, ((HALF_WINDOW, HALF_WINDOW), (0, 0), (0, 0)))
    values_pad = jnp.pad(values, ((HALF_WINDOW, HALF_WINDOW), (0, 0), (0, 0)))
    pos_pad = jnp.pad(pos, (HALF_WINDOW, HALF_WINDOW), constant_values=-1)

    def one_block(index):
        start = (index * rows).astype(jnp.int32)
        query_blk = lax.dynamic_slice_in_dim(query, start, rows, 0)
        keys_blk = lax.dynamic_slice_in_dim(keys_pad, start, span, 0)
        values_blk = lax.dynamic_slice_in_dim(values_pad, start, span, 0)
        query_pos = lax.dynamic_slice_in_dim(pos, start, rows, 0)
        key_pos = lax.dynamic_slice_in_dim(pos_pad, start, span, 0)
        scores = jnp.einsum('ihd,jhd->hij', query_blk, keys_blk, precision=highest) * HEAD_DIM ** (-0.5)
        allowed = window_mask(query_pos, key_pos, rows, HALF_WINDOW)
        scores = low_back(jnp.where(allowed[None], scores, masked_score))
        probs = low(jax.nn.softmax(scores, axis=-1))
        return jnp.einsum('hij,jhd->ihd', probs, values_blk, precision=highest).reshape(rows, D)
    blocks = lax.map(jax.checkpoint(one_block), jnp.arange(count, dtype=jnp.int32))
    return blocks.reshape(length, D)

def sequence_layer(stream, pos, qkv_w, out_w, in_w, down_w, gains):
    length = stream.shape[0]
    normed_one = low(layer_norm(stream, gains[0]))
    qkv = low_back(jnp.dot(normed_one, qkv_w, precision=highest))
    cosine, sine = rotary_tables(pos, HEAD_DIM)
    query = low(rotate_heads(qkv[:, :D].reshape(length, HEADS, HEAD_DIM), cosine, sine))
    keys = low(rotate_heads(qkv[:, D:2 * D].reshape(length, HEADS, HEAD_DIM), cosine, sine))
    values = low(qkv[:, 2 * D:].reshape(length, HEADS, HEAD_DIM))
    mixed = low_back(low(attention(query, keys, values, pos)))
    after_attn = stream + low_back(jnp.dot(mixed, out_w, precision=highest))
    normed_two = low(layer_norm(after_attn, gains[1]))
    up_proj = low_back(jnp.dot(normed_two, in_w, precision=highest))
    middle = low(jax.nn.gelu(up_proj[:, :FF], approximate=False) * up_proj[:, FF:])
    return after_attn + low_back(jnp.dot(middle, down_w, precision=highest))

def layer_all(positions, stream, qkv_w, out_w, in_w, down_w, gains):
    return lax.map(lambda item: sequence_layer(item[0], item[1], qkv_w, out_w, in_w, down_w, gains), (stream, positions))

def reference(tokens, positions, qkv_weight, out_weight, in_weight, down_weight, norm_gains, cotangent):
    inputs = (tokens.astype(jnp.float32), qkv_weight.astype(jnp.float32), out_weight.astype(jnp.float32), in_weight.astype(jnp.float32), down_weight.astype(jnp.float32), norm_gains.astype(jnp.float32))
    result, pull = jax.vjp(partial(layer_all, positions), *inputs)
    grads = pull(cotangent.astype(jnp.float32))
    return (result.astype(jnp.bfloat16), grads[0].astype(jnp.bfloat16), grads[1], grads[2], grads[3], grads[4], grads[5])
```

```python
import jax
import jax.numpy as jnp
from jax import lax
from jax.sharding import PartitionSpec as P

HEAD_DIM = 64
HALF_WINDOW = 64


masked_score = -1000000000.0
norm_epsilon = 1e-05


def with_halo(value, sides, width):
    for axis, dim in sides:
        size, length = (lax.axis_size(axis), value.shape[dim])
        up = [(i, (i + 1) % size) for i in range(size - 1)]
        down = [(j, i) for i, j in up]
        last = lax.slice_in_dim(value, length - width, length, axis=dim)
        leading = lax.slice_in_dim(value, 0, width, axis=dim)
        before = lax.ppermute(last, axis, up)
        after = lax.ppermute(leading, axis, down)
        value = jnp.concatenate([before, value, after], axis=dim)
    return value


def passed_along(block, axis, distance):
    devices = range(lax.axis_size(axis))
    route = [(i - distance, i) for i in devices if i - distance in devices]
    return lax.ppermute(block, axis, route)


def norm_parts(values):
    center = values - jnp.mean(values, -1, keepdims=True)
    factor = lax.rsqrt(jnp.mean(center * center, -1, keepdims=True) + norm_epsilon)
    return (center * factor, factor)


def norm_back(grad_normed, normed, factor):
    first = jnp.mean(grad_normed, -1, keepdims=True)
    second = jnp.mean(grad_normed * normed, -1, keepdims=True)
    return factor * (grad_normed - first - normed * second)


def rotary_tables(pos, head_width):
    half = head_width // 2
    freqs = 10000.0 ** (-(jnp.arange(half, dtype=jnp.float32) * 2.0 / head_width))
    angle = pos.astype(jnp.float32)[..., None] * freqs
    return (jnp.cos(angle)[..., None, :], jnp.sin(angle)[..., None, :])


def rotate_heads(values, cosine, sine):
    half = values.shape[-1] // 2
    first = values[..., :half]
    second = values[..., half:]
    return jnp.concatenate([first * cosine - second * sine, second * cosine + first * sine], -1)


def rotate_back(grads, cosine, sine):
    half = grads.shape[-1] // 2
    first = grads[..., :half]
    second = grads[..., half:]
    return jnp.concatenate([first * cosine + second * sine, second * cosine - first * sine], -1)


def window_mask(query_pos, key_pos, rows, half_span):
    offsets = (
        jnp.arange(rows + 2 * half_span, dtype=jnp.int32)[None, :]
        - half_span
        - jnp.arange(rows, dtype=jnp.int32)[:, None]
    )
    query_col = query_pos[..., :, None]
    key_row = key_pos[..., None, :]
    return (
        (jnp.abs(offsets) <= half_span)
        & (key_row >= 0)
        & ((offsets > 0) | (query_col >= -offsets))
        & ((offsets <= 0) | (key_row >= offsets))
    )


def weight_grad(left, right):
    left_rows = left.reshape(-1, left.shape[-1])
    right_rows = right.reshape(-1, right.shape[-1])
    return lax.dot_general(
        left_rows, right_rows, (((0,), (0,)), ((), ())), preferred_element_type=jnp.float32
    )


def through_weight(grads, weight):
    return lax.dot_general(
        grads, weight, (((grads.ndim - 1,), (1,)), ((), ())), preferred_element_type=jnp.float32
    )


def flip_route(size, bit):
    return [(i, i ^ bit) for i in range(size)]


def gather_shards(shards):
    own_y = lax.axis_index("fsdp")
    core = lax.axis_index("seq") % 2
    seq = lax.axis_size("seq")
    wholes = []
    for shard in shards:
        rows = shard.shape[0]
        half = rows // 2
        mine = lax.dynamic_slice_in_dim(shard, core * half, half, 0)
        far = lax.ppermute(mine, "fsdp", flip_route(2, 1))
        near = lax.ppermute(far, "seq", flip_route(seq, 1))
        other = jnp.where(
            core == 0, jnp.concatenate([far, near], 0), jnp.concatenate([near, far], 0)
        )
        wholes.append(
            jnp.where(
                own_y == 0,
                jnp.concatenate([shard, other], 0),
                jnp.concatenate([other, shard], 0),
            )
        )
    return wholes


def keep_and_send(block, bit, dim):
    half = block.shape[dim] // 2
    keep = lax.dynamic_slice_in_dim(block, bit * half, half, dim)
    send = lax.dynamic_slice_in_dim(block, (1 - bit) * half, half, dim)
    return keep, send


def exchange(block, stage):
    if stage < 0:
        return lax.ppermute(block, "fsdp", flip_route(2, 1))
    return lax.ppermute(block, "seq", flip_route(lax.axis_size("seq"), 1 << stage))


def stage_bit(stage):
    if stage < 0:
        return lax.axis_index("fsdp")
    return (lax.axis_index("seq") >> stage) & 1


def reduce_stage(block, stage):
    keep, send = keep_and_send(block, stage_bit(stage), 0 if stage < 0 else 1)
    got = exchange(send.astype(jnp.bfloat16), stage)
    return (keep.astype(jnp.float32) + got.astype(jnp.float32)).astype(jnp.bfloat16)


def summed_half(bundle):
    stages = (lax.axis_size("seq") - 1).bit_length()
    width = bundle.shape[2] // 2
    bundle = jnp.pad(bundle, ((0, 0), (0, -bundle.shape[1] % lax.axis_size("seq")), (0, 0)))
    bundle = reduce_stage(bundle, 0)
    parts = [bundle[:, :, :width], bundle[:, :, width:]]
    orders = [[-1] + list(range(1, stages)), [1, -1] + list(range(2, stages))]
    for step in range(stages):
        parts = [reduce_stage(part, order[step]) for part, order in zip(parts, orders)]
    parts = [part[0] for part in parts]
    for stage in reversed(range(stages)):
        if stage == 0:
            parts = [jnp.concatenate(parts, 1)]
        bit = stage_bit(stage)
        got = [exchange(part, stage) for part in parts]
        parts = [
            jnp.where(bit == 0, jnp.concatenate([p, g], 0), jnp.concatenate([g, p], 0))
            for p, g in zip(parts, got)
        ]
    return parts[0]


def summed_small(value):
    stages = (lax.axis_size("seq") - 1).bit_length()
    for stage in range(-1, stages):
        value = value + exchange(value, stage)
    return value


def fold_rows(block, width):
    count = width // block.shape[2]
    rows = block.shape[1] // count
    return jnp.concatenate([block[:, i * rows : (i + 1) * rows] for i in range(count)], 2)


def unfold_rows(block, width):
    count = block.shape[1] // width
    return jnp.concatenate([block[:, i * width : (i + 1) * width] for i in range(count)], 0)


def local(tokens, positions, qkv_weight, out_weight, in_weight, down_weight, norm_gains, cotangent):
    num_seqs, tok_block, model_width = tokens.shape
    head_width = HEAD_DIM
    head_count = model_width // head_width
    half_span = HALF_WINDOW
    span = tok_block + 2 * half_span
    scale = head_width ** (-0.5)
    gains_other = lax.ppermute(norm_gains, "fsdp", flip_route(2, 1))
    gains = jnp.where(
        lax.axis_index("fsdp") == 0,
        jnp.concatenate([norm_gains, gains_other], 1),
        jnp.concatenate([gains_other, norm_gains], 1),
    )
    w_qkv, w_out, w_in, w_down = gather_shards([qkv_weight, out_weight, in_weight, down_weight])
    ffn_width = w_in.shape[1] // 2
    gain_one = gains[0].astype(jnp.float32)
    gain_two = gains[1].astype(jnp.float32)
    stream = tokens.astype(jnp.float32)
    normed_one, factor_one = norm_parts(stream)
    hidden_one = (normed_one * gain_one).astype(jnp.bfloat16)
    qkv = jnp.dot(hidden_one, w_qkv, preferred_element_type=jnp.float32)
    block_index = lax.axis_index("seq")
    padded_pos = jnp.pad(positions, ((0, 0), (half_span, half_span)), constant_values=-1)
    key_pos = lax.dynamic_slice_in_dim(padded_pos, block_index * tok_block, span, 1)
    own_pos = key_pos[:, half_span : half_span + tok_block]
    cosine, sine = rotary_tables(own_pos, head_width)
    head_shape = (num_seqs, tok_block, head_count, head_width)
    query = rotate_heads(qkv[..., :model_width].reshape(head_shape), cosine, sine).astype(
        jnp.bfloat16
    )
    keys = rotate_heads(qkv[..., model_width : 2 * model_width].reshape(head_shape), cosine, sine)
    keys = keys.astype(jnp.bfloat16).reshape(num_seqs, tok_block, model_width)
    values = qkv[..., 2 * model_width :].astype(jnp.bfloat16)
    edges = with_halo(jnp.concatenate([keys, values], -1), (("seq", 1),), half_span)
    ext_shape = (num_seqs, span, head_count, head_width)
    key_ext = edges[..., :model_width].reshape(ext_shape)
    value_ext = edges[..., model_width:].reshape(ext_shape)
    allowed = window_mask(own_pos, key_pos, tok_block, half_span)

    def banded_scores(query_heads):
        raw = (
            jnp.einsum("gihd,gjhd->ghij", query_heads, key_ext, preferred_element_type=jnp.float32)
            * scale
        )
        return jnp.where(allowed[:, None], raw, masked_score)

    scores = banded_scores(query)
    row_top = jnp.max(scores, -1, keepdims=True)
    expo = jnp.exp(scores - row_top)
    row_total = jnp.sum(expo, -1, keepdims=True)
    log_total = row_top + jnp.log(row_total)
    probs = (expo / row_total).astype(jnp.bfloat16)
    mixed = jnp.einsum("ghij,gjhd->gihd", probs, value_ext, preferred_element_type=jnp.float32)
    mixed = mixed.reshape(num_seqs, tok_block, model_width).astype(jnp.bfloat16)
    after_attn = stream + jnp.dot(mixed, w_out, preferred_element_type=jnp.float32)
    normed_two, factor_two = norm_parts(after_attn)
    hidden_two = (normed_two * gain_two).astype(jnp.bfloat16)
    up_proj = jnp.dot(hidden_two, w_in, preferred_element_type=jnp.float32)
    act_input = up_proj[..., :ffn_width]
    gate_part = up_proj[..., ffn_width:]
    act_value, gelu_pull = jax.vjp(lambda value: jax.nn.gelu(value, approximate=False), act_input)
    middle = (act_value * gate_part).astype(jnp.bfloat16)
    layer_out = after_attn + jnp.dot(middle, w_down, preferred_element_type=jnp.float32)
    grad_down = weight_grad(middle, cotangent)
    grad_middle = through_weight(cotangent, w_down)
    grad_act = gelu_pull(grad_middle * gate_part)[0]
    grad_up = jnp.concatenate([grad_act, grad_middle * act_value], -1).astype(jnp.bfloat16)
    grad_in = weight_grad(hidden_two, grad_up)
    grad_hidden_two = through_weight(grad_up, w_in)
    gain_grad_two = jnp.sum((grad_hidden_two * normed_two).reshape(-1, model_width), 0)
    grad_stream = cotangent.astype(jnp.float32) + norm_back(
        grad_hidden_two * gain_two, normed_two, factor_two
    )
    grad_attn = grad_stream.astype(jnp.bfloat16)
    grad_out = weight_grad(mixed, grad_attn)
    grad_mixed = through_weight(grad_attn, w_out).astype(jnp.bfloat16).reshape(head_shape)
    again = jnp.exp(banded_scores(query) - log_total)
    grad_values = jnp.einsum(
        "ghij,gihd->gjhd",
        again.astype(jnp.bfloat16),
        grad_mixed,
        preferred_element_type=jnp.float32,
    )
    grad_probs = jnp.einsum(
        "gihd,gjhd->ghij", grad_mixed, value_ext, preferred_element_type=jnp.float32
    )
    inner_sum = jnp.sum(grad_probs * again, -1, keepdims=True)
    grad_scores = (again * (grad_probs - inner_sum)).astype(jnp.bfloat16)
    grad_query = (
        jnp.einsum("ghij,gjhd->gihd", grad_scores, key_ext, preferred_element_type=jnp.float32)
        * scale
    )
    grad_keys = (
        jnp.einsum("ghij,gihd->gjhd", grad_scores, query, preferred_element_type=jnp.float32)
        * scale
    )
    grad_edges = jnp.concatenate(
        [
            grad_keys.reshape(num_seqs, span, model_width),
            grad_values.reshape(num_seqs, span, model_width),
        ],
        -1,
    )
    from_next = passed_along(grad_edges[:, :half_span].astype(jnp.bfloat16), "seq", -1).astype(
        jnp.float32
    )
    from_prev = passed_along(grad_edges[:, tok_block + half_span :], "seq", 1)
    grad_own = grad_edges[:, half_span : half_span + tok_block]
    grad_own = (
        grad_own
        + jnp.pad(from_prev, ((0, 0), (0, tok_block - half_span), (0, 0)))
        + jnp.pad(from_next, ((0, 0), (tok_block - half_span, 0), (0, 0)))
    )
    grad_key_own = rotate_back(grad_own[..., :model_width].reshape(head_shape), cosine, sine)
    grad_query_raw = rotate_back(grad_query, cosine, sine)
    grad_qkv_all = jnp.concatenate(
        [
            grad_query_raw.reshape(num_seqs, tok_block, model_width),
            grad_key_own.reshape(num_seqs, tok_block, model_width),
            grad_own[..., model_width:],
        ],
        -1,
    ).astype(jnp.bfloat16)
    grad_qkv = weight_grad(hidden_one, grad_qkv_all)
    grad_hidden_one = through_weight(grad_qkv_all, w_qkv)
    gain_grad_one = jnp.sum((grad_hidden_one * normed_one).reshape(-1, model_width), 0)
    grad_tokens = grad_stream + norm_back(grad_hidden_one * gain_one, normed_one, factor_one)
    grad_gains = jnp.stack([gain_grad_one, gain_grad_two])
    qkv_sum = summed_half(grad_qkv.reshape(2, -1, grad_qkv.shape[1]))
    wide = grad_in.shape[1]
    bundle = jnp.concatenate(
        [
            grad_in.reshape(2, -1, wide),
            fold_rows(grad_down.reshape(2, -1, model_width), wide),
            fold_rows(grad_out.reshape(2, -1, model_width), wide),
        ],
        1,
    )
    bundle_sum = summed_half(bundle)
    in_rows = in_weight.shape[0]
    down_rows = down_weight.shape[0] * model_width // wide
    in_sum = bundle_sum[:in_rows]
    down_sum = unfold_rows(bundle_sum[in_rows : in_rows + down_rows], model_width)
    out_sum = unfold_rows(
        bundle_sum[in_rows + down_rows : in_rows + down_rows + out_weight.shape[0] * model_width // wide],
        model_width,
    )
    gains_sum = lax.dynamic_slice_in_dim(
        summed_small(grad_gains), lax.axis_index("fsdp") * norm_gains.shape[1], norm_gains.shape[1], 1
    )
    pieces = tuple(
        total.astype(jnp.float32) for total in (qkv_sum, out_sum, in_sum, down_sum, gains_sum)
    )
    return (
        layer_out.astype(jnp.bfloat16),
        grad_tokens.astype(jnp.bfloat16),
        pieces[0],
        pieces[1],
        pieces[2],
        pieces[3],
        pieces[4],
    )


def solution(mesh):
    in_specs = (
        P("fsdp", "seq", None),
        P("fsdp", None),
        P("fsdp", None),
        P("fsdp", None),
        P("fsdp", None),
        P("fsdp", None),
        P(None, "fsdp"),
        P("fsdp", "seq", None),
    )
    out_specs = (
        P("fsdp", "seq", None),
        P("fsdp", "seq", None),
        P("fsdp", None),
        P("fsdp", None),
        P("fsdp", None),
        P("fsdp", None),
        P(None, "fsdp"),
    )
    return jax.shard_map(local, mesh=mesh, in_specs=in_specs, out_specs=out_specs, check_vma=False)
```

```python
import jax
import jax.numpy as jnp
from jax import lax
from jax.experimental import pallas as pl
from jax.experimental.pallas import tpu as pltpu
from jax.sharding import PartitionSpec as P

HEAD_DIM = 64
HALF_WINDOW = 64
PAIR = 128
HEAD_ROWS = 16
MIB = 1 << 20


masked_score = -1000000000.0
norm_epsilon = 1e-05
root_half = 0.7071067811865476
normal_peak = 0.3989422804014327
f32 = jnp.float32
bf16 = jnp.bfloat16


def passed_along(block, axis, distance):
    devices = range(lax.axis_size(axis))
    route = [(i - distance, i) for i in devices if i - distance in devices]
    return lax.ppermute(block, axis, route)


def norm_parts(values):
    center = values - jnp.mean(values, -1, keepdims=True)
    factor = lax.rsqrt(jnp.mean(center * center, -1, keepdims=True) + norm_epsilon)
    return (center * factor, factor)


def norm_back(grad_normed, normed, factor):
    first = jnp.mean(grad_normed, -1, keepdims=True)
    second = jnp.mean(grad_normed * normed, -1, keepdims=True)
    return factor * (grad_normed - first - normed * second)


def dot(left, right):
    return jnp.dot(left, right, preferred_element_type=f32)


def dot_right(left, right):
    return lax.dot_general(left, right, (((1,), (1,)), ((), ())), preferred_element_type=f32)


def dot_left(left, right):
    return lax.dot_general(left, right, (((0,), (0,)), ((), ())), preferred_element_type=f32)


def half_swap(value, first_half):
    return jnp.where(first_half, pltpu.roll(value, PAIR - 32, 1), pltpu.roll(value, 32, 1))


def place_weight(place_ref, whole, own, far, near):
    rows = own.shape[0]
    half = rows // 2
    index, core = place_ref[0], place_ref[1]
    other = (1 - index) * rows
    whole[pl.ds(pl.multiple_of(index * rows, half), rows), :] = own[...]
    whole[pl.ds(pl.multiple_of(other + core * half, half), half), :] = far[...]
    whole[pl.ds(pl.multiple_of(other + (1 - core) * half, half), half), :] = near[...]


def attend_kernel(
    place_ref, before, own, after, cos_ref, sin_ref, bias_ref, gain_ref, w_own, w_far, w_near,
    h1_ref, q_ref, k_ref, v_ref, mix_ref, lse_ref, weight,
):
    @pl.when(pl.program_id(0) == 0)
    def _():
        place_weight(place_ref, weight, w_own, w_far, w_near)

    width = own.shape[2]
    rows = own.shape[1]
    span = rows + 2 * HALF_WINDOW
    stream = jnp.concatenate([before[0], own[0], after[0]], 0).astype(f32)
    normed, _ = norm_parts(stream)
    hidden = (normed * gain_ref[0:1, :].astype(f32)).astype(bf16)
    h1_ref[0] = hidden[HALF_WINDOW : HALF_WINDOW + rows]
    lane = lax.broadcasted_iota(jnp.int32, (1, PAIR), 1)
    first_half = (lane % HEAD_DIM) < HEAD_DIM // 2
    first_head = lane < HEAD_DIM
    cosine, sine = cos_ref[0], sin_ref[0]
    for start in range(0, 3 * width, 2 * PAIR):
        part = dot(hidden, weight[:, start : start + 2 * PAIR])
        for sub in range(0, 2 * PAIR, PAIR):
            value = part[:, sub : sub + PAIR]
            column = (start + sub) % width
            if start + sub < 2 * width:
                value = value * cosine + half_swap(value, first_half) * sine
            if start + sub < width:
                q_ref[0, :, column : column + PAIR] = (value * HEAD_DIM**-0.5).astype(bf16)
            elif start + sub < 2 * width:
                k_ref[0, :, column : column + PAIR] = value.astype(bf16)
            else:
                v_ref[0, :, column : column + PAIR] = value.astype(bf16)
    bias = bias_ref[0]
    bias = jnp.concatenate([bias, bias], 0)
    log_totals = jnp.zeros((rows, PAIR), f32)
    for pair in range(width // PAIR):
        columns = slice(pair * PAIR, (pair + 1) * PAIR)
        query = q_ref[0, HALF_WINDOW : HALF_WINDOW + rows, columns]
        zero = jnp.zeros_like(query)
        both = jnp.concatenate(
            [jnp.where(first_head, query, zero), jnp.where(first_head, zero, query)], 0
        )
        scores = dot_right(both, k_ref[0, :, columns]) + bias
        top = jnp.max(scores, -1, keepdims=True)
        expo = jnp.exp(scores - top)
        total = jnp.sum(expo, -1, keepdims=True)
        log_total = top + jnp.log(total)
        probs = (expo * (1.0 / total)).astype(bf16)
        mixed = dot(probs, v_ref[0, :, columns])
        mix_ref[0, :, columns] = jnp.where(first_head, mixed[:rows], mixed[rows:]).astype(bf16)
        log_totals = jnp.where(lane == 2 * pair, log_total[:rows], log_totals)
        log_totals = jnp.where(lane == 2 * pair + 1, log_total[rows:], log_totals)
    lse_ref[0] = jnp.transpose(log_totals)[:HEAD_ROWS]


def feed_kernel(
    place_ref, tok_ref, mix_ref, dy_ref, gain_ref,
    out_own, out_far, out_near, in_own, in_far, in_near, down_own, down_far, down_near,
    layer_ref, dx1_ref, do_ref, lo_ref, hi_ref, delta_ref, h2_ref, dup_ref, mid_ref, dmix_ref, gsum_ref,
    w_out, w_in, w_down,
):
    @pl.when(pl.program_id(0) == 0)
    def _():
        place_weight(place_ref, w_out, out_own, out_far, out_near)
        place_weight(place_ref, w_in, in_own, in_far, in_near)
        place_weight(place_ref, w_down, down_own, down_far, down_near)
        gsum_ref[...] = jnp.zeros_like(gsum_ref)

    rows, width = tok_ref.shape
    ffn = w_down.shape[0]
    block = 2 * HALF_WINDOW
    after_attn = tok_ref[...].astype(f32) + dot(mix_ref[...], w_out[...])
    normed, factor = norm_parts(after_attn)
    gain = gain_ref[1:2, :].astype(f32)
    h2_ref[...] = (normed * gain).astype(bf16)
    step = 3 * PAIR
    for start in range(0, ffn, step):
        columns = slice(start, start + step)
        gates = slice(ffn + start, ffn + start + step)
        act_input = dot(h2_ref[...], w_in[:, columns])
        gate_part = dot(h2_ref[...], w_in[:, gates])
        grad_middle = dot_right(dy_ref[...], w_down[columns, :])
        share = 0.5 + 0.5 * lax.erf(act_input * root_half)
        act_value = act_input * share
        slope = share + act_input * (normal_peak * jnp.exp(-0.5 * act_input * act_input))
        mid_ref[:, columns] = (act_value * gate_part).astype(bf16)
        dup_ref[:, columns] = (grad_middle * gate_part * slope).astype(bf16)
        dup_ref[:, gates] = (grad_middle * act_value).astype(bf16)
    layer_ref[...] = (after_attn + dot(mid_ref[...], w_down[...])).astype(bf16)
    grad_hidden = dot_right(dup_ref[...], w_in[...])
    gain_terms = grad_hidden * normed
    gsum_ref[...] += jnp.sum(gain_terms.reshape(rows // 8, 8, width), 0)
    grad_stream = dy_ref[...].astype(f32) + norm_back(grad_hidden * gain, normed, factor)
    dx1_ref[...] = grad_stream
    dmix_ref[...] = grad_stream.astype(bf16)
    grad_mixed = dot_right(dmix_ref[...], w_out[...]).astype(bf16)
    do_ref[...] = grad_mixed
    products = grad_mixed.astype(f32) * mix_ref[...].astype(f32)
    high = products.astype(bf16)
    low = (products - high.astype(f32)).astype(bf16)
    head_of = lax.broadcasted_iota(jnp.int32, (width, PAIR), 0) // HEAD_DIM
    slot = lax.broadcasted_iota(jnp.int32, (width, PAIR), 1)
    pick = jnp.where(head_of == slot, 1.0, 0.0).astype(bf16)
    delta = dot(high, pick) + dot(low, pick)
    for i in range(rows // block):
        piece = grad_mixed[i * block : (i + 1) * block]
        lo_ref[i] = piece[:HALF_WINDOW]
        hi_ref[i] = piece[HALF_WINDOW:]
        delta_ref[i] = jnp.transpose(delta[i * block : (i + 1) * block])[:HEAD_ROWS]


def grads_kernel(h2_ref, dup_ref, mid_ref, dy_ref, mix_ref, dmix_ref, out_ref):
    step = pl.program_id(0)
    width = dy_ref.shape[1]
    half = out_ref.shape[0] // 2
    part = width // 2
    ffn_rows = mid_ref.shape[1]
    ffn_part = 3 * ffn_rows // 2
    grad = dot_left(h2_ref[...], dup_ref[...]).astype(bf16)
    at = pl.multiple_of(step * part, part)
    out_ref[pl.ds(at, part), :] = grad[:part]
    out_ref[pl.ds(half + at, part), :] = grad[part:]
    grad = dot_left(mid_ref[...], dy_ref[...]).astype(bf16)
    third = ffn_rows // 2
    for i in range(2):
        index = 2 * step + i
        owner = index // 3
        at = pl.multiple_of(owner * half + 3 * part + (index - 3 * owner) * third, 64)
        out_ref[pl.ds(at, third), :] = grad[i * third : (i + 1) * third]
    grad = dot_left(mix_ref[...], dmix_ref[...]).astype(bf16)
    columns = pl.ds(pl.multiple_of(step * (width // 3), PAIR), width // 3)
    at = 3 * part + ffn_part
    out_ref[at : at + part, columns] = grad[:part]
    out_ref[half + at : half + at + part, columns] = grad[part:]


def attend_back_kernel(
    q_ref, k_ref, v_ref, do_ref, do_before, do_after, lse_ref, lse_edge, delta_ref, delta_edge,
    bias_ref, bias_edge, cos_ref, sin_ref, out_ref,
):
    rows, width = do_ref.shape[1], do_ref.shape[2]
    inner = slice(HALF_WINDOW, HALF_WINDOW + rows)
    lane = lax.broadcasted_iota(jnp.int32, (1, PAIR), 1)
    first_half = (lane % HEAD_DIM) < HEAD_DIM // 2
    first_head = lane < HEAD_DIM
    top_rows = lax.broadcasted_iota(jnp.int32, (PAIR, 1), 0) < HEAD_DIM
    cosine, sine = cos_ref[0, inner], sin_ref[0, inner]
    bias = jnp.concatenate([bias_ref[0], bias_ref[0]], 1)
    edge = jnp.concatenate([bias_edge[0], bias_edge[0]], 1)

    def split(value):
        zero = jnp.zeros_like(value)
        return jnp.concatenate(
            [jnp.where(first_head, value, zero), jnp.where(first_head, zero, value)], 0
        )

    def row_of(ref, pair):
        return jnp.concatenate(
            [ref[0, 2 * pair : 2 * pair + 1, :], ref[0, 2 * pair + 1 : 2 * pair + 2, :]], 1
        )

    def back(keys, values, query, grad_mixed, offsets, log_total, inner_sum):
        probs = jnp.exp(dot_right(keys, query) + offsets - log_total)
        grad_probs = dot_right(values, grad_mixed)
        return probs.astype(bf16), (probs * (grad_probs - inner_sum)).astype(bf16)

    def rotated_back(value):
        return value * cosine - half_swap(value, first_half) * sine

    for pair in range(width // PAIR):
        columns = slice(pair * PAIR, (pair + 1) * PAIR)
        keys, values = k_ref[0, :, columns], v_ref[0, :, columns]
        query = split(q_ref[0, inner, columns])
        grad_mixed = split(do_ref[0, :, columns])
        probs, grad_scores = back(
            keys, values, query, grad_mixed, bias, row_of(lse_ref, pair), row_of(delta_ref, pair)
        )
        query_edge = split(
            jnp.concatenate(
                [
                    q_ref[0, HALF_WINDOW + rows :, columns],
                    q_ref[0, :HALF_WINDOW, columns],
                ],
                0,
            )
        )
        grad_edge = split(jnp.concatenate([do_after[0, :, columns], do_before[0, :, columns]], 0))
        probs_edge, scores_edge = back(
            keys[inner], values[inner], query_edge, grad_edge, edge,
            row_of(lse_edge, pair), row_of(delta_edge, pair),
        )
        grad_values = dot(
            jnp.concatenate([probs[inner], probs_edge], 1),
            jnp.concatenate([grad_mixed, grad_edge], 0),
        )
        grad_keys = dot(
            jnp.concatenate([grad_scores[inner], scores_edge], 1),
            jnp.concatenate([query, query_edge], 0),
        )
        grad_query = dot_left(grad_scores, keys)
        grad_query = jnp.where(first_head, grad_query[:rows], grad_query[rows:]) * HEAD_DIM**-0.5
        out_ref[0, :, columns] = rotated_back(grad_query).astype(bf16)
        out_ref[0, :, width + pair * PAIR : width + (pair + 1) * PAIR] = rotated_back(
            grad_keys
        ).astype(bf16)
        out_ref[0, :, 2 * width + pair * PAIR : 2 * width + (pair + 1) * PAIR] = (
            grad_values.astype(bf16)
        )


def grad_qkv_kernel(h1_ref, dqkv_ref, out_ref):
    out_ref[...] = dot_left(h1_ref[...], dqkv_ref[...]).astype(bf16)


def stream_back_kernel(
    place_ref, dqkv_ref, tok_ref, dx1_ref, gain_ref, w_own, w_far, w_near, out_ref, gsum_ref, weight
):
    @pl.when(pl.program_id(0) == 0)
    def _():
        place_weight(place_ref, weight, w_own, w_far, w_near)
        gsum_ref[...] = jnp.zeros_like(gsum_ref)

    rows, width = tok_ref.shape
    grad_hidden = dot_right(dqkv_ref[...], weight[...])
    normed, factor = norm_parts(tok_ref[...].astype(f32))
    gsum_ref[...] += jnp.sum((grad_hidden * normed).reshape(rows // 8, 8, width), 0)
    grad_normed = grad_hidden * gain_ref[0:1, :].astype(f32)
    out_ref[...] = (dx1_ref[...] + norm_back(grad_normed, normed, factor)).astype(bf16)


def shape_of(*dims, dtype=bf16):
    return jax.ShapeDtypeStruct(dims, dtype)


def whole_spec(array):
    return pl.BlockSpec(array.shape, lambda i: (0,) * array.ndim)


def run(kernel, grid, inputs, outputs, scratch=(), flops=0, whole=()):
    def spec(block, place):
        return pl.BlockSpec(block, place)

    specs = []
    for item in inputs:
        if item[1] is None and item[0].dtype == jnp.int32:
            specs.append(pl.BlockSpec(memory_space=pltpu.SMEM))
        elif item[1] is None:
            specs.append(whole_spec(item[0]))
        else:
            specs.append(spec(item[1], item[2]))
    out_specs = [whole_spec(o[0]) if o[1] is None else spec(o[1], o[2]) for o in outputs]
    moved = sum(x[0].size * x[0].dtype.itemsize for x in list(inputs) + list(outputs))
    return pl.pallas_call(
        kernel,
        grid=(grid,),
        in_specs=specs,
        out_specs=out_specs,
        out_shape=[o[0] for o in outputs],
        scratch_shapes=list(scratch),
        cost_estimate=pl.CostEstimate(flops=flops, bytes_accessed=moved, transcendentals=0),
        compiler_params=pltpu.CompilerParams(
            dimension_semantics=("arbitrary",), vmem_limit_bytes=56 * MIB
        ),
    )(*[x[0] for x in inputs])


def flip_route(size, bit):
    return [(i, i ^ bit) for i in range(size)]


def fetch_shards(shards):
    core = lax.axis_index("seq") % 2
    seq = lax.axis_size("seq")
    pieces = []
    for shard in shards:
        half = shard.shape[0] // 2
        mine = lax.dynamic_slice_in_dim(shard, core * half, half, 0)
        far = lax.ppermute(mine, "fsdp", flip_route(2, 1))
        near = lax.ppermute(far, "seq", flip_route(seq, 1))
        pieces.append((shard, far, near))
    return pieces


def keep_and_send(block, bit, dim):
    half = block.shape[dim] // 2
    keep = lax.dynamic_slice_in_dim(block, bit * half, half, dim)
    send = lax.dynamic_slice_in_dim(block, (1 - bit) * half, half, dim)
    return keep, send


def exchange(block, stage):
    if stage < 0:
        return lax.ppermute(block, "fsdp", flip_route(2, 1))
    return lax.ppermute(block, "seq", flip_route(lax.axis_size("seq"), 1 << stage))


def stage_bit(stage):
    if stage < 0:
        return lax.axis_index("fsdp")
    return (lax.axis_index("seq") >> stage) & 1


def reduce_stage(block, stage):
    keep, send = keep_and_send(block, stage_bit(stage), 0 if stage < 0 else 1)
    got = exchange(send.astype(jnp.bfloat16), stage)
    return (keep.astype(jnp.float32) + got.astype(jnp.float32)).astype(jnp.bfloat16)


def summed_half(bundle):
    stages = (lax.axis_size("seq") - 1).bit_length()
    width = bundle.shape[2] // 2
    bundle = jnp.pad(bundle, ((0, 0), (0, -bundle.shape[1] % lax.axis_size("seq")), (0, 0)))
    bundle = reduce_stage(bundle, 0)
    parts = [bundle[:, :, :width], bundle[:, :, width:]]
    orders = [[-1] + list(range(1, stages)), [1, -1] + list(range(2, stages))]
    for step in range(stages):
        parts = [reduce_stage(part, order[step]) for part, order in zip(parts, orders)]
    parts = [part[0] for part in parts]
    for stage in reversed(range(stages)):
        if stage == 0:
            parts = [jnp.concatenate(parts, 1)]
        bit = stage_bit(stage)
        got = [exchange(part, stage) for part in parts]
        parts = [
            jnp.where(bit == 0, jnp.concatenate([p, g], 0), jnp.concatenate([g, p], 0))
            for p, g in zip(parts, got)
        ]
    return parts[0]


def summed_small(value):
    stages = (lax.axis_size("seq") - 1).bit_length()
    for stage in range(-1, stages):
        value = value + exchange(value, stage)
    return value


def window_tables(pos, rows, head_width):
    half = head_width // 2
    freqs = 10000.0 ** (-(jnp.arange(half, dtype=f32) * 2.0 / head_width))
    angle = pos.astype(f32)[..., None] * freqs
    cosine, sine = jnp.cos(angle), jnp.sin(angle)
    cosine = jnp.concatenate([cosine] * 4, -1)
    sine = jnp.concatenate([-sine, sine, -sine, sine], -1)
    span = pos.shape[1]
    index = jnp.arange(span, dtype=jnp.int32)

    def offsets(query_pos, query_index, key_pos, key_index):
        gap = key_index - query_index
        allowed = (
            (jnp.abs(gap) <= HALF_WINDOW)
            & (key_pos >= 0)
            & (query_pos >= 0)
            & ((gap > 0) | (query_pos >= -gap))
            & ((gap <= 0) | (key_pos >= gap))
        )
        return jnp.where(allowed, 0.0, masked_score).astype(f32)

    inner = slice(HALF_WINDOW, HALF_WINDOW + rows)
    outer_pos = jnp.concatenate([pos[:, HALF_WINDOW + rows :], pos[:, :HALF_WINDOW]], 1)
    outer_index = jnp.concatenate([index[HALF_WINDOW + rows :], index[:HALF_WINDOW]])
    bias = offsets(
        pos[:, inner, None], index[None, inner, None], pos[:, None, :], index[None, None, :]
    )
    bias_t = offsets(
        pos[:, None, inner], index[None, None, inner], pos[:, :, None], index[None, :, None]
    )
    bias_edge = offsets(
        outer_pos[:, None, :],
        outer_index[None, None, :],
        pos[:, inner, None],
        index[None, inner, None],
    )
    return cosine, sine, bias, bias_t, bias_edge


def local(tokens, positions, qkv_weight, out_weight, in_weight, down_weight, norm_gains, cotangent):
    num_seqs, rows, width = tokens.shape
    span = rows + 2 * HALF_WINDOW
    count = num_seqs * rows
    ffn = 2 * down_weight.shape[0]
    seq_index, own_y = lax.axis_index("seq"), lax.axis_index("fsdp")
    place = jnp.stack([own_y, seq_index % 2]).astype(jnp.int32)
    tok_before = passed_along(tokens[:, rows - HALF_WINDOW :], "seq", 1)
    tok_after = passed_along(tokens[:, :HALF_WINDOW], "seq", -1)
    gains_other = lax.ppermute(norm_gains, "fsdp", flip_route(2, 1))
    gains = jnp.where(
        own_y == 0,
        jnp.concatenate([norm_gains, gains_other], 1),
        jnp.concatenate([gains_other, norm_gains], 1),
    )
    w_qkv, w_out, w_in, w_down = fetch_shards([qkv_weight, out_weight, in_weight, down_weight])
    padded_pos = jnp.pad(positions, ((0, 0), (HALF_WINDOW, HALF_WINDOW)), constant_values=-1)
    key_pos = lax.dynamic_slice_in_dim(padded_pos, seq_index * rows, span, 1)
    cosine, sine, bias, bias_t, bias_edge = window_tables(key_pos, rows, HEAD_DIM)

    def per_seq(i):
        return (i, 0, 0)

    def row_block(i):
        return (i, 0)

    def column_block(i):
        return (0, i)

    qkv_pieces = [(piece, None) for piece in w_qkv]
    wide = (1, span, width)
    hidden_one, query, keys, values, mixed, log_total = run(
        attend_kernel,
        num_seqs,
        [
            (place, None),
            (tok_before, (1, HALF_WINDOW, width), per_seq),
            (tokens, (1, rows, width), per_seq),
            (tok_after, (1, HALF_WINDOW, width), per_seq),
            (cosine, (1, span, PAIR), per_seq),
            (sine, (1, span, PAIR), per_seq),
            (bias, (1, rows, span), per_seq),
            (gains, None),
            *qkv_pieces,
        ],
        [
            (shape_of(num_seqs, rows, width), (1, rows, width), per_seq),
            (shape_of(num_seqs, span, width), wide, per_seq),
            (shape_of(num_seqs, span, width), wide, per_seq),
            (shape_of(num_seqs, span, width), wide, per_seq),
            (shape_of(num_seqs, rows, width), (1, rows, width), per_seq),
            (shape_of(num_seqs, HEAD_ROWS, PAIR, dtype=f32), (1, HEAD_ROWS, PAIR), per_seq),
        ],
        [pltpu.VMEM((width, 3 * width), bf16)],
        flops=2 * num_seqs * span * width * 3 * width,
    )
    lse_before = passed_along(log_total, "seq", 1)
    lse_after = passed_along(log_total, "seq", -1)

    flat_tokens = tokens.reshape(count, width)
    flat_dy = cotangent.reshape(count, width)
    flat_mixed = mixed.reshape(count, width)
    step = 2 * rows
    tok_block = (step, width)
    half_block = (2, HALF_WINDOW, width)
    (
        layer_out, grad_stream, grad_mixed, grad_lo, grad_hi, inner_sum,
        hidden_two, grad_up, middle, grad_attn, gain_sum_two,
    ) = run(
        feed_kernel,
        count // step,
        [
            (place, None),
            (flat_tokens, tok_block, row_block),
            (flat_mixed, tok_block, row_block),
            (flat_dy, tok_block, row_block),
            (gains, None),
            *[(piece, None) for piece in (*w_out, *w_in, *w_down)],
        ],
        [
            (shape_of(count, width), tok_block, row_block),
            (shape_of(count, width, dtype=f32), tok_block, row_block),
            (shape_of(count, width), tok_block, row_block),
            (shape_of(num_seqs, HALF_WINDOW, width), half_block, per_seq),
            (shape_of(num_seqs, HALF_WINDOW, width), half_block, per_seq),
            (shape_of(num_seqs, HEAD_ROWS, PAIR, dtype=f32), (2, HEAD_ROWS, PAIR), per_seq),
            (shape_of(count, width), tok_block, row_block),
            (shape_of(count, 2 * ffn), (step, 2 * ffn), row_block),
            (shape_of(count, ffn), (step, ffn), row_block),
            (shape_of(count, width), tok_block, row_block),
            (shape_of(8, width, dtype=f32), None),
        ],
        [
            pltpu.VMEM((width, width), bf16),
            pltpu.VMEM((width, 2 * ffn), bf16),
            pltpu.VMEM((ffn, width), bf16),
        ],
        flops=2 * count * width * (2 * width + 4 * ffn + 2 * ffn),
    )
    do_before = passed_along(grad_hi, "seq", 1)
    do_after = passed_along(grad_lo, "seq", -1)
    sum_before = passed_along(inner_sum, "seq", 1)
    sum_after = passed_along(inner_sum, "seq", -1)

    bundle_rows = 2 * (3 * width // 2 + ffn // 2 + width // 2)
    (bundle,) = run(
        grads_kernel,
        3,
        [
            (hidden_two, None),
            (grad_up, (count, 2 * ffn // 3), column_block),
            (middle, (count, ffn // 3), column_block),
            (flat_dy, None),
            (flat_mixed, None),
            (grad_attn, (count, width // 3), column_block),
        ],
        [(shape_of(bundle_rows, width), None)],
        flops=2 * count * width * (3 * ffn + width),
    )
    bundle_sum = summed_half(bundle.reshape(2, bundle_rows // 2, width))

    after_lane = (jnp.arange(PAIR) < HALF_WINDOW)[None, None]
    lse_edge = jnp.where(after_lane, lse_after, lse_before)
    sum_edge = jnp.where(after_lane, sum_after, sum_before)
    half = (1, HALF_WINDOW, width)
    heads = (1, HEAD_ROWS, PAIR)
    (grad_qkv_all,) = run(
        attend_back_kernel,
        num_seqs,
        [
            (query, wide, per_seq),
            (keys, wide, per_seq),
            (values, wide, per_seq),
            (grad_mixed.reshape(num_seqs, rows, width), (1, rows, width), per_seq),
            (do_before, half, per_seq),
            (do_after, half, per_seq),
            (log_total, heads, per_seq),
            (lse_edge, heads, per_seq),
            (inner_sum, heads, per_seq),
            (sum_edge, heads, per_seq),
            (bias_t, (1, span, rows), per_seq),
            (bias_edge, (1, rows, PAIR), per_seq),
            (cosine, (1, span, PAIR), per_seq),
            (sine, (1, span, PAIR), per_seq),
        ],
        [(shape_of(num_seqs, rows, 3 * width), (1, rows, 3 * width), per_seq)],
        flops=2 * num_seqs * (width // PAIR) * 7 * 256 * 256 * 128,
    )
    flat_grad = grad_qkv_all.reshape(count, 3 * width)
    (grad_qkv,) = run(
        grad_qkv_kernel,
        3,
        [
            (hidden_one.reshape(count, width), None),
            (flat_grad, (count, width), column_block),
        ],
        [(shape_of(width, 3 * width), (width, width), column_block)],
        flops=2 * count * width * 3 * width,
    )
    qkv_sum = summed_half(grad_qkv.reshape(2, width // 2, 3 * width))
    grad_tokens, gain_sum_one = run(
        stream_back_kernel,
        count // step,
        [
            (place, None),
            (flat_grad, (step, 3 * width), row_block),
            (flat_tokens, tok_block, row_block),
            (grad_stream, tok_block, row_block),
            (gains, None),
            *qkv_pieces,
        ],
        [
            (shape_of(count, width), tok_block, row_block),
            (shape_of(8, width, dtype=f32), None),
        ],
        [pltpu.VMEM((width, 3 * width), bf16)],
        flops=2 * count * width * 3 * width,
    )
    gain_sums = summed_small(jnp.stack([jnp.sum(gain_sum_one, 0), jnp.sum(gain_sum_two, 0)]))
    gain_width = norm_gains.shape[1]
    part = in_weight.shape[0]
    in_sum = jnp.concatenate([bundle_sum[i * part : (i + 1) * part] for i in range(3)], 1)
    down_rows = down_weight.shape[0]
    down_sum = bundle_sum[3 * part : 3 * part + down_rows]
    out_sum = bundle_sum[3 * part + down_rows : 4 * part + down_rows]
    return (
        layer_out.reshape(tokens.shape),
        grad_tokens.reshape(tokens.shape),
        qkv_sum.astype(f32),
        out_sum.astype(f32),
        in_sum.astype(f32),
        down_sum.astype(f32),
        lax.dynamic_slice_in_dim(gain_sums, own_y * gain_width, gain_width, 1),
    )


def solution(mesh):
    in_specs = (
        P("fsdp", "seq", None),
        P("fsdp", None),
        P("fsdp", None),
        P("fsdp", None),
        P("fsdp", None),
        P("fsdp", None),
        P(None, "fsdp"),
        P("fsdp", "seq", None),
    )
    out_specs = (
        P("fsdp", "seq", None),
        P("fsdp", "seq", None),
        P("fsdp", None),
        P("fsdp", None),
        P("fsdp", None),
        P("fsdp", None),
        P(None, "fsdp"),
    )
    return jax.shard_map(local, mesh=mesh, in_specs=in_specs, out_specs=out_specs, check_vma=False)
```

```python
from functools import partial

import jax
import jax.numpy as jnp
from jax import lax
from jax.experimental import pallas as pl
from jax.experimental.pallas import tpu as pltpu
from jax.sharding import PartitionSpec as P

HEAD_DIM = 64
HALF_WINDOW = 64
PAIR = 128
HEAD_ROWS = 16
MIB = 1 << 20


masked_score = -1000000000.0
norm_epsilon = 1e-05
root_half = 0.7071067811865476
normal_peak = 0.3989422804014327
f32 = jnp.float32
bf16 = jnp.bfloat16


def passed_along(block, axis, distance):
    devices = range(lax.axis_size(axis))
    route = [(i - distance, i) for i in devices if i - distance in devices]
    return lax.ppermute(block, axis, route)


def norm_parts(values):
    center = values - jnp.mean(values, -1, keepdims=True)
    factor = lax.rsqrt(jnp.mean(center * center, -1, keepdims=True) + norm_epsilon)
    return (center * factor, factor)


def norm_back(grad_normed, normed, factor):
    first = jnp.mean(grad_normed, -1, keepdims=True)
    second = jnp.mean(grad_normed * normed, -1, keepdims=True)
    return factor * (grad_normed - first - normed * second)


def dot(left, right):
    return jnp.dot(left, right, preferred_element_type=f32)


def dot_right(left, right):
    return lax.dot_general(left, right, (((1,), (1,)), ((), ())), preferred_element_type=f32)


def dot_left(left, right):
    return lax.dot_general(left, right, (((0,), (0,)), ((), ())), preferred_element_type=f32)


def half_swap(value, first_half):
    return jnp.where(first_half, pltpu.roll(value, PAIR - 32, 1), pltpu.roll(value, 32, 1))


def place_weight(place_ref, whole, own, far, near):
    rows = own.shape[0]
    half = rows // 2
    index, core = place_ref[0], place_ref[1]
    other = (1 - index) * rows
    whole[pl.ds(pl.multiple_of(index * rows, half), rows), :] = own[...]
    whole[pl.ds(pl.multiple_of(other + core * half, half), half), :] = far[:half]
    whole[pl.ds(pl.multiple_of(other + (1 - core) * half, half), half), :] = near[:half]


def place_folded(place_ref, whole, own, far, near, at):
    rows, width = own.shape
    third = rows // 6
    index, core = place_ref[0], place_ref[1]
    other = (1 - index) * rows
    whole[pl.ds(pl.multiple_of(index * rows, third), rows), :] = own[...]
    for i in range(3):
        columns = slice(i * width, (i + 1) * width)
        first = other + core * 3 * third + i * third
        whole[pl.ds(pl.multiple_of(first, third), third), :] = far[at : at + third, columns]
        first = other + (1 - core) * 3 * third + i * third
        whole[pl.ds(pl.multiple_of(first, third), third), :] = near[at : at + third, columns]


def attend_kernel(
    place_ref, before, own, after, cos_ref, sin_ref, bias_ref, gain_ref, w_own, w_far, w_near,
    h1_ref, q_ref, k_ref, v_ref, mix_ref, lse_ref, weight,
):
    @pl.when(pl.program_id(0) == 0)
    def _():
        place_weight(place_ref, weight, w_own, w_far, w_near)

    width = own.shape[2]
    rows = own.shape[1]
    span = rows + 2 * HALF_WINDOW
    stream = jnp.concatenate([before[0], own[0], after[0]], 0).astype(f32)
    normed, _ = norm_parts(stream)
    hidden = (normed * gain_ref[0:1, :].astype(f32)).astype(bf16)
    h1_ref[0] = hidden[HALF_WINDOW : HALF_WINDOW + rows]
    lane = lax.broadcasted_iota(jnp.int32, (1, PAIR), 1)
    first_half = (lane % HEAD_DIM) < HEAD_DIM // 2
    first_head = lane < HEAD_DIM
    cosine, sine = cos_ref[0], sin_ref[0]
    for start in range(0, 3 * width, 2 * PAIR):
        part = dot(hidden, weight[:, start : start + 2 * PAIR])
        for sub in range(0, 2 * PAIR, PAIR):
            value = part[:, sub : sub + PAIR]
            column = (start + sub) % width
            if start + sub < 2 * width:
                value = value * cosine + half_swap(value, first_half) * sine
            if start + sub < width:
                q_ref[0, :, column : column + PAIR] = (value * HEAD_DIM**-0.5).astype(bf16)
            elif start + sub < 2 * width:
                k_ref[0, :, column : column + PAIR] = value.astype(bf16)
            else:
                v_ref[0, :, column : column + PAIR] = value.astype(bf16)
    bias = bias_ref[0]
    bias = jnp.concatenate([bias, bias], 0)
    log_totals = jnp.zeros((rows, PAIR), f32)
    for pair in range(width // PAIR):
        columns = slice(pair * PAIR, (pair + 1) * PAIR)
        query = q_ref[0, HALF_WINDOW : HALF_WINDOW + rows, columns]
        zero = jnp.zeros_like(query)
        both = jnp.concatenate(
            [jnp.where(first_head, query, zero), jnp.where(first_head, zero, query)], 0
        )
        scores = dot_right(both, k_ref[0, :, columns]) + bias
        top = jnp.max(scores, -1, keepdims=True)
        expo = jnp.exp(scores - top)
        total = jnp.sum(expo, -1, keepdims=True)
        log_total = top + jnp.log(total)
        probs = (expo * (1.0 / total)).astype(bf16)
        mixed = dot(probs, v_ref[0, :, columns])
        mix_ref[0, :, columns] = jnp.where(first_head, mixed[:rows], mixed[rows:]).astype(bf16)
        log_totals = jnp.where(lane == 2 * pair, log_total[:rows], log_totals)
        log_totals = jnp.where(lane == 2 * pair + 1, log_total[rows:], log_totals)
    lse_ref[0] = jnp.transpose(log_totals)[:HEAD_ROWS]


def three_parts(value):
    parts = []
    for _ in range(3):
        parts.append(value.astype(bf16))
        value = value - parts[-1].astype(f32)
    return parts


def feed_kernel(
    place_ref, tok_ref, mix_ref, dy_ref, lse_ref, gain_ref,
    out_own, in_own, down_own, far_ref, near_ref,
    layer_ref, dx1_ref, do_ref, lo_ref, hi_ref, rows_ref, h2_ref, dup_ref, mid_ref, dmix_ref, gsum_ref,
    w_out, w_in, w_down,
):
    @pl.when(pl.program_id(0) == 0)
    def _():
        at = in_own.shape[0] // 2
        place_weight(place_ref, w_in, in_own, far_ref, near_ref)
        for whole, own in ((w_down, down_own), (w_out, out_own)):
            place_folded(place_ref, whole, own, far_ref, near_ref, at)
            at += own.shape[0] // 6
        gsum_ref[...] = jnp.zeros_like(gsum_ref)

    rows, width = tok_ref.shape
    ffn = w_down.shape[0]
    block = 2 * HALF_WINDOW
    after_attn = tok_ref[...].astype(f32) + dot(mix_ref[...], w_out[...])
    normed, factor = norm_parts(after_attn)
    gain = gain_ref[1:2, :].astype(f32)
    h2_ref[...] = (normed * gain).astype(bf16)
    step = 3 * PAIR
    for start in range(0, ffn, step):
        columns = slice(start, start + step)
        gates = slice(ffn + start, ffn + start + step)
        act_input = dot(h2_ref[...], w_in[:, columns])
        gate_part = dot(h2_ref[...], w_in[:, gates])
        grad_middle = dot_right(dy_ref[...], w_down[columns, :])
        share = 0.5 + 0.5 * lax.erf(act_input * root_half)
        act_value = act_input * share
        slope = share + act_input * (normal_peak * jnp.exp(-0.5 * act_input * act_input))
        mid_ref[:, columns] = (act_value * gate_part).astype(bf16)
        dup_ref[:, columns] = (grad_middle * gate_part * slope).astype(bf16)
        dup_ref[:, gates] = (grad_middle * act_value).astype(bf16)
    layer_ref[...] = (after_attn + dot(mid_ref[...], w_down[...])).astype(bf16)
    grad_hidden = dot_right(dup_ref[...], w_in[...])
    gain_terms = grad_hidden * normed
    gsum_ref[...] += jnp.sum(gain_terms.reshape(rows // 8, 8, width), 0)
    grad_stream = dy_ref[...].astype(f32) + norm_back(grad_hidden * gain, normed, factor)
    dx1_ref[...] = grad_stream
    dmix_ref[...] = grad_stream.astype(bf16)
    grad_mixed = dot_right(dmix_ref[...], w_out[...]).astype(bf16)
    do_ref[...] = grad_mixed
    products = grad_mixed.astype(f32) * mix_ref[...].astype(f32)
    high = products.astype(bf16)
    low = (products - high.astype(f32)).astype(bf16)
    head_of = lax.broadcasted_iota(jnp.int32, (width, PAIR), 0) // HEAD_DIM
    slot = lax.broadcasted_iota(jnp.int32, (width, PAIR), 1)
    pick = jnp.where(head_of == slot, 1.0, 0.0).astype(bf16)
    delta = dot(high, pick) + dot(low, pick)
    for i in range(rows // block):
        piece = grad_mixed[i * block : (i + 1) * block]
        inner_sum = jnp.transpose(delta[i * block : (i + 1) * block])[:HEAD_ROWS]
        rows_ref[i, :HEAD_ROWS] = inner_sum
        rows_ref[i, HEAD_ROWS:] = lse_ref[i]
        parts = jnp.concatenate(three_parts(lse_ref[i]) + three_parts(inner_sum), 1)
        for ref, own in ((lo_ref, piece[:HALF_WINDOW]), (hi_ref, piece[HALF_WINDOW:])):
            ref[i, :HALF_WINDOW] = own
            ref[i, HALF_WINDOW:] = parts


def pack_first_kernel(place_ref, qkv_ref, gain_ref, out_ref):
    half = qkv_ref.shape[0] // 2
    count, width = gain_ref.shape
    out_ref[:half] = qkv_ref[pl.ds(pl.multiple_of(place_ref[1] * half, half), half), :]
    out_ref[half:] = jnp.zeros_like(out_ref[half:])
    filler = jnp.zeros((out_ref.shape[0] - half - count, width), bf16)
    out_ref[half:, :width] = jnp.concatenate([gain_ref[...], filler], 0)


def pack_later_kernel(place_ref, out_w, in_w, down_w, tok_ref, later_ref, head_ref, tail_ref):
    core = place_ref[1]
    half = in_w.shape[0] // 2
    width = out_w.shape[1]
    later_ref[:half] = in_w[pl.ds(pl.multiple_of(core * half, half), half), :]
    at = half
    for ref in (down_w, out_w):
        third = ref.shape[0] // 6
        for i in range(3):
            first = pl.multiple_of((core * 3 + i) * third, third)
            later_ref[at : at + third, i * width : (i + 1) * width] = ref[pl.ds(first, third), :]
        at += third
    rows = tok_ref.shape[1]
    for i in range(tok_ref.shape[0]):
        head_ref[i] = tok_ref[i, :HALF_WINDOW]
        tail_ref[i] = tok_ref[i, rows - HALF_WINDOW :]


def part_rows(place_ref, whole, keep_ref, send_ref):
    rows = keep_ref.shape[1]
    core = place_ref[1]
    for i in range(2):
        keep_ref[i] = whole[pl.ds(pl.multiple_of((2 * i + core) * rows, 16), rows), :]
        send_ref[i] = whole[pl.ds(pl.multiple_of((2 * i + 1 - core) * rows, 16), rows), :]


def as_column(row_groups):
    ones = jnp.ones((row_groups.shape[0], PAIR), bf16)
    return sum(dot_left(part, ones) for part in three_parts(row_groups))


def grad_qkv_kernel(place_ref, left_ref, right_ref, one_ref, two_ref, keep_ref, send_ref, whole):
    step = pl.program_id(0)
    whole[...] = dot_left(left_ref[...], right_ref[...]).astype(bf16)

    @pl.when(step == pl.num_programs(0) - 1)
    def _():
        lane = lax.broadcasted_iota(jnp.int32, (1, PAIR), 1)
        first, second = as_column(one_ref[...]), as_column(two_ref[...])
        columns = jnp.where(lane == 0, first, jnp.where(lane == 1, second, 0.0)).astype(bf16)
        at = whole.shape[1] - 2 * PAIR
        whole[:, at : at + PAIR] = columns
        whole[:, at + PAIR :] = jnp.zeros_like(columns)

    part_rows(place_ref, whole, keep_ref, send_ref)


def grads_kernel(place_ref, h2_ref, dup_ref, mid_ref, dy_ref, mix_ref, dmix_ref, keep_ref, send_ref, whole):
    step = pl.program_id(0)
    width = dy_ref.shape[1]
    half = whole.shape[0] // 2
    part = width // 2
    third = mid_ref.shape[1] // 2
    grad = dot_left(h2_ref[...], dup_ref[...]).astype(bf16)
    at = pl.multiple_of(step * part, part)
    whole[pl.ds(at, part), :] = grad[:part]
    whole[pl.ds(half + at, part), :] = grad[part:]
    grad = dot_left(mid_ref[...], dy_ref[...]).astype(bf16)
    for i in range(2):
        index = 2 * step + i
        owner = index // 3
        at = pl.multiple_of(owner * half + 3 * part + (index - 3 * owner) * third, 64)
        whole[pl.ds(at, third), :] = grad[i * third : (i + 1) * third]
    grad = dot_left(mix_ref[...], dmix_ref[...]).astype(bf16)
    columns = pl.ds(pl.multiple_of(step * (width // 3), PAIR), width // 3)
    at = 3 * part + 3 * third
    whole[at : at + part, columns] = grad[:part]
    whole[half + at : half + at + part, columns] = grad[part:]

    @pl.when(step == pl.num_programs(0) - 1)
    def _():
        spare = half - at - part
        if spare:
            for start in (at + part, half + at + part):
                whole[start : start + spare] = jnp.zeros((spare, width), bf16)
        part_rows(place_ref, whole, keep_ref, send_ref)


def total_of(*values):
    total = values[0].astype(f32)
    for value in values[1:]:
        total += value.astype(f32)
    return total.astype(bf16)


def split_first_kernel(place_ref, held, got, hold_y, send_y, hold_x, send_x):
    owner, bit = place_ref[0], place_ref[2]
    width = held.shape[2] // 2
    for j in range(2):
        for to, ref in ((owner, hold_y), (1 - owner, send_y)):
            ref[j] = total_of(held[2 * to + j, :, :width], got[2 * to + j, :, :width])
        for to, ref in ((bit, hold_x), (1 - bit, send_x)):
            ref[j] = total_of(held[2 * j + to, :, width:], got[2 * j + to, :, width:])


def split_second_kernel(place_ref, hold_y, got_y, hold_x, got_x, keep, send_x, send_y):
    owner, bit = place_ref[0], place_ref[2]
    width = hold_y.shape[2]
    keep[:, :width] = total_of(hold_y[bit], got_y[bit])
    send_x[...] = total_of(hold_y[1 - bit], got_y[1 - bit])
    keep[:, width:] = total_of(hold_x[owner], got_x[owner])
    send_y[...] = total_of(hold_x[1 - owner], got_x[1 - owner])


def split_third_kernel(place_ref, held, got_left, got_right, *refs, slot):
    index = place_ref[slot]
    width = got_left.shape[2]
    for d, ref in enumerate(refs):
        ref[:, :width] = total_of(held[index ^ d, :, :width], got_left[index ^ d])
        ref[:, width:] = total_of(held[index ^ d, :, width:], got_right[index ^ d])


def sum_cut_kernel(place_ref, held, *refs, slot, arrived):
    index = place_ref[slot]
    for d, out_ref in enumerate(refs[arrived:]):
        total = held[index ^ d].astype(f32)
        for got in refs[:arrived]:
            total += got[index ^ d].astype(f32)
        out_ref[...] = total.astype(bf16)


def join_kernel(place_ref, *refs, slot):
    index = place_ref[slot]
    for d, ref in enumerate(refs[:-1]):
        refs[-1][index ^ d] = ref[...]


def attend_back_kernel(
    q_ref, k_ref, v_ref, do_ref, do_before, do_after, own_rows, rows_before, rows_after,
    bias_ref, bias_edge, cos_ref, sin_ref, *refs,
):
    out_ref, mark_ref = refs[-2:]
    mark_ref[...] = jnp.zeros_like(mark_ref)
    rows, width = do_ref.shape[1], do_ref.shape[2]
    out_ref[0, :, 3 * width :] = jnp.zeros((rows, 2 * PAIR), bf16)
    inner = slice(HALF_WINDOW, HALF_WINDOW + rows)
    lane = lax.broadcasted_iota(jnp.int32, (1, PAIR), 1)
    first_half = (lane % HEAD_DIM) < HEAD_DIM // 2
    first_head = lane < HEAD_DIM
    top_rows = lax.broadcasted_iota(jnp.int32, (PAIR, 1), 0) < HEAD_DIM
    cosine, sine = cos_ref[0, inner], sin_ref[0, inner]
    bias = jnp.concatenate([bias_ref[0], bias_ref[0]], 1)
    offsets_edge = jnp.concatenate([bias_edge[0], bias_edge[0]], 1)

    def split(value):
        zero = jnp.zeros_like(value)
        return jnp.concatenate(
            [jnp.where(first_head, value, zero), jnp.where(first_head, zero, value)], 0
        )

    after_lane = lane < HALF_WINDOW
    edge = []
    for base in (3 * PAIR, 0):
        value = jnp.zeros((HEAD_ROWS, PAIR), f32)
        for at in (base, base + PAIR, base + 2 * PAIR):
            columns = slice(at, at + PAIR)
            value += jnp.where(
                after_lane, rows_after[0, :, columns].astype(f32), rows_before[0, :, columns].astype(f32)
            )
        edge.append(value)
    edge_sum, edge_lse = edge
    own_sum, own_lse = own_rows[0, :HEAD_ROWS], own_rows[0, HEAD_ROWS:]

    def row_of(value, pair):
        at = 2 * pair
        return jnp.concatenate([value[at : at + 1, :], value[at + 1 : at + 2, :]], 1)

    def back(keys, values, query, grad_mixed, offsets, log_total, inner_sum):
        probs = jnp.exp(dot_right(keys, query) + offsets - log_total)
        grad_probs = dot_right(values, grad_mixed)
        return probs.astype(bf16), (probs * (grad_probs - inner_sum)).astype(bf16)

    def rotated_back(value):
        return value * cosine - half_swap(value, first_half) * sine

    for pair in range(width // PAIR):
        columns = slice(pair * PAIR, (pair + 1) * PAIR)
        keys, values = k_ref[0, :, columns], v_ref[0, :, columns]
        query = split(q_ref[0, inner, columns])
        grad_mixed = split(do_ref[0, :, columns])
        probs, grad_scores = back(
            keys, values, query, grad_mixed, bias,
            row_of(own_lse, pair), row_of(own_sum, pair),
        )
        query_edge = split(
            jnp.concatenate(
                [
                    q_ref[0, HALF_WINDOW + rows :, columns],
                    q_ref[0, :HALF_WINDOW, columns],
                ],
                0,
            )
        )
        grad_edge = split(jnp.concatenate([do_after[0, :, columns], do_before[0, :, columns]], 0))
        probs_edge, scores_edge = back(
            keys[inner], values[inner], query_edge, grad_edge, offsets_edge,
            row_of(edge_lse, pair), row_of(edge_sum, pair),
        )
        grad_values = dot(
            jnp.concatenate([probs[inner], probs_edge], 1),
            jnp.concatenate([grad_mixed, grad_edge], 0),
        )
        grad_keys = dot(
            jnp.concatenate([grad_scores[inner], scores_edge], 1),
            jnp.concatenate([query, query_edge], 0),
        )
        grad_query = dot_left(grad_scores, keys)
        grad_query = jnp.where(first_head, grad_query[:rows], grad_query[rows:]) * HEAD_DIM**-0.5
        out_ref[0, :, columns] = rotated_back(grad_query).astype(bf16)
        out_ref[0, :, width + pair * PAIR : width + (pair + 1) * PAIR] = rotated_back(
            grad_keys
        ).astype(bf16)
        out_ref[0, :, 2 * width + pair * PAIR : 2 * width + (pair + 1) * PAIR] = (
            grad_values.astype(bf16)
        )


def stream_back_kernel(
    place_ref, dqkv_ref, tok_ref, dx1_ref, gain_ref, w_own, w_far, w_near, out_ref, gsum_ref, weight
):
    @pl.when(pl.program_id(0) == 0)
    def _():
        place_weight(place_ref, weight, w_own, w_far, w_near)
        gsum_ref[...] = jnp.zeros_like(gsum_ref)

    rows, width = tok_ref.shape
    grad_hidden = dot_right(dqkv_ref[...], weight[...])
    normed, factor = norm_parts(tok_ref[...].astype(f32))
    gsum_ref[...] += jnp.sum((grad_hidden * normed).reshape(rows // 8, 8, width), 0)
    grad_normed = grad_hidden * gain_ref[0:1, :].astype(f32)
    out_ref[...] = (dx1_ref[...] + norm_back(grad_normed, normed, factor)).astype(bf16)


def join_halves(place_ref, whole, mine, other):
    rows = mine.shape[0]
    core = place_ref[1]
    whole[pl.ds(pl.multiple_of(core * rows, 16), rows), :] = mine[...]
    whole[pl.ds(pl.multiple_of((1 - core) * rows, 16), rows), :] = other[...]


def finish_qkv_kernel(place_ref, mine, other, out_ref, gain_ref, columns):
    rows = mine.shape[0]
    core = place_ref[1]
    width = out_ref.shape[1]
    for ref, at in ((mine, core * rows), (other, (1 - core) * rows)):
        at = pl.ds(pl.multiple_of(at, 16), rows)
        out_ref[at, :] = ref[:, :width].astype(f32)
        columns[at, :] = ref[:, width : width + PAIR].astype(f32)
    gain_ref[...] = columns[...].T[: gain_ref.shape[0]]


def finish_three_kernel(place_ref, mine, other, in_ref, down_ref, out_ref, whole):
    join_halves(place_ref, whole, mine, other)
    width = whole.shape[1]
    at = 0
    for i in range(in_ref.shape[1] // width):
        in_ref[:, i * width : (i + 1) * width] = whole[at : at + in_ref.shape[0]].astype(f32)
        at += in_ref.shape[0]
    for ref in (down_ref, out_ref):
        ref[...] = whole[at : at + ref.shape[0]].astype(f32)
        at += ref.shape[0]


def shape_of(*dims, dtype=bf16):
    return jax.ShapeDtypeStruct(dims, dtype)


def whole_spec(array):
    return pl.BlockSpec(array.shape, lambda i: (0,) * array.ndim)


def run(kernel, grid, inputs, outputs, scratch=(), aliases=None, later=()):
    first = len(inputs)
    later = jax.tree.leaves(later)
    inputs = [*inputs, *[(x, pl.ANY) for x in later]]

    def body(*refs):
        kernel(*refs[:first], *refs[first + len(later) :])

    def spec(block, place):
        return pl.BlockSpec(block, place)

    specs = []
    for item in inputs:
        if item[1] is None and item[0].dtype == jnp.int32:
            specs.append(pl.BlockSpec(memory_space=pltpu.SMEM))
        elif item[1] is pl.ANY:
            specs.append(pl.BlockSpec(memory_space=pl.ANY))
        elif item[1] is None:
            specs.append(whole_spec(item[0]))
        else:
            specs.append(spec(item[1], item[2]))
    out_specs = [whole_spec(o[0]) if o[1] is None else spec(o[1], o[2]) for o in outputs]
    return pl.pallas_call(
        body,
        grid=(grid,),
        in_specs=specs,
        out_specs=out_specs,
        out_shape=[o[0] for o in outputs],
        scratch_shapes=list(scratch),
        input_output_aliases=aliases or {},
        cost_estimate=pl.CostEstimate(flops=1, bytes_accessed=1, transcendentals=0),
        compiler_params=pltpu.CompilerParams(
            dimension_semantics=("arbitrary",), vmem_limit_bytes=56 * MIB
        ),
    )(*[x[0] for x in inputs])


def flip_route(size, bit):
    return [(i, i ^ bit) for i in range(size)]


def swap_half(half):
    return lax.ppermute(half, "seq", flip_route(lax.axis_size("seq"), 1))


def exchange(block, distance):
    if distance == 0:
        return lax.ppermute(block, "fsdp", flip_route(2, 1))
    return lax.ppermute(block, "seq", flip_route(lax.axis_size("seq"), distance))


def together(*values):
    return lax.optimization_barrier(values)


def column_steps(rows, columns):
    return 3 if rows * columns > 400_000 and columns % (3 * PAIR) == 0 else 1


def sum_cut(place, slot, held, gots, later):
    parts, rows, columns = held.shape
    return run(
        partial(sum_cut_kernel, slot=slot, arrived=len(gots)),
        1,
        [(place, None), *[(x, None) for x in (held, *gots)]],
        [(shape_of(rows, columns), None) for _ in range(parts)],
        later=later,
    )


def split_run(kernel, place, rows, inputs, outputs, later):
    steps = 3 if rows % 48 == 0 else 1

    def item(array):
        block = (*array.shape[:-2], rows // steps, array.shape[-1])
        lead = (0,) * (len(block) - 2)
        return (array, block, lambda i: (*lead, i, 0))

    return run(kernel, steps, [(place, None), *map(item, inputs)], [item(x) for x in outputs], later=later)


def join(place, slot, parts, later):
    rows, columns = parts[0].shape
    steps = column_steps(len(parts) * rows, columns)
    (whole,) = run(
        partial(join_kernel, slot=slot),
        steps,
        [(place, None), *[(x, (rows, columns // steps), lambda i: (0, i)) for x in parts]],
        [
            (
                shape_of(len(parts), rows, columns),
                (len(parts), rows, columns // steps),
                lambda i: (0, 0, i),
            )
        ],
        later=later,
    )
    return whole.reshape(len(parts) * rows, columns)


def bit_groups():
    stages = (lax.axis_size("seq") - 1).bit_length()
    return [(0, 1), (1, 1)] + [(at, min(2, stages - at)) for at in range(2, stages, 2)]


def member(group):
    at, bits = group
    return (lax.axis_index("seq") >> at) & ((1 << bits) - 1)


def sum_stages(place, keep, send):
    (got,), later = yield [(send, 1)]
    rows, columns = keep.shape[1] // 2, keep.shape[2]
    four = (4, rows, columns)
    part = shape_of(2, rows, columns // 2)
    hold_y, send_y, hold_x, send_x = split_run(
        split_first_kernel, place, rows, [keep.reshape(four), got.reshape(four)], [part] * 4,
        later,
    )
    (got_y, got_x), later = yield [(send_y, 0), (send_x, 2)]
    block, send_x, send_y = split_run(
        split_second_kernel,
        place,
        rows,
        [hold_y, got_y, hold_x, got_x],
        [shape_of(rows, columns), *[shape_of(rows, columns // 2)] * 2],
        later,
    )
    arrived, later = yield [(send_x, 2), (send_y, 0)]
    groups = list(enumerate(bit_groups()[2:], 3))
    for step, (slot, group) in enumerate(groups):
        count = 1 << group[1]
        size = block.shape[0] // count
        if step == 0:
            block, *sends = run(
                partial(split_third_kernel, slot=slot),
                1,
                [
                    (place, None),
                    *[(x.reshape(count, size, x.shape[1]), None) for x in (block, *arrived)],
                ],
                [(shape_of(size, columns), None) for _ in range(count)],
                later=later,
            )
        else:
            shape = (count, size, columns)
            block, *sends = sum_cut(
                place, slot, block.reshape(shape), [x.reshape(shape) for x in arrived], later
            )
        arrived, later = yield [(x, (d + 1) << group[0]) for d, x in enumerate(sends)]
    (block,) = sum_cut(place, len(groups) + 3, block[None], [x[None] for x in arrived], later)
    for slot, group in reversed([(2, (1, 1)), *groups]):
        held, later = yield [(block, d << group[0]) for d in range(1, 1 << group[1])]
        block = join(place, slot, [block, *held], later)
    (other,), _ = yield [(block, 1)]
    return block, other


class Chain:
    def __init__(self, stages):
        self.stages, self.result = stages, None
        self.post(next(stages))

    def post(self, sends, gate=None, arrived=0):
        blocks = [block for block, _ in sends]
        if gate is not None:
            held = together(*blocks, *gate.got[:arrived])
            blocks = list(held[: len(blocks)])
            gate.got[:arrived] = held[len(blocks) :]
        self.sent = blocks
        self.got = [exchange(block, distance) for block, (_, distance) in zip(blocks, sends)]

    def advance(self, *later, gate=None, arrived=0):
        try:
            self.post(self.stages.send((self.got, later)), gate, arrived)
        except StopIteration as end:
            self.result = end.value
        return self.sent


def window_tables(pos, rows, head_width):
    half = head_width // 2
    freqs = 10000.0 ** (-(jnp.arange(half, dtype=f32) * 2.0 / head_width))
    angle = pos.astype(f32)[..., None] * freqs
    cosine, sine = jnp.cos(angle), jnp.sin(angle)
    cosine = jnp.concatenate([cosine] * 4, -1)
    sine = jnp.concatenate([-sine, sine, -sine, sine], -1)
    span = pos.shape[1]
    index = jnp.arange(span, dtype=jnp.int32)

    def offsets(query_pos, query_index, key_pos, key_index):
        gap = key_index - query_index
        allowed = (
            (jnp.abs(gap) <= HALF_WINDOW)
            & (key_pos >= 0)
            & (query_pos >= 0)
            & ((gap > 0) | (query_pos >= -gap))
            & ((gap <= 0) | (key_pos >= gap))
        )
        return jnp.where(allowed, 0.0, masked_score).astype(f32)

    inner = slice(HALF_WINDOW, HALF_WINDOW + rows)
    outer_pos = jnp.concatenate([pos[:, HALF_WINDOW + rows :], pos[:, :HALF_WINDOW]], 1)
    outer_index = jnp.concatenate([index[HALF_WINDOW + rows :], index[:HALF_WINDOW]])
    bias = offsets(
        pos[:, inner, None], index[None, inner, None], pos[:, None, :], index[None, None, :]
    )
    bias_t = offsets(
        pos[:, None, inner], index[None, None, inner], pos[:, :, None], index[None, :, None]
    )
    bias_edge = offsets(
        outer_pos[:, None, :],
        outer_index[None, None, :],
        pos[:, inner, None],
        index[None, inner, None],
    )
    return cosine, sine, bias, bias_t, bias_edge


def local(tokens, positions, qkv_weight, out_weight, in_weight, down_weight, norm_gains, cotangent):
    num_seqs, rows, width = tokens.shape
    span = rows + 2 * HALF_WINDOW
    count = num_seqs * rows
    ffn = 2 * down_weight.shape[0]
    seq_index, own_y = lax.axis_index("seq"), lax.axis_index("fsdp")
    place = jnp.stack(
        [own_y, seq_index % 2, *[member(group) for group in bit_groups()[1:]], 0 * own_y]
    ).astype(jnp.int32)

    gain_width = norm_gains.shape[1]
    half = qkv_weight.shape[0] // 2
    (first_half,) = run(
        pack_first_kernel,
        1,
        [(place, None), (qkv_weight, None), (norm_gains, None)],
        [(shape_of(half + 16, qkv_weight.shape[1]), None)],
    )
    far_qkv = exchange(first_half, 0)
    later_rows = half + down_weight.shape[0] // 6 + out_weight.shape[0] // 6
    halo = shape_of(num_seqs, HALF_WINDOW, width)
    later_half, tok_head, tok_tail = run(
        pack_later_kernel,
        1,
        [
            (place, None),
            *[(x, None) for x in (out_weight, in_weight, down_weight)],
            (tokens, None),
        ],
        [(shape_of(later_rows, in_weight.shape[1]), None), (halo, None), (halo, None)],
        later=first_half,
    )
    far_later = exchange(later_half, 0)
    tok_before = passed_along(tok_tail, "seq", 1)
    tok_after = passed_along(tok_head, "seq", -1)
    padded_pos = jnp.pad(positions, ((0, 0), (HALF_WINDOW, HALF_WINDOW)), constant_values=-1)
    key_pos = lax.dynamic_slice_in_dim(padded_pos, seq_index * rows, span, 1)
    cosine, sine, bias, bias_t, bias_edge = window_tables(key_pos, rows, HEAD_DIM)
    far_qkv, tok_before, tok_after, cosine, sine, bias, bias_t, bias_edge = together(
        far_qkv, tok_before, tok_after, cosine, sine, bias, bias_t, bias_edge
    )
    w_qkv = (qkv_weight, far_qkv, swap_half(far_qkv))
    gains_other = far_qkv[qkv_weight.shape[0] // 2 :, :gain_width][: norm_gains.shape[0]]
    gains = jnp.where(
        own_y == 0,
        jnp.concatenate([norm_gains, gains_other], 1),
        jnp.concatenate([gains_other, norm_gains], 1),
    )

    def per_seq(i):
        return (i, 0, 0)

    def row_block(i):
        return (i, 0)

    def column_block(i):
        return (0, i)

    qkv_pieces = [(piece, None) for piece in w_qkv]
    wide = (1, span, width)
    hidden_one, query, keys, values, mixed, log_total = run(
        attend_kernel,
        num_seqs,
        [
            (place, None),
            (tok_before, (1, HALF_WINDOW, width), per_seq),
            (tokens, (1, rows, width), per_seq),
            (tok_after, (1, HALF_WINDOW, width), per_seq),
            (cosine, (1, span, PAIR), per_seq),
            (sine, (1, span, PAIR), per_seq),
            (bias, (1, rows, span), per_seq),
            (gains, None),
            *qkv_pieces,
        ],
        [
            (shape_of(num_seqs, rows, width), (1, rows, width), per_seq),
            (shape_of(num_seqs, span, width), wide, per_seq),
            (shape_of(num_seqs, span, width), wide, per_seq),
            (shape_of(num_seqs, span, width), wide, per_seq),
            (shape_of(num_seqs, rows, width), (1, rows, width), per_seq),
            (shape_of(num_seqs, HEAD_ROWS, PAIR, dtype=f32), (1, HEAD_ROWS, PAIR), per_seq),
        ],
        [pltpu.VMEM((width, 3 * width), bf16)],
    )
    far_later, mixed = together(far_later, mixed)
    near_later = swap_half(far_later)

    flat_tokens = tokens.reshape(count, width)
    flat_dy = cotangent.reshape(count, width)
    flat_mixed = mixed.reshape(count, width)
    step = 2 * rows
    tok_block = (step, width)
    pack = HALF_WINDOW + HEAD_ROWS
    half_block = (2, pack, width)
    (
        layer_out, grad_stream, grad_mixed, grad_lo, grad_hi, inner_sum,
        hidden_two, grad_up, middle, grad_attn, gain_sum_two,
    ) = run(
        feed_kernel,
        count // step,
        [
            (place, None),
            (flat_tokens, tok_block, row_block),
            (flat_mixed, tok_block, row_block),
            (flat_dy, tok_block, row_block),
            (log_total, (2, HEAD_ROWS, PAIR), per_seq),
            (gains, None),
            *[(x, None) for x in (out_weight, in_weight, down_weight, far_later, near_later)],
        ],
        [
            (shape_of(count, width), tok_block, row_block),
            (shape_of(count, width, dtype=f32), tok_block, row_block),
            (shape_of(count, width), tok_block, row_block),
            (shape_of(num_seqs, pack, width), half_block, per_seq),
            (shape_of(num_seqs, pack, width), half_block, per_seq),
            (shape_of(num_seqs, 2 * HEAD_ROWS, PAIR, dtype=f32), (2, 2 * HEAD_ROWS, PAIR), per_seq),
            (shape_of(count, width), tok_block, row_block),
            (shape_of(count, 2 * ffn), (step, 2 * ffn), row_block),
            (shape_of(count, ffn), (step, ffn), row_block),
            (shape_of(count, width), tok_block, row_block),
            (shape_of(8, width, dtype=f32), None),
        ],
        [
            pltpu.VMEM((width, width), bf16),
            pltpu.VMEM((width, 2 * ffn), bf16),
            pltpu.VMEM((ffn, width), bf16),
        ],
    )
    do_before = passed_along(grad_hi, "seq", 1)
    do_after = passed_along(grad_lo, "seq", -1)

    size = max(lax.axis_size("seq"), PAIR)
    bundle_rows = -(-(3 * width // 2 + ffn // 2 + width // 2) // size) * size
    bundle_part = shape_of(2, bundle_rows // 2, width)
    keep, send = run(
        grads_kernel,
        3,
        [
            (place, None),
            (hidden_two, None),
            (grad_up, (count, 2 * ffn // 3), column_block),
            (middle, (count, ffn // 3), column_block),
            (flat_dy, None),
            (flat_mixed, None),
            (grad_attn, (count, width // 3), column_block),
        ],
        [(bundle_part, None), (bundle_part, None)],
        [pltpu.VMEM((2 * bundle_rows, width), bf16)],
    )
    do_before, do_after, send = together(do_before, do_after, send)
    chain_mlp = Chain(sum_stages(place, keep, send))
    heads = (1, 2 * HEAD_ROWS, PAIR)
    half_part = (1, HALF_WINDOW, width)
    edge_pack = (1, HEAD_ROWS, width)

    wider = 3 * width + 2 * PAIR

    def back_part(first, many, later, earlier=None):
        def at(i):
            return (first + i, 0, 0)

        def pack_rows(i):
            return (first + i, HALF_WINDOW // HEAD_ROWS, 0)

        return run(
            attend_back_kernel,
            many,
            [
                (query, wide, at),
                (keys, wide, at),
                (values, wide, at),
                (grad_mixed.reshape(num_seqs, rows, width), (1, rows, width), at),
                (do_before, half_part, at),
                (do_after, half_part, at),
                (inner_sum, heads, at),
                (do_before, edge_pack, pack_rows),
                (do_after, edge_pack, pack_rows),
                (bias_t, (1, span, rows), at),
                (bias_edge, (1, rows, PAIR), at),
                (cosine, (1, span, PAIR), at),
                (sine, (1, span, PAIR), at),
                *([] if earlier is None else [(earlier, pl.ANY)]),
            ],
            [
                (shape_of(num_seqs, rows, wider), (1, rows, wider), at),
                (shape_of(8, PAIR, dtype=f32), None),
            ],
            aliases=None if earlier is None else {13: 0},
            later=later,
        )

    few = num_seqs // 2
    grads, mark = back_part(0, few, ())
    grads, _ = back_part(few, num_seqs - few, chain_mlp.advance(mark), grads)
    flat_grad = grads.reshape(count, wider)
    large = 4 * rows
    grad_tokens, gain_sum_one = run(
        stream_back_kernel,
        count // large,
        [
            (place, None),
            (flat_grad, (large, 3 * width), row_block),
            (flat_tokens, (large, width), row_block),
            (grad_stream, (large, width), row_block),
            (gains, None),
            *qkv_pieces,
        ],
        [
            (shape_of(count, width), (large, width), row_block),
            (shape_of(8, width, dtype=f32), None),
        ],
        [pltpu.VMEM((width, 3 * width), bf16)],
    )
    sent = chain_mlp.advance(gain_sum_one)
    step_columns = wider // 2
    part = shape_of(2, width // 4, wider)
    block = (2, width // 4, step_columns)

    def last_block(i):
        return (0, 0, i)

    keep, send = run(
        grad_qkv_kernel,
        wider // step_columns,
        [
            (place, None),
            (hidden_one.reshape(count, width), None),
            (flat_grad, (count, step_columns), column_block),
            (gain_sum_one, None),
            (gain_sum_two, None),
        ],
        [(part, block, last_block), (part, block, last_block)],
        [pltpu.VMEM((width, step_columns), bf16)],
        later=sent,
    )
    send, *chain_mlp.got = together(send, *chain_mlp.got)
    chain_qkv = Chain(sum_stages(place, keep, send))
    sent = chain_mlp.advance()
    sent = chain_qkv.advance(sent, gate=chain_mlp, arrived=2)
    sent = chain_mlp.advance(sent)
    sent = chain_qkv.advance(sent)
    while chain_mlp.result is None:
        sent = chain_qkv.advance(sent)
        sent = chain_mlp.advance(sent)
    in_sum, down_sum, out_sum = run(
        finish_three_kernel,
        1,
        [(place, None), *[(x, None) for x in chain_mlp.result]],
        [
            (shape_of(*in_weight.shape, dtype=f32), None),
            (shape_of(*down_weight.shape, dtype=f32), None),
            (shape_of(*out_weight.shape, dtype=f32), None),
        ],
        [pltpu.VMEM((bundle_rows, width), bf16)],
        later=sent,
    )
    sent = down_sum
    while chain_qkv.result is None:
        sent = chain_qkv.advance(sent)
    qkv_sum, gains_sum = run(
        finish_qkv_kernel,
        1,
        [(place, None), *[(x, None) for x in chain_qkv.result]],
        [
            (shape_of(*qkv_weight.shape, dtype=f32), None),
            (shape_of(*norm_gains.shape, dtype=f32), None),
        ],
        [pltpu.VMEM((qkv_weight.shape[0], PAIR), f32)],
    )
    return (
        layer_out.reshape(tokens.shape),
        grad_tokens.reshape(tokens.shape),
        qkv_sum,
        out_sum,
        in_sum,
        down_sum,
        gains_sum,
    )


def solution(mesh):
    in_specs = (
        P("fsdp", "seq", None),
        P("fsdp", None),
        P("fsdp", None),
        P("fsdp", None),
        P("fsdp", None),
        P("fsdp", None),
        P(None, "fsdp"),
        P("fsdp", "seq", None),
    )
    out_specs = (
        P("fsdp", "seq", None),
        P("fsdp", "seq", None),
        P("fsdp", None),
        P("fsdp", None),
        P("fsdp", None),
        P("fsdp", None),
        P(None, "fsdp"),
    )
    return jax.shard_map(local, mesh=mesh, in_specs=in_specs, out_specs=out_specs, check_vma=False)
```

```python
import math
from functools import partial

import jax
import jax.numpy as jnp
from jax import lax
from jax.experimental import pallas as pl
from jax.experimental.pallas import tpu as pltpu
from jax.sharding import PartitionSpec as P

HEAD_DIM = 64
HALF_WINDOW = 64
PAIR = 128
HEAD_ROWS = 16
MIB = 1 << 20


masked_score = -1000000000.0
norm_epsilon = 1e-05
root_half = 0.7071067811865476
normal_peak = 0.3989422804014327
f32 = jnp.float32
bf16 = jnp.bfloat16


def passed_along(block, axis, distance):
    devices = range(lax.axis_size(axis))
    route = [(i - distance, i) for i in devices if i - distance in devices]
    return lax.ppermute(block, axis, route)


def norm_parts(values):
    center = values - jnp.mean(values, -1, keepdims=True)
    factor = lax.rsqrt(jnp.mean(center * center, -1, keepdims=True) + norm_epsilon)
    return (center * factor, factor)


def norm_back(grad_normed, normed, factor):
    first = jnp.mean(grad_normed, -1, keepdims=True)
    second = jnp.mean(grad_normed * normed, -1, keepdims=True)
    return factor * (grad_normed - first - normed * second)


def dot(left, right):
    return jnp.dot(left, right, preferred_element_type=f32)


def dot_right(left, right):
    return lax.dot_general(left, right, (((1,), (1,)), ((), ())), preferred_element_type=f32)


def dot_left(left, right):
    return lax.dot_general(left, right, (((0,), (0,)), ((), ())), preferred_element_type=f32)


def half_swap(value, first_half):
    return jnp.where(first_half, pltpu.roll(value, PAIR - 32, 1), pltpu.roll(value, 32, 1))


def place_weight(place_ref, whole, own, far, near):
    rows = own.shape[0]
    half = rows // 2
    index, core = place_ref[0], place_ref[1]
    other = (1 - index) * rows
    whole[pl.ds(pl.multiple_of(index * rows, half), rows), :] = own[...]
    whole[pl.ds(pl.multiple_of(other + core * half, half), half), :] = far[:half]
    whole[pl.ds(pl.multiple_of(other + (1 - core) * half, half), half), :] = near[:half]


def place_folded(place_ref, whole, own, far, near, at):
    rows, width = own.shape
    third = rows // 6
    index, core = place_ref[0], place_ref[1]
    other = (1 - index) * rows
    whole[pl.ds(pl.multiple_of(index * rows, third), rows), :] = own[...]
    for i in range(3):
        columns = slice(i * width, (i + 1) * width)
        first = other + core * 3 * third + i * third
        whole[pl.ds(pl.multiple_of(first, third), third), :] = far[at : at + third, columns]
        first = other + (1 - core) * 3 * third + i * third
        whole[pl.ds(pl.multiple_of(first, third), third), :] = near[at : at + third, columns]


def attend_kernel(
    place_ref, before, own, after, cos_ref, sin_ref, bias_ref, gain_ref, w_own, w_far, w_near,
    h1_ref, q_ref, k_ref, v_ref, mix_ref, lse_ref, weight,
):
    @pl.when(pl.program_id(0) == 0)
    def _():
        place_weight(place_ref, weight, w_own, w_far, w_near)

    width = own.shape[2]
    rows = own.shape[1]
    span = rows + 2 * HALF_WINDOW
    stream = jnp.concatenate([before[0], own[0], after[0]], 0).astype(f32)
    normed, _ = norm_parts(stream)
    hidden = (normed * gain_ref[0:1, :].astype(f32)).astype(bf16)
    h1_ref[0] = hidden[HALF_WINDOW : HALF_WINDOW + rows]
    lane = lax.broadcasted_iota(jnp.int32, (1, PAIR), 1)
    first_half = (lane % HEAD_DIM) < HEAD_DIM // 2
    first_head = lane < HEAD_DIM
    cosine, sine = cos_ref[0], sin_ref[0]
    for start in range(0, 3 * width, 2 * PAIR):
        part = dot(hidden, weight[:, start : start + 2 * PAIR])
        for sub in range(0, 2 * PAIR, PAIR):
            value = part[:, sub : sub + PAIR]
            column = (start + sub) % width
            if start + sub < 2 * width:
                value = value * cosine + half_swap(value, first_half) * sine
            if start + sub < width:
                q_ref[0, :, column : column + PAIR] = (value * HEAD_DIM**-0.5).astype(bf16)
            elif start + sub < 2 * width:
                k_ref[0, :, column : column + PAIR] = value.astype(bf16)
            else:
                v_ref[0, :, column : column + PAIR] = value.astype(bf16)
    bias = bias_ref[0]
    bias = jnp.concatenate([bias, bias], 0)
    log_totals = jnp.zeros((rows, PAIR), f32)
    for pair in range(width // PAIR):
        columns = slice(pair * PAIR, (pair + 1) * PAIR)
        query = q_ref[0, HALF_WINDOW : HALF_WINDOW + rows, columns]
        zero = jnp.zeros_like(query)
        both = jnp.concatenate(
            [jnp.where(first_head, query, zero), jnp.where(first_head, zero, query)], 0
        )
        scores = dot_right(both, k_ref[0, :, columns]) + bias
        top = jnp.max(scores, -1, keepdims=True)
        expo = jnp.exp(scores - top)
        total = jnp.sum(expo, -1, keepdims=True)
        log_total = top + jnp.log(total)
        probs = (expo * (1.0 / total)).astype(bf16)
        mixed = dot(probs, v_ref[0, :, columns])
        mix_ref[0, :, columns] = jnp.where(first_head, mixed[:rows], mixed[rows:]).astype(bf16)
        log_totals = jnp.where(lane == 2 * pair, log_total[:rows], log_totals)
        log_totals = jnp.where(lane == 2 * pair + 1, log_total[rows:], log_totals)
    lse_ref[0] = jnp.transpose(log_totals)[:HEAD_ROWS]


def three_parts(value):
    parts = []
    for _ in range(3):
        parts.append(value.astype(bf16))
        value = value - parts[-1].astype(f32)
    return parts


def feed_kernel(
    place_ref, tok_ref, mix_ref, dy_ref, lse_ref, gain_ref,
    out_own, in_own, down_own, far_ref, near_ref,
    layer_ref, dx1_ref, do_ref, lo_ref, hi_ref, rows_ref, h2_ref, dup_ref, mid_ref, dmix_ref, gsum_ref,
    w_out, w_in, w_down,
):
    @pl.when(pl.program_id(0) == 0)
    def _():
        at = in_own.shape[0] // 2
        place_weight(place_ref, w_in, in_own, far_ref, near_ref)
        for whole, own in ((w_down, down_own), (w_out, out_own)):
            place_folded(place_ref, whole, own, far_ref, near_ref, at)
            at += own.shape[0] // 6
        gsum_ref[...] = jnp.zeros_like(gsum_ref)

    rows, width = tok_ref.shape
    ffn = w_down.shape[0]
    block = 2 * HALF_WINDOW
    after_attn = tok_ref[...].astype(f32) + dot(mix_ref[...], w_out[...])
    normed, factor = norm_parts(after_attn)
    gain = gain_ref[1:2, :].astype(f32)
    h2_ref[...] = (normed * gain).astype(bf16)
    step = 3 * PAIR
    for start in range(0, ffn, step):
        columns = slice(start, start + step)
        gates = slice(ffn + start, ffn + start + step)
        act_input = dot(h2_ref[...], w_in[:, columns])
        gate_part = dot(h2_ref[...], w_in[:, gates])
        grad_middle = dot_right(dy_ref[...], w_down[columns, :])
        share = 0.5 + 0.5 * lax.erf(act_input * root_half)
        act_value = act_input * share
        slope = share + act_input * (normal_peak * jnp.exp(-0.5 * act_input * act_input))
        mid_ref[:, columns] = (act_value * gate_part).astype(bf16)
        dup_ref[:, columns] = (grad_middle * gate_part * slope).astype(bf16)
        dup_ref[:, gates] = (grad_middle * act_value).astype(bf16)
    layer_ref[...] = (after_attn + dot(mid_ref[...], w_down[...])).astype(bf16)
    grad_hidden = dot_right(dup_ref[...], w_in[...])
    gain_terms = grad_hidden * normed
    gsum_ref[...] += jnp.sum(gain_terms.reshape(rows // 8, 8, width), 0)
    grad_stream = dy_ref[...].astype(f32) + norm_back(grad_hidden * gain, normed, factor)
    dx1_ref[...] = grad_stream
    dmix_ref[...] = grad_stream.astype(bf16)
    grad_mixed = dot_right(dmix_ref[...], w_out[...]).astype(bf16)
    do_ref[...] = grad_mixed
    products = grad_mixed.astype(f32) * mix_ref[...].astype(f32)
    high = products.astype(bf16)
    low = (products - high.astype(f32)).astype(bf16)
    head_of = lax.broadcasted_iota(jnp.int32, (width, PAIR), 0) // HEAD_DIM
    slot = lax.broadcasted_iota(jnp.int32, (width, PAIR), 1)
    pick = jnp.where(head_of == slot, 1.0, 0.0).astype(bf16)
    delta = dot(high, pick) + dot(low, pick)
    for i in range(rows // block):
        piece = grad_mixed[i * block : (i + 1) * block]
        inner_sum = jnp.transpose(delta[i * block : (i + 1) * block])[:HEAD_ROWS]
        rows_ref[i, :HEAD_ROWS] = inner_sum
        rows_ref[i, HEAD_ROWS:] = lse_ref[i]
        parts = jnp.concatenate(three_parts(lse_ref[i]) + three_parts(inner_sum), 1)
        for ref, own in ((lo_ref, piece[:HALF_WINDOW]), (hi_ref, piece[HALF_WINDOW:])):
            ref[i, :HALF_WINDOW] = own
            ref[i, HALF_WINDOW:] = parts


def pack_first_kernel(place_ref, qkv_ref, gain_ref, out_ref):
    half = qkv_ref.shape[0] // 2
    count, width = gain_ref.shape
    out_ref[:half] = qkv_ref[pl.ds(pl.multiple_of(place_ref[1] * half, half), half), :]
    out_ref[half:] = jnp.zeros_like(out_ref[half:])
    filler = jnp.zeros((out_ref.shape[0] - half - count, width), bf16)
    out_ref[half:, :width] = jnp.concatenate([gain_ref[...], filler], 0)


def pack_later_kernel(place_ref, out_w, in_w, down_w, tok_ref, later_ref, head_ref, tail_ref):
    core = place_ref[1]
    half = in_w.shape[0] // 2
    width = out_w.shape[1]
    later_ref[:half] = in_w[pl.ds(pl.multiple_of(core * half, half), half), :]
    at = half
    for ref in (down_w, out_w):
        third = ref.shape[0] // 6
        for i in range(3):
            first = pl.multiple_of((core * 3 + i) * third, third)
            later_ref[at : at + third, i * width : (i + 1) * width] = ref[pl.ds(first, third), :]
        at += third
    rows = tok_ref.shape[1]
    for i in range(tok_ref.shape[0]):
        head_ref[i] = tok_ref[i, :HALF_WINDOW]
        tail_ref[i] = tok_ref[i, rows - HALF_WINDOW :]


def part_rows(place_ref, whole, keep_ref, send_ref):
    rows = keep_ref.shape[1]
    core = place_ref[1]
    for i in range(2):
        keep_ref[i] = whole[pl.ds(pl.multiple_of((2 * i + core) * rows, 16), rows), :]
        send_ref[i] = whole[pl.ds(pl.multiple_of((2 * i + 1 - core) * rows, 16), rows), :]


def as_column(row_groups):
    ones = jnp.ones((row_groups.shape[0], PAIR), bf16)
    return sum(dot_left(part, ones) for part in three_parts(row_groups))


def grad_qkv_kernel(place_ref, left_ref, right_ref, one_ref, two_ref, keep_ref, send_ref, whole):
    step = pl.program_id(0)
    whole[...] = dot_left(left_ref[...], right_ref[...]).astype(bf16)

    @pl.when(step == pl.num_programs(0) - 1)
    def _():
        lane = lax.broadcasted_iota(jnp.int32, (1, PAIR), 1)
        first, second = as_column(one_ref[...]), as_column(two_ref[...])
        columns = jnp.where(lane == 0, first, jnp.where(lane == 1, second, 0.0)).astype(bf16)
        at = whole.shape[1] - 2 * PAIR
        whole[:, at : at + PAIR] = columns
        whole[:, at + PAIR :] = jnp.zeros_like(columns)

    part_rows(place_ref, whole, keep_ref, send_ref)


def grads_kernel(place_ref, h2_ref, dup_ref, mid_ref, dy_ref, mix_ref, dmix_ref, keep_ref, send_ref, whole):
    step = pl.program_id(0)
    width = dy_ref.shape[1]
    half = whole.shape[0] // 2
    part = width // 2
    third = mid_ref.shape[1] // 2
    grad = dot_left(h2_ref[...], dup_ref[...]).astype(bf16)
    at = pl.multiple_of(step * part, part)
    whole[pl.ds(at, part), :] = grad[:part]
    whole[pl.ds(half + at, part), :] = grad[part:]
    grad = dot_left(mid_ref[...], dy_ref[...]).astype(bf16)
    for i in range(2):
        index = 2 * step + i
        owner = index // 3
        at = pl.multiple_of(owner * half + 3 * part + (index - 3 * owner) * third, 64)
        whole[pl.ds(at, third), :] = grad[i * third : (i + 1) * third]
    grad = dot_left(mix_ref[...], dmix_ref[...]).astype(bf16)
    columns = pl.ds(pl.multiple_of(step * (width // 3), PAIR), width // 3)
    at = 3 * part + 3 * third
    whole[at : at + part, columns] = grad[:part]
    whole[half + at : half + at + part, columns] = grad[part:]

    @pl.when(step == pl.num_programs(0) - 1)
    def _():
        spare = half - at - part
        if spare:
            for start in (at + part, half + at + part):
                whole[start : start + spare] = jnp.zeros((spare, width), bf16)
        part_rows(place_ref, whole, keep_ref, send_ref)


def total_of(*values):
    total = values[0].astype(f32)
    for value in values[1:]:
        total += value.astype(f32)
    return total.astype(bf16)


def split_first_kernel(place_ref, held, got, hold_y, send_y, hold_x, send_x):
    owner, bit = place_ref[0], place_ref[2]
    width = held.shape[2] // 2
    for j in range(2):
        for to, ref in ((owner, hold_y), (1 - owner, send_y)):
            ref[j] = total_of(held[2 * to + j, :, :width], got[2 * to + j, :, :width])
        for to, ref in ((bit, hold_x), (1 - bit, send_x)):
            ref[j] = total_of(held[2 * j + to, :, width:], got[2 * j + to, :, width:])


def split_second_kernel(place_ref, hold_y, got_y, hold_x, got_x, keep, send_x, send_y):
    owner, bit = place_ref[0], place_ref[2]
    width = hold_y.shape[2]
    keep[:, :width] = total_of(hold_y[bit], got_y[bit])
    send_x[...] = total_of(hold_y[1 - bit], got_y[1 - bit])
    keep[:, width:] = total_of(hold_x[owner], got_x[owner])
    send_y[...] = total_of(hold_x[1 - owner], got_x[1 - owner])


def split_third_kernel(place_ref, held, got_left, got_right, *refs, slot):
    index = place_ref[slot]
    width = got_left.shape[2]
    for d, ref in enumerate(refs):
        ref[:, :width] = total_of(held[index ^ d, :, :width], got_left[index ^ d])
        ref[:, width:] = total_of(held[index ^ d, :, width:], got_right[index ^ d])


def sum_cut_kernel(place_ref, held, *refs, slot, arrived):
    index = place_ref[slot]
    for d, out_ref in enumerate(refs[arrived:]):
        total = held[index ^ d].astype(f32)
        for got in refs[:arrived]:
            total += got[index ^ d].astype(f32)
        out_ref[...] = total.astype(bf16)


def join_kernel(place_ref, *refs, slot):
    index = place_ref[slot]
    for d, ref in enumerate(refs[:-1]):
        refs[-1][index ^ d] = ref[...]


def attend_back_kernel(
    q_ref, k_ref, v_ref, do_ref, do_before, do_after, own_rows, rows_before, rows_after,
    bias_ref, bias_edge, cos_ref, sin_ref, *refs,
):
    out_ref, mark_ref = refs[-2:]
    mark_ref[...] = jnp.zeros_like(mark_ref)
    rows, width = do_ref.shape[1], do_ref.shape[2]
    out_ref[0, :, 3 * width :] = jnp.zeros((rows, 2 * PAIR), bf16)
    inner = slice(HALF_WINDOW, HALF_WINDOW + rows)
    lane = lax.broadcasted_iota(jnp.int32, (1, PAIR), 1)
    first_half = (lane % HEAD_DIM) < HEAD_DIM // 2
    first_head = lane < HEAD_DIM
    top_rows = lax.broadcasted_iota(jnp.int32, (PAIR, 1), 0) < HEAD_DIM
    cosine, sine = cos_ref[0, inner], sin_ref[0, inner]
    bias = jnp.concatenate([bias_ref[0], bias_ref[0]], 1)
    offsets_edge = jnp.concatenate([bias_edge[0], bias_edge[0]], 1)

    def split(value):
        zero = jnp.zeros_like(value)
        return jnp.concatenate(
            [jnp.where(first_head, value, zero), jnp.where(first_head, zero, value)], 0
        )

    after_lane = lane < HALF_WINDOW
    edge = []
    for base in (3 * PAIR, 0):
        value = jnp.zeros((HEAD_ROWS, PAIR), f32)
        for at in (base, base + PAIR, base + 2 * PAIR):
            columns = slice(at, at + PAIR)
            value += jnp.where(
                after_lane, rows_after[0, :, columns].astype(f32), rows_before[0, :, columns].astype(f32)
            )
        edge.append(value)
    edge_sum, edge_lse = edge
    own_sum, own_lse = own_rows[0, :HEAD_ROWS], own_rows[0, HEAD_ROWS:]

    def row_of(value, pair):
        at = 2 * pair
        return jnp.concatenate([value[at : at + 1, :], value[at + 1 : at + 2, :]], 1)

    def back(keys, values, query, grad_mixed, offsets, log_total, inner_sum):
        probs = jnp.exp(dot_right(keys, query) + offsets - log_total)
        grad_probs = dot_right(values, grad_mixed)
        return probs.astype(bf16), (probs * (grad_probs - inner_sum)).astype(bf16)

    def rotated_back(value):
        return value * cosine - half_swap(value, first_half) * sine

    for pair in range(width // PAIR):
        columns = slice(pair * PAIR, (pair + 1) * PAIR)
        keys, values = k_ref[0, :, columns], v_ref[0, :, columns]
        query = split(q_ref[0, inner, columns])
        grad_mixed = split(do_ref[0, :, columns])
        probs, grad_scores = back(
            keys, values, query, grad_mixed, bias,
            row_of(own_lse, pair), row_of(own_sum, pair),
        )
        query_edge = split(
            jnp.concatenate(
                [
                    q_ref[0, HALF_WINDOW + rows :, columns],
                    q_ref[0, :HALF_WINDOW, columns],
                ],
                0,
            )
        )
        grad_edge = split(jnp.concatenate([do_after[0, :, columns], do_before[0, :, columns]], 0))
        probs_edge, scores_edge = back(
            keys[inner], values[inner], query_edge, grad_edge, offsets_edge,
            row_of(edge_lse, pair), row_of(edge_sum, pair),
        )
        grad_values = dot(
            jnp.concatenate([probs[inner], probs_edge], 1),
            jnp.concatenate([grad_mixed, grad_edge], 0),
        )
        grad_keys = dot(
            jnp.concatenate([grad_scores[inner], scores_edge], 1),
            jnp.concatenate([query, query_edge], 0),
        )
        grad_query = dot_left(grad_scores, keys)
        grad_query = jnp.where(first_head, grad_query[:rows], grad_query[rows:]) * HEAD_DIM**-0.5
        out_ref[0, :, columns] = rotated_back(grad_query).astype(bf16)
        out_ref[0, :, width + pair * PAIR : width + (pair + 1) * PAIR] = rotated_back(
            grad_keys
        ).astype(bf16)
        out_ref[0, :, 2 * width + pair * PAIR : 2 * width + (pair + 1) * PAIR] = (
            grad_values.astype(bf16)
        )


def stream_back_kernel(
    place_ref, dqkv_ref, tok_ref, dx1_ref, gain_ref, w_own, w_far, w_near, out_ref, gsum_ref, weight
):
    @pl.when(pl.program_id(0) == 0)
    def _():
        place_weight(place_ref, weight, w_own, w_far, w_near)
        gsum_ref[...] = jnp.zeros_like(gsum_ref)

    rows, width = tok_ref.shape
    grad_hidden = dot_right(dqkv_ref[...], weight[...])
    normed, factor = norm_parts(tok_ref[...].astype(f32))
    gsum_ref[...] += jnp.sum((grad_hidden * normed).reshape(rows // 8, 8, width), 0)
    grad_normed = grad_hidden * gain_ref[0:1, :].astype(f32)
    out_ref[...] = (dx1_ref[...] + norm_back(grad_normed, normed, factor)).astype(bf16)


def join_halves(place_ref, whole, mine, other):
    rows = mine.shape[0]
    core = place_ref[1]
    whole[pl.ds(pl.multiple_of(core * rows, 16), rows), :] = mine[...]
    whole[pl.ds(pl.multiple_of((1 - core) * rows, 16), rows), :] = other[...]


def finish_qkv_kernel(place_ref, mine, other, out_ref, gain_ref, columns):
    rows = mine.shape[0]
    core = place_ref[1]
    width = out_ref.shape[1]
    for ref, at in ((mine, core * rows), (other, (1 - core) * rows)):
        at = pl.ds(pl.multiple_of(at, 16), rows)
        out_ref[at, :] = ref[:, :width].astype(f32)
        columns[at, :] = ref[:, width : width + PAIR].astype(f32)
    gain_ref[...] = columns[...].T[: gain_ref.shape[0]]


def finish_three_kernel(place_ref, mine, other, in_ref, down_ref, out_ref, whole):
    join_halves(place_ref, whole, mine, other)
    width = whole.shape[1]
    at = 0
    for i in range(in_ref.shape[1] // width):
        in_ref[:, i * width : (i + 1) * width] = whole[at : at + in_ref.shape[0]].astype(f32)
        at += in_ref.shape[0]
    for ref in (down_ref, out_ref):
        ref[...] = whole[at : at + ref.shape[0]].astype(f32)
        at += ref.shape[0]


def shape_of(*dims, dtype=bf16):
    return jax.ShapeDtypeStruct(dims, dtype)


def whole_spec(array):
    return pl.BlockSpec(array.shape, lambda i: (0,) * array.ndim)


def run(kernel, grid, inputs, outputs, scratch=(), aliases=None, later=(), spare=4):
    first = len(inputs)
    later = jax.tree.leaves(later)
    inputs = [*inputs, *[(x, pl.ANY) for x in later]]

    def body(*refs):
        kernel(*refs[:first], *refs[first + len(later) :])

    def spec(block, place):
        return pl.BlockSpec(block, place)

    specs = []
    for item in inputs:
        if item[1] is None and item[0].dtype == jnp.int32:
            specs.append(pl.BlockSpec(memory_space=pltpu.SMEM))
        elif item[1] is pl.ANY:
            specs.append(pl.BlockSpec(memory_space=pl.ANY))
        elif item[1] is None:
            specs.append(whole_spec(item[0]))
        else:
            specs.append(spec(item[1], item[2]))
    held = sum(
        math.prod(x[1] or x[0].shape) * x[0].dtype.itemsize
        for x in (*inputs, *outputs)
        if x[1] is not pl.ANY
    )
    kept = sum(math.prod(x.shape) * jnp.dtype(x.dtype).itemsize for x in scratch)
    out_specs = [whole_spec(o[0]) if o[1] is None else spec(o[1], o[2]) for o in outputs]
    return pl.pallas_call(
        body,
        grid=(grid,),
        in_specs=specs,
        out_specs=out_specs,
        out_shape=[o[0] for o in outputs],
        scratch_shapes=list(scratch),
        input_output_aliases=aliases or {},
        cost_estimate=pl.CostEstimate(flops=1, bytes_accessed=1, transcendentals=0),
        compiler_params=pltpu.CompilerParams(
            dimension_semantics=("arbitrary",),
            vmem_limit_bytes=min(56 * MIB, 2 * held + kept + spare * MIB),
        ),
    )(*[x[0] for x in inputs])


def flip_route(size, bit):
    return [(i, i ^ bit) for i in range(size)]


def swap_half(half):
    return lax.ppermute(half, "seq", flip_route(lax.axis_size("seq"), 1))


def exchange(block, distance):
    if distance == 0:
        return lax.ppermute(block, "fsdp", flip_route(2, 1))
    return lax.ppermute(block, "seq", flip_route(lax.axis_size("seq"), distance))


def together(*values):
    return lax.optimization_barrier(values)


def column_steps(rows, columns):
    return 3 if rows * columns > 400_000 and columns % (3 * PAIR) == 0 else 1


def sum_cut(place, slot, held, gots, later):
    parts, rows, columns = held.shape
    return run(
        partial(sum_cut_kernel, slot=slot, arrived=len(gots)),
        1,
        [(place, None), *[(x, None) for x in (held, *gots)]],
        [(shape_of(rows, columns), None) for _ in range(parts)],
        later=later,
    )


def split_run(kernel, place, rows, inputs, outputs, later):
    steps = 3 if rows % 48 == 0 else 1

    def item(array):
        block = (*array.shape[:-2], rows // steps, array.shape[-1])
        lead = (0,) * (len(block) - 2)
        return (array, block, lambda i: (*lead, i, 0))

    return run(kernel, steps, [(place, None), *map(item, inputs)], [item(x) for x in outputs], later=later)


def join(place, slot, parts, later):
    rows, columns = parts[0].shape
    steps = column_steps(len(parts) * rows, columns)
    (whole,) = run(
        partial(join_kernel, slot=slot),
        steps,
        [(place, None), *[(x, (rows, columns // steps), lambda i: (0, i)) for x in parts]],
        [
            (
                shape_of(len(parts), rows, columns),
                (len(parts), rows, columns // steps),
                lambda i: (0, 0, i),
            )
        ],
        later=later,
    )
    return whole.reshape(len(parts) * rows, columns)


def bit_groups():
    stages = (lax.axis_size("seq") - 1).bit_length()
    return [(0, 1), (1, 1)] + [(at, min(2, stages - at)) for at in range(2, stages, 2)]


def member(group):
    at, bits = group
    return (lax.axis_index("seq") >> at) & ((1 << bits) - 1)


def sum_stages(place, keep, send):
    (got,), later = yield [(send, 1)]
    rows, columns = keep.shape[1] // 2, keep.shape[2]
    four = (4, rows, columns)
    part = shape_of(2, rows, columns // 2)
    hold_y, send_y, hold_x, send_x = split_run(
        split_first_kernel, place, rows, [keep.reshape(four), got.reshape(four)], [part] * 4,
        later,
    )
    (got_y, got_x), later = yield [(send_y, 0), (send_x, 2)]
    block, send_x, send_y = split_run(
        split_second_kernel,
        place,
        rows,
        [hold_y, got_y, hold_x, got_x],
        [shape_of(rows, columns), *[shape_of(rows, columns // 2)] * 2],
        later,
    )
    arrived, later = yield [(send_x, 2), (send_y, 0)]
    groups = list(enumerate(bit_groups()[2:], 3))
    for step, (slot, group) in enumerate(groups):
        count = 1 << group[1]
        size = block.shape[0] // count
        if step == 0:
            block, *sends = run(
                partial(split_third_kernel, slot=slot),
                1,
                [
                    (place, None),
                    *[(x.reshape(count, size, x.shape[1]), None) for x in (block, *arrived)],
                ],
                [(shape_of(size, columns), None) for _ in range(count)],
                later=later,
            )
        else:
            shape = (count, size, columns)
            block, *sends = sum_cut(
                place, slot, block.reshape(shape), [x.reshape(shape) for x in arrived], later
            )
        arrived, later = yield [(x, (d + 1) << group[0]) for d, x in enumerate(sends)]
    (block,) = sum_cut(place, len(groups) + 3, block[None], [x[None] for x in arrived], later)
    for slot, group in reversed([(2, (1, 1)), *groups]):
        held, later = yield [(block, d << group[0]) for d in range(1, 1 << group[1])]
        block = join(place, slot, [block, *held], later)
    (other,), _ = yield [(block, 1)]
    return block, other


class Chain:
    def __init__(self, stages):
        self.stages, self.result = stages, None
        self.post(next(stages))

    def post(self, sends, gate=None, arrived=0):
        blocks = [block for block, _ in sends]
        if gate is not None:
            held = together(*blocks, *gate.got[:arrived])
            blocks = list(held[: len(blocks)])
            gate.got[:arrived] = held[len(blocks) :]
        self.sent = blocks
        self.got = [exchange(block, distance) for block, (_, distance) in zip(blocks, sends)]

    def advance(self, *later, gate=None, arrived=0):
        try:
            self.post(self.stages.send((self.got, later)), gate, arrived)
        except StopIteration as end:
            self.result = end.value
        return self.sent


def window_tables(pos, rows, head_width):
    half = head_width // 2
    freqs = 10000.0 ** (-(jnp.arange(half, dtype=f32) * 2.0 / head_width))
    angle = pos.astype(f32)[..., None] * freqs
    cosine, sine = jnp.cos(angle), jnp.sin(angle)
    cosine = jnp.concatenate([cosine] * 4, -1)
    sine = jnp.concatenate([-sine, sine, -sine, sine], -1)
    span = pos.shape[1]
    index = jnp.arange(span, dtype=jnp.int32)

    def offsets(query_pos, query_index, key_pos, key_index):
        gap = key_index - query_index
        allowed = (
            (jnp.abs(gap) <= HALF_WINDOW)
            & (key_pos >= 0)
            & (query_pos >= 0)
            & ((gap > 0) | (query_pos >= -gap))
            & ((gap <= 0) | (key_pos >= gap))
        )
        return jnp.where(allowed, 0.0, masked_score).astype(f32)

    inner = slice(HALF_WINDOW, HALF_WINDOW + rows)
    outer_pos = jnp.concatenate([pos[:, HALF_WINDOW + rows :], pos[:, :HALF_WINDOW]], 1)
    outer_index = jnp.concatenate([index[HALF_WINDOW + rows :], index[:HALF_WINDOW]])
    bias = offsets(
        pos[:, inner, None], index[None, inner, None], pos[:, None, :], index[None, None, :]
    )
    bias_t = offsets(
        pos[:, None, inner], index[None, None, inner], pos[:, :, None], index[None, :, None]
    )
    bias_edge = offsets(
        outer_pos[:, None, :],
        outer_index[None, None, :],
        pos[:, inner, None],
        index[None, inner, None],
    )
    return cosine, sine, bias, bias_t, bias_edge


def local(tokens, positions, qkv_weight, out_weight, in_weight, down_weight, norm_gains, cotangent):
    num_seqs, rows, width = tokens.shape
    span = rows + 2 * HALF_WINDOW
    count = num_seqs * rows
    ffn = 2 * down_weight.shape[0]
    seq_index, own_y = lax.axis_index("seq"), lax.axis_index("fsdp")
    place = jnp.stack(
        [own_y, seq_index % 2, *[member(group) for group in bit_groups()[1:]], 0 * own_y]
    ).astype(jnp.int32)

    gain_width = norm_gains.shape[1]
    half = qkv_weight.shape[0] // 2
    (first_half,) = run(
        pack_first_kernel,
        1,
        [(place, None), (qkv_weight, None), (norm_gains, None)],
        [(shape_of(half + 16, qkv_weight.shape[1]), None)],
        spare=56,
    )
    far_qkv = exchange(first_half, 0)
    later_rows = half + down_weight.shape[0] // 6 + out_weight.shape[0] // 6
    halo = shape_of(num_seqs, HALF_WINDOW, width)
    later_half, tok_head, tok_tail = run(
        pack_later_kernel,
        1,
        [
            (place, None),
            *[(x, None) for x in (out_weight, in_weight, down_weight)],
            (tokens, None),
        ],
        [(shape_of(later_rows, in_weight.shape[1]), None), (halo, None), (halo, None)],
        later=first_half,
        spare=56,
    )
    far_later = exchange(later_half, 0)
    tok_before = passed_along(tok_tail, "seq", 1)
    tok_after = passed_along(tok_head, "seq", -1)
    padded_pos = jnp.pad(positions, ((0, 0), (HALF_WINDOW, HALF_WINDOW)), constant_values=-1)
    key_pos = lax.dynamic_slice_in_dim(padded_pos, seq_index * rows, span, 1)
    cosine, sine, bias, bias_t, bias_edge = window_tables(key_pos, rows, HEAD_DIM)
    far_qkv, tok_before, tok_after, cosine, sine, bias, bias_t, bias_edge = together(
        far_qkv, tok_before, tok_after, cosine, sine, bias, bias_t, bias_edge
    )
    w_qkv = (qkv_weight, far_qkv, swap_half(far_qkv))
    gains_other = far_qkv[qkv_weight.shape[0] // 2 :, :gain_width][: norm_gains.shape[0]]
    gains = jnp.where(
        own_y == 0,
        jnp.concatenate([norm_gains, gains_other], 1),
        jnp.concatenate([gains_other, norm_gains], 1),
    )

    def per_seq(i):
        return (i, 0, 0)

    def row_block(i):
        return (i, 0)

    def column_block(i):
        return (0, i)

    qkv_pieces = [(piece, None) for piece in w_qkv]
    wide = (1, span, width)
    hidden_one, query, keys, values, mixed, log_total = run(
        attend_kernel,
        num_seqs,
        [
            (place, None),
            (tok_before, (1, HALF_WINDOW, width), per_seq),
            (tokens, (1, rows, width), per_seq),
            (tok_after, (1, HALF_WINDOW, width), per_seq),
            (cosine, (1, span, PAIR), per_seq),
            (sine, (1, span, PAIR), per_seq),
            (bias, (1, rows, span), per_seq),
            (gains, None),
            *qkv_pieces,
        ],
        [
            (shape_of(num_seqs, rows, width), (1, rows, width), per_seq),
            (shape_of(num_seqs, span, width), wide, per_seq),
            (shape_of(num_seqs, span, width), wide, per_seq),
            (shape_of(num_seqs, span, width), wide, per_seq),
            (shape_of(num_seqs, rows, width), (1, rows, width), per_seq),
            (shape_of(num_seqs, HEAD_ROWS, PAIR, dtype=f32), (1, HEAD_ROWS, PAIR), per_seq),
        ],
        [pltpu.VMEM((width, 3 * width), bf16)],
        spare=56,
    )
    far_later, mixed = together(far_later, mixed)
    near_later = swap_half(far_later)

    flat_tokens = tokens.reshape(count, width)
    flat_dy = cotangent.reshape(count, width)
    flat_mixed = mixed.reshape(count, width)
    step = 2 * rows
    tok_block = (step, width)
    pack = HALF_WINDOW + HEAD_ROWS
    half_block = (2, pack, width)
    (
        layer_out, grad_stream, grad_mixed, grad_lo, grad_hi, inner_sum,
        hidden_two, grad_up, middle, grad_attn, gain_sum_two,
    ) = run(
        feed_kernel,
        count // step,
        [
            (place, None),
            (flat_tokens, tok_block, row_block),
            (flat_mixed, tok_block, row_block),
            (flat_dy, tok_block, row_block),
            (log_total, (2, HEAD_ROWS, PAIR), per_seq),
            (gains, None),
            *[(x, None) for x in (out_weight, in_weight, down_weight, far_later, near_later)],
        ],
        [
            (shape_of(count, width), tok_block, row_block),
            (shape_of(count, width, dtype=f32), tok_block, row_block),
            (shape_of(count, width), tok_block, row_block),
            (shape_of(num_seqs, pack, width), half_block, per_seq),
            (shape_of(num_seqs, pack, width), half_block, per_seq),
            (shape_of(num_seqs, 2 * HEAD_ROWS, PAIR, dtype=f32), (2, 2 * HEAD_ROWS, PAIR), per_seq),
            (shape_of(count, width), tok_block, row_block),
            (shape_of(count, 2 * ffn), (step, 2 * ffn), row_block),
            (shape_of(count, ffn), (step, ffn), row_block),
            (shape_of(count, width), tok_block, row_block),
            (shape_of(8, width, dtype=f32), None),
        ],
        [
            pltpu.VMEM((width, width), bf16),
            pltpu.VMEM((width, 2 * ffn), bf16),
            pltpu.VMEM((ffn, width), bf16),
        ],
        spare=56,
    )
    do_before = passed_along(grad_hi, "seq", 1)
    do_after = passed_along(grad_lo, "seq", -1)

    size = max(lax.axis_size("seq"), PAIR)
    bundle_rows = -(-(3 * width // 2 + ffn // 2 + width // 2) // size) * size
    bundle_part = shape_of(2, bundle_rows // 2, width)
    keep, send = run(
        grads_kernel,
        3,
        [
            (place, None),
            (hidden_two, None),
            (grad_up, (count, 2 * ffn // 3), column_block),
            (middle, (count, ffn // 3), column_block),
            (flat_dy, None),
            (flat_mixed, None),
            (grad_attn, (count, width // 3), column_block),
        ],
        [(bundle_part, None), (bundle_part, None)],
        [pltpu.VMEM((2 * bundle_rows, width), bf16)],
        spare=56,
    )
    do_before, do_after, send = together(do_before, do_after, send)
    chain_mlp = Chain(sum_stages(place, keep, send))
    heads = (1, 2 * HEAD_ROWS, PAIR)
    half_part = (1, HALF_WINDOW, width)
    edge_pack = (1, HEAD_ROWS, width)

    wider = 3 * width + 2 * PAIR

    def back_part(first, many, later, earlier=None):
        def at(i):
            return (first + i, 0, 0)

        def pack_rows(i):
            return (first + i, HALF_WINDOW // HEAD_ROWS, 0)

        return run(
            attend_back_kernel,
            many,
            [
                (query, wide, at),
                (keys, wide, at),
                (values, wide, at),
                (grad_mixed.reshape(num_seqs, rows, width), (1, rows, width), at),
                (do_before, half_part, at),
                (do_after, half_part, at),
                (inner_sum, heads, at),
                (do_before, edge_pack, pack_rows),
                (do_after, edge_pack, pack_rows),
                (bias_t, (1, span, rows), at),
                (bias_edge, (1, rows, PAIR), at),
                (cosine, (1, span, PAIR), at),
                (sine, (1, span, PAIR), at),
                *([] if earlier is None else [(earlier, pl.ANY)]),
            ],
            [
                (shape_of(num_seqs, rows, wider), (1, rows, wider), at),
                (shape_of(8, PAIR, dtype=f32), None),
            ],
            aliases=None if earlier is None else {13: 0},
            later=later,
            spare=56,
        )

    few = num_seqs // 2
    grads, mark = back_part(0, few, ())
    grads, _ = back_part(few, num_seqs - few, chain_mlp.advance(mark), grads)
    flat_grad = grads.reshape(count, wider)
    large = 4 * rows
    grad_tokens, gain_sum_one = run(
        stream_back_kernel,
        count // large,
        [
            (place, None),
            (flat_grad, (large, 3 * width), row_block),
            (flat_tokens, (large, width), row_block),
            (grad_stream, (large, width), row_block),
            (gains, None),
            *qkv_pieces,
        ],
        [
            (shape_of(count, width), (large, width), row_block),
            (shape_of(8, width, dtype=f32), None),
        ],
        [pltpu.VMEM((width, 3 * width), bf16)],
        spare=12,
    )
    sent = chain_mlp.advance(gain_sum_one)
    step_columns = wider // 2
    part = shape_of(2, width // 4, wider)
    block = (2, width // 4, step_columns)

    def last_block(i):
        return (0, 0, i)

    keep, send = run(
        grad_qkv_kernel,
        wider // step_columns,
        [
            (place, None),
            (hidden_one.reshape(count, width), None),
            (flat_grad, (count, step_columns), column_block),
            (gain_sum_one, None),
            (gain_sum_two, None),
        ],
        [(part, block, last_block), (part, block, last_block)],
        [pltpu.VMEM((width, step_columns), bf16)],
        later=sent,
        spare=12,
    )
    send, *chain_mlp.got = together(send, *chain_mlp.got)
    chain_qkv = Chain(sum_stages(place, keep, send))
    sent = chain_mlp.advance()
    sent = chain_qkv.advance(sent, gate=chain_mlp, arrived=2)
    sent = chain_mlp.advance(sent)
    sent = chain_qkv.advance(sent)
    while chain_mlp.result is None:
        sent = chain_qkv.advance(sent)
        sent = chain_mlp.advance(sent, gate=chain_qkv, arrived=len(chain_qkv.got))
    in_sum, down_sum, out_sum = run(
        finish_three_kernel,
        1,
        [(place, None), *[(x, None) for x in chain_mlp.result]],
        [
            (shape_of(*in_weight.shape, dtype=f32), None),
            (shape_of(*down_weight.shape, dtype=f32), None),
            (shape_of(*out_weight.shape, dtype=f32), None),
        ],
        [pltpu.VMEM((bundle_rows, width), bf16)],
        later=sent,
    )
    sent = down_sum
    while chain_qkv.result is None:
        sent = chain_qkv.advance(sent)
    qkv_sum, gains_sum = run(
        finish_qkv_kernel,
        1,
        [(place, None), *[(x, None) for x in chain_qkv.result]],
        [
            (shape_of(*qkv_weight.shape, dtype=f32), None),
            (shape_of(*norm_gains.shape, dtype=f32), None),
        ],
        [pltpu.VMEM((qkv_weight.shape[0], PAIR), f32)],
    )
    return (
        layer_out.reshape(tokens.shape),
        grad_tokens.reshape(tokens.shape),
        qkv_sum,
        out_sum,
        in_sum,
        down_sum,
        gains_sum,
    )


def solution(mesh):
    in_specs = (
        P("fsdp", "seq", None),
        P("fsdp", None),
        P("fsdp", None),
        P("fsdp", None),
        P("fsdp", None),
        P("fsdp", None),
        P(None, "fsdp"),
        P("fsdp", "seq", None),
    )
    out_specs = (
        P("fsdp", "seq", None),
        P("fsdp", "seq", None),
        P("fsdp", None),
        P("fsdp", None),
        P("fsdp", None),
        P("fsdp", None),
        P(None, "fsdp"),
    )
    return jax.shard_map(local, mesh=mesh, in_specs=in_specs, out_specs=out_specs, check_vma=False)
```

```python
import math
from functools import partial

import jax
import jax.numpy as jnp
from jax import lax
from jax.experimental import pallas as pl
from jax.experimental.pallas import tpu as pltpu
from jax.sharding import PartitionSpec as P

HEAD_DIM = 64
HALF_WINDOW = 64
PAIR = 128
HEAD_ROWS = 16
MIB = 1 << 20


masked_score = -1000000000.0
norm_epsilon = 1e-05
root_half = 0.7071067811865476
normal_peak = 0.3989422804014327
f32 = jnp.float32
bf16 = jnp.bfloat16


def passed_along(block, axis, distance):
    devices = range(lax.axis_size(axis))
    route = [(i - distance, i) for i in devices if i - distance in devices]
    return lax.ppermute(block, axis, route)


def norm_parts(values):
    center = values - jnp.mean(values, -1, keepdims=True)
    factor = lax.rsqrt(jnp.mean(center * center, -1, keepdims=True) + norm_epsilon)
    return (center * factor, factor)


def norm_back(grad_normed, normed, factor):
    first = jnp.mean(grad_normed, -1, keepdims=True)
    second = jnp.mean(grad_normed * normed, -1, keepdims=True)
    return factor * (grad_normed - first - normed * second)


def dot(left, right):
    return jnp.dot(left, right, preferred_element_type=f32)


def dot_right(left, right):
    return lax.dot_general(left, right, (((1,), (1,)), ((), ())), preferred_element_type=f32)


def dot_left(left, right):
    return lax.dot_general(left, right, (((0,), (0,)), ((), ())), preferred_element_type=f32)


def half_swap(value, first_half):
    return jnp.where(first_half, pltpu.roll(value, PAIR - 32, 1), pltpu.roll(value, 32, 1))


def place_weight(place_ref, whole, own, far, near):
    rows = own.shape[0]
    half = rows // 2
    index, core = place_ref[0], place_ref[1]
    other = (1 - index) * rows
    whole[pl.ds(pl.multiple_of(index * rows, half), rows), :] = own[...]
    whole[pl.ds(pl.multiple_of(other + core * half, half), half), :] = far[:half]
    whole[pl.ds(pl.multiple_of(other + (1 - core) * half, half), half), :] = near[:half]


def place_folded(place_ref, whole, own, far, near, at):
    rows, width = own.shape
    third = rows // 6
    index, core = place_ref[0], place_ref[1]
    other = (1 - index) * rows
    whole[pl.ds(pl.multiple_of(index * rows, third), rows), :] = own[...]
    for i in range(3):
        columns = slice(i * width, (i + 1) * width)
        first = other + core * 3 * third + i * third
        whole[pl.ds(pl.multiple_of(first, third), third), :] = far[at : at + third, columns]
        first = other + (1 - core) * 3 * third + i * third
        whole[pl.ds(pl.multiple_of(first, third), third), :] = near[at : at + third, columns]


def attend_kernel(
    place_ref, before, own, after, cos_ref, sin_ref, bias_ref, gain_ref, w_own, w_far, w_near,
    h1_ref, q_ref, k_ref, v_ref, mix_ref, lse_ref, weight,
):
    @pl.when(pl.program_id(0) == 0)
    def _():
        place_weight(place_ref, weight, w_own, w_far, w_near)

    width = own.shape[2]
    rows = own.shape[1]
    span = rows + 2 * HALF_WINDOW
    stream = jnp.concatenate([before[0], own[0], after[0]], 0).astype(f32)
    normed, _ = norm_parts(stream)
    hidden = (normed * gain_ref[0:1, :].astype(f32)).astype(bf16)
    h1_ref[0] = hidden[HALF_WINDOW : HALF_WINDOW + rows]
    lane = lax.broadcasted_iota(jnp.int32, (1, PAIR), 1)
    first_half = (lane % HEAD_DIM) < HEAD_DIM // 2
    first_head = lane < HEAD_DIM
    cosine, sine = cos_ref[0], sin_ref[0]
    for start in range(0, 3 * width, 2 * PAIR):
        part = dot(hidden, weight[:, start : start + 2 * PAIR])
        for sub in range(0, 2 * PAIR, PAIR):
            value = part[:, sub : sub + PAIR]
            column = (start + sub) % width
            if start + sub < 2 * width:
                value = value * cosine + half_swap(value, first_half) * sine
            if start + sub < width:
                q_ref[0, :, column : column + PAIR] = (value * HEAD_DIM**-0.5).astype(bf16)
            elif start + sub < 2 * width:
                k_ref[0, :, column : column + PAIR] = value.astype(bf16)
            else:
                v_ref[0, :, column : column + PAIR] = value.astype(bf16)
    bias = bias_ref[0]
    bias = jnp.concatenate([bias, bias], 0)
    log_totals = jnp.zeros((rows, PAIR), f32)
    for pair in range(width // PAIR):
        columns = slice(pair * PAIR, (pair + 1) * PAIR)
        query = q_ref[0, HALF_WINDOW : HALF_WINDOW + rows, columns]
        zero = jnp.zeros_like(query)
        both = jnp.concatenate(
            [jnp.where(first_head, query, zero), jnp.where(first_head, zero, query)], 0
        )
        scores = dot_right(both, k_ref[0, :, columns]) + bias
        top = jnp.max(scores, -1, keepdims=True)
        expo = jnp.exp(scores - top)
        total = jnp.sum(expo, -1, keepdims=True)
        log_total = top + jnp.log(total)
        probs = (expo * (1.0 / total)).astype(bf16)
        mixed = dot(probs, v_ref[0, :, columns])
        mix_ref[0, :, columns] = jnp.where(first_head, mixed[:rows], mixed[rows:]).astype(bf16)
        log_totals = jnp.where(lane == 2 * pair, log_total[:rows], log_totals)
        log_totals = jnp.where(lane == 2 * pair + 1, log_total[rows:], log_totals)
    lse_ref[0] = jnp.transpose(log_totals)[:HEAD_ROWS]


def three_parts(value):
    parts = []
    for _ in range(3):
        parts.append(value.astype(bf16))
        value = value - parts[-1].astype(f32)
    return parts


def feed_kernel(
    place_ref, tok_ref, mix_ref, dy_ref, lse_ref, gain_ref,
    out_own, in_own, down_own, far_ref, near_ref,
    layer_ref, dx1_ref, do_ref, lo_ref, hi_ref, rows_ref, h2_ref, dup_ref, mid_ref, dmix_ref, gsum_ref,
    w_out, w_in, w_down,
):
    @pl.when(pl.program_id(0) == 0)
    def _():
        at = in_own.shape[0] // 2
        place_weight(place_ref, w_in, in_own, far_ref, near_ref)
        for whole, own in ((w_down, down_own), (w_out, out_own)):
            place_folded(place_ref, whole, own, far_ref, near_ref, at)
            at += own.shape[0] // 6
        gsum_ref[...] = jnp.zeros_like(gsum_ref)

    rows, width = tok_ref.shape
    ffn = w_down.shape[0]
    block = 2 * HALF_WINDOW
    after_attn = tok_ref[...].astype(f32) + dot(mix_ref[...], w_out[...])
    normed, factor = norm_parts(after_attn)
    gain = gain_ref[1:2, :].astype(f32)
    h2_ref[...] = (normed * gain).astype(bf16)
    step = 3 * PAIR
    for start in range(0, ffn, step):
        columns = slice(start, start + step)
        gates = slice(ffn + start, ffn + start + step)
        act_input = dot(h2_ref[...], w_in[:, columns])
        gate_part = dot(h2_ref[...], w_in[:, gates])
        grad_middle = dot_right(dy_ref[...], w_down[columns, :])
        share = 0.5 + 0.5 * lax.erf(act_input * root_half)
        act_value = act_input * share
        slope = share + act_input * (normal_peak * jnp.exp(-0.5 * act_input * act_input))
        mid_ref[:, columns] = (act_value * gate_part).astype(bf16)
        dup_ref[:, columns] = (grad_middle * gate_part * slope).astype(bf16)
        dup_ref[:, gates] = (grad_middle * act_value).astype(bf16)
    layer_ref[...] = (after_attn + dot(mid_ref[...], w_down[...])).astype(bf16)
    grad_hidden = dot_right(dup_ref[...], w_in[...])
    gain_terms = grad_hidden * normed
    gsum_ref[...] += jnp.sum(gain_terms.reshape(rows // 8, 8, width), 0)
    grad_stream = dy_ref[...].astype(f32) + norm_back(grad_hidden * gain, normed, factor)
    dx1_ref[...] = grad_stream
    dmix_ref[...] = grad_stream.astype(bf16)
    grad_mixed = dot_right(dmix_ref[...], w_out[...]).astype(bf16)
    do_ref[...] = grad_mixed
    products = grad_mixed.astype(f32) * mix_ref[...].astype(f32)
    high = products.astype(bf16)
    low = (products - high.astype(f32)).astype(bf16)
    head_of = lax.broadcasted_iota(jnp.int32, (width, PAIR), 0) // HEAD_DIM
    slot = lax.broadcasted_iota(jnp.int32, (width, PAIR), 1)
    pick = jnp.where(head_of == slot, 1.0, 0.0).astype(bf16)
    delta = dot(high, pick) + dot(low, pick)
    for i in range(rows // block):
        piece = grad_mixed[i * block : (i + 1) * block]
        inner_sum = jnp.transpose(delta[i * block : (i + 1) * block])[:HEAD_ROWS]
        rows_ref[i, :HEAD_ROWS] = inner_sum
        rows_ref[i, HEAD_ROWS:] = lse_ref[i]
        parts = jnp.concatenate(three_parts(lse_ref[i]) + three_parts(inner_sum), 1)
        for ref, own in ((lo_ref, piece[:HALF_WINDOW]), (hi_ref, piece[HALF_WINDOW:])):
            ref[i, :HALF_WINDOW] = own
            ref[i, HALF_WINDOW:] = parts


def pack_first_kernel(place_ref, qkv_ref, gain_ref, out_ref):
    half = qkv_ref.shape[0] // 2
    count, width = gain_ref.shape
    out_ref[:half] = qkv_ref[pl.ds(pl.multiple_of(place_ref[1] * half, half), half), :]
    out_ref[half:] = jnp.zeros_like(out_ref[half:])
    filler = jnp.zeros((out_ref.shape[0] - half - count, width), bf16)
    out_ref[half:, :width] = jnp.concatenate([gain_ref[...], filler], 0)


def pack_later_kernel(place_ref, out_w, in_w, down_w, tok_ref, later_ref, head_ref, tail_ref):
    core = place_ref[1]
    half = in_w.shape[0] // 2
    width = out_w.shape[1]
    later_ref[:half] = in_w[pl.ds(pl.multiple_of(core * half, half), half), :]
    at = half
    for ref in (down_w, out_w):
        third = ref.shape[0] // 6
        for i in range(3):
            first = pl.multiple_of((core * 3 + i) * third, third)
            later_ref[at : at + third, i * width : (i + 1) * width] = ref[pl.ds(first, third), :]
        at += third
    rows = tok_ref.shape[1]
    for i in range(tok_ref.shape[0]):
        head_ref[i] = tok_ref[i, :HALF_WINDOW]
        tail_ref[i] = tok_ref[i, rows - HALF_WINDOW :]


def part_rows(place_ref, whole, keep_ref, send_ref):
    rows = keep_ref.shape[1]
    core = place_ref[1]
    for i in range(2):
        keep_ref[i] = whole[pl.ds(pl.multiple_of((2 * i + core) * rows, 16), rows), :]
        send_ref[i] = whole[pl.ds(pl.multiple_of((2 * i + 1 - core) * rows, 16), rows), :]


def as_column(row_groups):
    ones = jnp.ones((row_groups.shape[0], PAIR), bf16)
    return sum(dot_left(part, ones) for part in three_parts(row_groups))


def grad_qkv_kernel(
    place_ref, left_ref, right_ref, gain_ref, two_ref, w_own, w_far, w_near,
    keep_ref, send_ref, whole, weight, terms,
):
    step = pl.program_id(0)

    @pl.when(step == 0)
    def _():
        place_weight(place_ref, weight, w_own, w_far, w_near)
        terms[...] = jnp.zeros_like(terms)

    grad = dot_left(left_ref[...], right_ref[...])
    whole[...] = grad.astype(bf16)
    width = whole.shape[1]
    for start in range(0, weight.shape[1], width):
        size = min(width, weight.shape[1] - start)

        @pl.when(step == start // width)
        def _():
            total = terms[...]
            for at in range(0, size, PAIR):
                total += grad[:, at : at + PAIR] * weight[:, start + at : start + at + PAIR].astype(f32)
            terms[...] = total

    @pl.when(step == pl.num_programs(0) - 1)
    def _():
        lane = lax.broadcasted_iota(jnp.int32, (1, PAIR), 1)
        pick = jnp.where(lax.broadcasted_iota(jnp.int32, (2, PAIR), 0) == 0, 1.0, 0.0).astype(bf16)
        first = jnp.sum(terms[...], -1, keepdims=True) / dot_left(gain_ref[...], pick)
        second = as_column(two_ref[...])
        columns = jnp.where(lane == 0, first, jnp.where(lane == 1, second, 0.0)).astype(bf16)
        at = width - 2 * PAIR
        whole[:, at : at + PAIR] = columns
        whole[:, at + PAIR :] = jnp.zeros_like(columns)

    part_rows(place_ref, whole, keep_ref, send_ref)


def grads_kernel(place_ref, h2_ref, dup_ref, mid_ref, dy_ref, mix_ref, dmix_ref, keep_ref, send_ref, whole):
    step = pl.program_id(0)
    width = dy_ref.shape[1]
    half = whole.shape[0] // 2
    part = width // 2
    third = mid_ref.shape[1] // 2
    grad = dot_left(h2_ref[...], dup_ref[...]).astype(bf16)
    at = pl.multiple_of(step * part, part)
    whole[pl.ds(at, part), :] = grad[:part]
    whole[pl.ds(half + at, part), :] = grad[part:]
    grad = dot_left(mid_ref[...], dy_ref[...]).astype(bf16)
    for i in range(2):
        index = 2 * step + i
        owner = index // 3
        at = pl.multiple_of(owner * half + 3 * part + (index - 3 * owner) * third, 64)
        whole[pl.ds(at, third), :] = grad[i * third : (i + 1) * third]
    grad = dot_left(mix_ref[...], dmix_ref[...]).astype(bf16)
    columns = pl.ds(pl.multiple_of(step * (width // 3), PAIR), width // 3)
    at = 3 * part + 3 * third
    whole[at : at + part, columns] = grad[:part]
    whole[half + at : half + at + part, columns] = grad[part:]

    @pl.when(step == pl.num_programs(0) - 1)
    def _():
        spare = half - at - part
        if spare:
            for start in (at + part, half + at + part):
                whole[start : start + spare] = jnp.zeros((spare, width), bf16)
        part_rows(place_ref, whole, keep_ref, send_ref)


def total_of(*values):
    total = values[0].astype(f32)
    for value in values[1:]:
        total += value.astype(f32)
    return total.astype(bf16)


def split_first_kernel(place_ref, held, got, hold_y, send_y, hold_x, send_x):
    owner, bit = place_ref[0], place_ref[2]
    width = held.shape[2] // 2
    for j in range(2):
        for to, ref in ((owner, hold_y), (1 - owner, send_y)):
            ref[j] = total_of(held[2 * to + j, :, :width], got[2 * to + j, :, :width])
        for to, ref in ((bit, hold_x), (1 - bit, send_x)):
            ref[j] = total_of(held[2 * j + to, :, width:], got[2 * j + to, :, width:])


def split_second_kernel(place_ref, hold_y, got_y, hold_x, got_x, keep, send_x, send_y):
    owner, bit = place_ref[0], place_ref[2]
    width = hold_y.shape[2]
    keep[:, :width] = total_of(hold_y[bit], got_y[bit])
    send_x[...] = total_of(hold_y[1 - bit], got_y[1 - bit])
    keep[:, width:] = total_of(hold_x[owner], got_x[owner])
    send_y[...] = total_of(hold_x[1 - owner], got_x[1 - owner])


def split_third_kernel(place_ref, held, got_left, got_right, *refs, slot):
    index = place_ref[slot]
    width = got_left.shape[2]
    for d, ref in enumerate(refs):
        ref[:, :width] = total_of(held[index ^ d, :, :width], got_left[index ^ d])
        ref[:, width:] = total_of(held[index ^ d, :, width:], got_right[index ^ d])


def sum_cut_kernel(place_ref, held, *refs, slot, arrived):
    index = place_ref[slot]
    for d, out_ref in enumerate(refs[arrived:]):
        total = held[index ^ d].astype(f32)
        for got in refs[:arrived]:
            total += got[index ^ d].astype(f32)
        out_ref[...] = total.astype(bf16)


def join_kernel(place_ref, *refs, slot):
    index = place_ref[slot]
    for d, ref in enumerate(refs[:-1]):
        refs[-1][index ^ d] = ref[...]


def attend_back_kernel(
    q_ref, k_ref, v_ref, do_ref, do_before, do_after, own_rows, rows_before, rows_after,
    bias_ref, bias_edge, cos_ref, sin_ref, *refs,
):
    out_ref, mark_ref = refs[-2:]
    mark_ref[...] = jnp.zeros_like(mark_ref)
    rows, width = do_ref.shape[1], do_ref.shape[2]
    out_ref[0, :, 3 * width :] = jnp.zeros((rows, 2 * PAIR), bf16)
    inner = slice(HALF_WINDOW, HALF_WINDOW + rows)
    lane = lax.broadcasted_iota(jnp.int32, (1, PAIR), 1)
    first_half = (lane % HEAD_DIM) < HEAD_DIM // 2
    first_head = lane < HEAD_DIM
    top_rows = lax.broadcasted_iota(jnp.int32, (PAIR, 1), 0) < HEAD_DIM
    cosine, sine = cos_ref[0, inner], sin_ref[0, inner]
    bias = jnp.concatenate([bias_ref[0], bias_ref[0]], 1)
    offsets_edge = jnp.concatenate([bias_edge[0], bias_edge[0]], 1)

    def split(value):
        zero = jnp.zeros_like(value)
        return jnp.concatenate(
            [jnp.where(first_head, value, zero), jnp.where(first_head, zero, value)], 0
        )

    after_lane = lane < HALF_WINDOW
    edge = []
    for base in (3 * PAIR, 0):
        value = jnp.zeros((HEAD_ROWS, PAIR), f32)
        for at in (base, base + PAIR, base + 2 * PAIR):
            columns = slice(at, at + PAIR)
            value += jnp.where(
                after_lane, rows_after[0, :, columns].astype(f32), rows_before[0, :, columns].astype(f32)
            )
        edge.append(value)
    edge_sum, edge_lse = edge
    own_sum, own_lse = own_rows[0, :HEAD_ROWS], own_rows[0, HEAD_ROWS:]

    def row_of(value, pair):
        at = 2 * pair
        return jnp.concatenate([value[at : at + 1, :], value[at + 1 : at + 2, :]], 1)

    def back(keys, values, query, grad_mixed, offsets, log_total, inner_sum):
        probs = jnp.exp(dot_right(keys, query) + offsets - log_total)
        grad_probs = dot_right(values, grad_mixed)
        return probs.astype(bf16), (probs * (grad_probs - inner_sum)).astype(bf16)

    def rotated_back(value):
        return value * cosine - half_swap(value, first_half) * sine

    for pair in range(width // PAIR):
        columns = slice(pair * PAIR, (pair + 1) * PAIR)
        keys, values = k_ref[0, :, columns], v_ref[0, :, columns]
        query = split(q_ref[0, inner, columns])
        grad_mixed = split(do_ref[0, :, columns])
        probs, grad_scores = back(
            keys, values, query, grad_mixed, bias,
            row_of(own_lse, pair), row_of(own_sum, pair),
        )
        query_edge = split(
            jnp.concatenate(
                [
                    q_ref[0, HALF_WINDOW + rows :, columns],
                    q_ref[0, :HALF_WINDOW, columns],
                ],
                0,
            )
        )
        grad_edge = split(jnp.concatenate([do_after[0, :, columns], do_before[0, :, columns]], 0))
        probs_edge, scores_edge = back(
            keys[inner], values[inner], query_edge, grad_edge, offsets_edge,
            row_of(edge_lse, pair), row_of(edge_sum, pair),
        )
        grad_values = dot(
            jnp.concatenate([probs[inner], probs_edge], 1),
            jnp.concatenate([grad_mixed, grad_edge], 0),
        )
        grad_keys = dot(
            jnp.concatenate([grad_scores[inner], scores_edge], 1),
            jnp.concatenate([query, query_edge], 0),
        )
        grad_query = dot_left(grad_scores, keys)
        grad_query = jnp.where(first_head, grad_query[:rows], grad_query[rows:]) * HEAD_DIM**-0.5
        out_ref[0, :, columns] = rotated_back(grad_query).astype(bf16)
        out_ref[0, :, width + pair * PAIR : width + (pair + 1) * PAIR] = rotated_back(
            grad_keys
        ).astype(bf16)
        out_ref[0, :, 2 * width + pair * PAIR : 2 * width + (pair + 1) * PAIR] = (
            grad_values.astype(bf16)
        )


def stream_back_kernel(
    place_ref, dqkv_ref, tok_ref, dx1_ref, gain_ref, w_own, w_far, w_near, out_ref, weight
):
    @pl.when(pl.program_id(0) == 0)
    def _():
        place_weight(place_ref, weight, w_own, w_far, w_near)

    grad_hidden = dot_right(dqkv_ref[...], weight[...])
    normed, factor = norm_parts(tok_ref[...].astype(f32))
    grad_normed = grad_hidden * gain_ref[0:1, :].astype(f32)
    out_ref[...] = (dx1_ref[...] + norm_back(grad_normed, normed, factor)).astype(bf16)


def join_halves(place_ref, whole, mine, other):
    rows = mine.shape[0]
    core = place_ref[1]
    whole[pl.ds(pl.multiple_of(core * rows, 16), rows), :] = mine[...]
    whole[pl.ds(pl.multiple_of((1 - core) * rows, 16), rows), :] = other[...]


def finish_qkv_kernel(place_ref, mine, other, out_ref, gain_ref, columns):
    rows = mine.shape[0]
    core = place_ref[1]
    width = out_ref.shape[1]
    for ref, at in ((mine, core * rows), (other, (1 - core) * rows)):
        at = pl.ds(pl.multiple_of(at, 16), rows)
        out_ref[at, :] = ref[:, :width].astype(f32)
        columns[at, :] = ref[:, width : width + PAIR].astype(f32)
    gain_ref[...] = columns[...].T[: gain_ref.shape[0]]


def finish_three_kernel(place_ref, mine, other, in_ref, down_ref, out_ref, whole):
    join_halves(place_ref, whole, mine, other)
    width = whole.shape[1]
    at = 0
    for i in range(in_ref.shape[1] // width):
        in_ref[:, i * width : (i + 1) * width] = whole[at : at + in_ref.shape[0]].astype(f32)
        at += in_ref.shape[0]
    for ref in (down_ref, out_ref):
        ref[...] = whole[at : at + ref.shape[0]].astype(f32)
        at += ref.shape[0]


def shape_of(*dims, dtype=bf16):
    return jax.ShapeDtypeStruct(dims, dtype)


def whole_spec(array):
    return pl.BlockSpec(array.shape, lambda i: (0,) * array.ndim)


def run(kernel, grid, inputs, outputs, scratch=(), aliases=None, later=(), spare=4):
    first = len(inputs)
    later = jax.tree.leaves(later)
    inputs = [*inputs, *[(x, pl.ANY) for x in later]]

    def body(*refs):
        kernel(*refs[:first], *refs[first + len(later) :])

    def spec(block, place):
        return pl.BlockSpec(block, place)

    specs = []
    for item in inputs:
        if item[1] is None and item[0].dtype == jnp.int32:
            specs.append(pl.BlockSpec(memory_space=pltpu.SMEM))
        elif item[1] is pl.ANY:
            specs.append(pl.BlockSpec(memory_space=pl.ANY))
        elif item[1] is None:
            specs.append(whole_spec(item[0]))
        else:
            specs.append(spec(item[1], item[2]))
    held = sum(
        math.prod(x[1] or x[0].shape) * x[0].dtype.itemsize
        for x in (*inputs, *outputs)
        if x[1] is not pl.ANY
    )
    kept = sum(math.prod(x.shape) * jnp.dtype(x.dtype).itemsize for x in scratch)
    out_specs = [whole_spec(o[0]) if o[1] is None else spec(o[1], o[2]) for o in outputs]
    return pl.pallas_call(
        body,
        grid=(grid,),
        in_specs=specs,
        out_specs=out_specs,
        out_shape=[o[0] for o in outputs],
        scratch_shapes=list(scratch),
        input_output_aliases=aliases or {},
        cost_estimate=pl.CostEstimate(flops=1, bytes_accessed=1, transcendentals=0),
        compiler_params=pltpu.CompilerParams(
            dimension_semantics=("arbitrary",),
            vmem_limit_bytes=min(56 * MIB, 2 * held + kept + spare * MIB),
        ),
    )(*[x[0] for x in inputs])


def flip_route(size, bit):
    return [(i, i ^ bit) for i in range(size)]


def swap_half(half):
    return lax.ppermute(half, "seq", flip_route(lax.axis_size("seq"), 1))


def exchange(block, distance):
    if distance == 0:
        return lax.ppermute(block, "fsdp", flip_route(2, 1))
    return lax.ppermute(block, "seq", flip_route(lax.axis_size("seq"), distance))


def together(*values):
    return lax.optimization_barrier(values)


def column_steps(rows, columns):
    return 3 if rows * columns > 400_000 and columns % (3 * PAIR) == 0 else 1


def sum_cut(place, slot, held, gots, later):
    parts, rows, columns = held.shape
    return run(
        partial(sum_cut_kernel, slot=slot, arrived=len(gots)),
        1,
        [(place, None), *[(x, None) for x in (held, *gots)]],
        [(shape_of(rows, columns), None) for _ in range(parts)],
        later=later,
    )


def split_run(kernel, place, rows, inputs, outputs, later):
    steps = 3 if rows % 48 == 0 else 1

    def item(array):
        block = (*array.shape[:-2], rows // steps, array.shape[-1])
        lead = (0,) * (len(block) - 2)
        return (array, block, lambda i: (*lead, i, 0))

    return run(kernel, steps, [(place, None), *map(item, inputs)], [item(x) for x in outputs], later=later)


def join(place, slot, parts, later):
    rows, columns = parts[0].shape
    steps = column_steps(len(parts) * rows, columns)
    (whole,) = run(
        partial(join_kernel, slot=slot),
        steps,
        [(place, None), *[(x, (rows, columns // steps), lambda i: (0, i)) for x in parts]],
        [
            (
                shape_of(len(parts), rows, columns),
                (len(parts), rows, columns // steps),
                lambda i: (0, 0, i),
            )
        ],
        later=later,
    )
    return whole.reshape(len(parts) * rows, columns)


def bit_groups():
    stages = (lax.axis_size("seq") - 1).bit_length()
    return [(0, 1), (1, 1)] + [(at, min(2, stages - at)) for at in range(2, stages, 2)]


def member(group):
    at, bits = group
    return (lax.axis_index("seq") >> at) & ((1 << bits) - 1)


def sum_stages(place, keep, send):
    (got,), later = yield [(send, 1)]
    rows, columns = keep.shape[1] // 2, keep.shape[2]
    four = (4, rows, columns)
    part = shape_of(2, rows, columns // 2)
    hold_y, send_y, hold_x, send_x = split_run(
        split_first_kernel, place, rows, [keep.reshape(four), got.reshape(four)], [part] * 4,
        later,
    )
    (got_y, got_x), later = yield [(send_y, 0), (send_x, 2)]
    block, send_x, send_y = split_run(
        split_second_kernel,
        place,
        rows,
        [hold_y, got_y, hold_x, got_x],
        [shape_of(rows, columns), *[shape_of(rows, columns // 2)] * 2],
        later,
    )
    arrived, later = yield [(send_x, 2), (send_y, 0)]
    groups = list(enumerate(bit_groups()[2:], 3))
    for step, (slot, group) in enumerate(groups):
        count = 1 << group[1]
        size = block.shape[0] // count
        if step == 0:
            block, *sends = run(
                partial(split_third_kernel, slot=slot),
                1,
                [
                    (place, None),
                    *[(x.reshape(count, size, x.shape[1]), None) for x in (block, *arrived)],
                ],
                [(shape_of(size, columns), None) for _ in range(count)],
                later=later,
            )
        else:
            shape = (count, size, columns)
            block, *sends = sum_cut(
                place, slot, block.reshape(shape), [x.reshape(shape) for x in arrived], later
            )
        arrived, later = yield [(x, (d + 1) << group[0]) for d, x in enumerate(sends)]
    (block,) = sum_cut(place, len(groups) + 3, block[None], [x[None] for x in arrived], later)
    for slot, group in reversed([(2, (1, 1)), *groups]):
        held, later = yield [(block, d << group[0]) for d in range(1, 1 << group[1])]
        block = join(place, slot, [block, *held], later)
    (other,), _ = yield [(block, 1)]
    return block, other


class Chain:
    def __init__(self, stages):
        self.stages, self.result = stages, None
        self.post(next(stages))

    def post(self, sends, gate=None, arrived=0):
        blocks = [block for block, _ in sends]
        if gate is not None:
            held = together(*blocks, *gate.got[:arrived])
            blocks = list(held[: len(blocks)])
            gate.got[:arrived] = held[len(blocks) :]
        self.sent = blocks
        self.got = [exchange(block, distance) for block, (_, distance) in zip(blocks, sends)]

    def advance(self, *later, gate=None, arrived=0):
        try:
            self.post(self.stages.send((self.got, later)), gate, arrived)
        except StopIteration as end:
            self.result = end.value
        return self.sent


def window_tables(pos, rows, head_width):
    half = head_width // 2
    freqs = 10000.0 ** (-(jnp.arange(half, dtype=f32) * 2.0 / head_width))
    angle = pos.astype(f32)[..., None] * freqs
    cosine, sine = jnp.cos(angle), jnp.sin(angle)
    cosine = jnp.concatenate([cosine] * 4, -1)
    sine = jnp.concatenate([-sine, sine, -sine, sine], -1)
    span = pos.shape[1]
    index = jnp.arange(span, dtype=jnp.int32)

    def offsets(query_pos, query_index, key_pos, key_index):
        gap = key_index - query_index
        allowed = (
            (jnp.abs(gap) <= HALF_WINDOW)
            & (key_pos >= 0)
            & (query_pos >= 0)
            & ((gap > 0) | (query_pos >= -gap))
            & ((gap <= 0) | (key_pos >= gap))
        )
        return jnp.where(allowed, 0.0, masked_score).astype(f32)

    inner = slice(HALF_WINDOW, HALF_WINDOW + rows)
    outer_pos = jnp.concatenate([pos[:, HALF_WINDOW + rows :], pos[:, :HALF_WINDOW]], 1)
    outer_index = jnp.concatenate([index[HALF_WINDOW + rows :], index[:HALF_WINDOW]])
    bias = offsets(
        pos[:, inner, None], index[None, inner, None], pos[:, None, :], index[None, None, :]
    )
    bias_t = offsets(
        pos[:, None, inner], index[None, None, inner], pos[:, :, None], index[None, :, None]
    )
    bias_edge = offsets(
        outer_pos[:, None, :],
        outer_index[None, None, :],
        pos[:, inner, None],
        index[None, inner, None],
    )
    return cosine, sine, bias, bias_t, bias_edge


def local(tokens, positions, qkv_weight, out_weight, in_weight, down_weight, norm_gains, cotangent):
    num_seqs, rows, width = tokens.shape
    span = rows + 2 * HALF_WINDOW
    count = num_seqs * rows
    ffn = 2 * down_weight.shape[0]
    seq_index, own_y = lax.axis_index("seq"), lax.axis_index("fsdp")
    place = jnp.stack(
        [own_y, seq_index % 2, *[member(group) for group in bit_groups()[1:]], 0 * own_y]
    ).astype(jnp.int32)

    gain_width = norm_gains.shape[1]
    half = qkv_weight.shape[0] // 2
    (first_half,) = run(
        pack_first_kernel,
        1,
        [(place, None), (qkv_weight, None), (norm_gains, None)],
        [(shape_of(half + 16, qkv_weight.shape[1]), None)],
        spare=56,
    )
    far_qkv = exchange(first_half, 0)
    later_rows = half + down_weight.shape[0] // 6 + out_weight.shape[0] // 6
    halo = shape_of(num_seqs, HALF_WINDOW, width)
    later_half, tok_head, tok_tail = run(
        pack_later_kernel,
        1,
        [
            (place, None),
            *[(x, None) for x in (out_weight, in_weight, down_weight)],
            (tokens, None),
        ],
        [(shape_of(later_rows, in_weight.shape[1]), None), (halo, None), (halo, None)],
        later=first_half,
        spare=56,
    )
    far_later = exchange(later_half, 0)
    tok_before = passed_along(tok_tail, "seq", 1)
    tok_after = passed_along(tok_head, "seq", -1)
    padded_pos = jnp.pad(positions, ((0, 0), (HALF_WINDOW, HALF_WINDOW)), constant_values=-1)
    key_pos = lax.dynamic_slice_in_dim(padded_pos, seq_index * rows, span, 1)
    cosine, sine, bias, bias_t, bias_edge = window_tables(key_pos, rows, HEAD_DIM)
    far_qkv, tok_before, tok_after, cosine, sine, bias, bias_t, bias_edge = together(
        far_qkv, tok_before, tok_after, cosine, sine, bias, bias_t, bias_edge
    )
    w_qkv = (qkv_weight, far_qkv, swap_half(far_qkv))
    gains_other = far_qkv[qkv_weight.shape[0] // 2 :, :gain_width][: norm_gains.shape[0]]
    gains = jnp.where(
        own_y == 0,
        jnp.concatenate([norm_gains, gains_other], 1),
        jnp.concatenate([gains_other, norm_gains], 1),
    )

    def per_seq(i):
        return (i, 0, 0)

    def row_block(i):
        return (i, 0)

    def column_block(i):
        return (0, i)

    qkv_pieces = [(piece, None) for piece in w_qkv]
    wide = (1, span, width)
    hidden_one, query, keys, values, mixed, log_total = run(
        attend_kernel,
        num_seqs,
        [
            (place, None),
            (tok_before, (1, HALF_WINDOW, width), per_seq),
            (tokens, (1, rows, width), per_seq),
            (tok_after, (1, HALF_WINDOW, width), per_seq),
            (cosine, (1, span, PAIR), per_seq),
            (sine, (1, span, PAIR), per_seq),
            (bias, (1, rows, span), per_seq),
            (gains, None),
            *qkv_pieces,
        ],
        [
            (shape_of(num_seqs, rows, width), (1, rows, width), per_seq),
            (shape_of(num_seqs, span, width), wide, per_seq),
            (shape_of(num_seqs, span, width), wide, per_seq),
            (shape_of(num_seqs, span, width), wide, per_seq),
            (shape_of(num_seqs, rows, width), (1, rows, width), per_seq),
            (shape_of(num_seqs, HEAD_ROWS, PAIR, dtype=f32), (1, HEAD_ROWS, PAIR), per_seq),
        ],
        [pltpu.VMEM((width, 3 * width), bf16)],
        spare=56,
    )
    far_later, mixed = together(far_later, mixed)
    near_later = swap_half(far_later)

    flat_tokens = tokens.reshape(count, width)
    flat_dy = cotangent.reshape(count, width)
    flat_mixed = mixed.reshape(count, width)
    step = 2 * rows
    tok_block = (step, width)
    pack = HALF_WINDOW + HEAD_ROWS
    half_block = (2, pack, width)
    (
        layer_out, grad_stream, grad_mixed, grad_lo, grad_hi, inner_sum,
        hidden_two, grad_up, middle, grad_attn, gain_sum_two,
    ) = run(
        feed_kernel,
        count // step,
        [
            (place, None),
            (flat_tokens, tok_block, row_block),
            (flat_mixed, tok_block, row_block),
            (flat_dy, tok_block, row_block),
            (log_total, (2, HEAD_ROWS, PAIR), per_seq),
            (gains, None),
            *[(x, None) for x in (out_weight, in_weight, down_weight, far_later, near_later)],
        ],
        [
            (shape_of(count, width), tok_block, row_block),
            (shape_of(count, width, dtype=f32), tok_block, row_block),
            (shape_of(count, width), tok_block, row_block),
            (shape_of(num_seqs, pack, width), half_block, per_seq),
            (shape_of(num_seqs, pack, width), half_block, per_seq),
            (shape_of(num_seqs, 2 * HEAD_ROWS, PAIR, dtype=f32), (2, 2 * HEAD_ROWS, PAIR), per_seq),
            (shape_of(count, width), tok_block, row_block),
            (shape_of(count, 2 * ffn), (step, 2 * ffn), row_block),
            (shape_of(count, ffn), (step, ffn), row_block),
            (shape_of(count, width), tok_block, row_block),
            (shape_of(8, width, dtype=f32), None),
        ],
        [
            pltpu.VMEM((width, width), bf16),
            pltpu.VMEM((width, 2 * ffn), bf16),
            pltpu.VMEM((ffn, width), bf16),
        ],
        spare=56,
    )
    do_before = passed_along(grad_hi, "seq", 1)
    do_after = passed_along(grad_lo, "seq", -1)

    size = max(lax.axis_size("seq"), PAIR)
    bundle_rows = -(-(3 * width // 2 + ffn // 2 + width // 2) // size) * size
    bundle_part = shape_of(2, bundle_rows // 2, width)
    keep, send = run(
        grads_kernel,
        3,
        [
            (place, None),
            (hidden_two, None),
            (grad_up, (count, 2 * ffn // 3), column_block),
            (middle, (count, ffn // 3), column_block),
            (flat_dy, None),
            (flat_mixed, None),
            (grad_attn, (count, width // 3), column_block),
        ],
        [(bundle_part, None), (bundle_part, None)],
        [pltpu.VMEM((2 * bundle_rows, width), bf16)],
        spare=56,
    )
    do_before, do_after, send = together(do_before, do_after, send)
    chain_mlp = Chain(sum_stages(place, keep, send))
    heads = (1, 2 * HEAD_ROWS, PAIR)
    half_part = (1, HALF_WINDOW, width)
    edge_pack = (1, HEAD_ROWS, width)

    wider = 3 * width + 2 * PAIR

    def back_part(first, many, later, earlier=None):
        def at(i):
            return (first + i, 0, 0)

        def pack_rows(i):
            return (first + i, HALF_WINDOW // HEAD_ROWS, 0)

        return run(
            attend_back_kernel,
            many,
            [
                (query, wide, at),
                (keys, wide, at),
                (values, wide, at),
                (grad_mixed.reshape(num_seqs, rows, width), (1, rows, width), at),
                (do_before, half_part, at),
                (do_after, half_part, at),
                (inner_sum, heads, at),
                (do_before, edge_pack, pack_rows),
                (do_after, edge_pack, pack_rows),
                (bias_t, (1, span, rows), at),
                (bias_edge, (1, rows, PAIR), at),
                (cosine, (1, span, PAIR), at),
                (sine, (1, span, PAIR), at),
                *([] if earlier is None else [(earlier, pl.ANY)]),
            ],
            [
                (shape_of(num_seqs, rows, wider), (1, rows, wider), at),
                (shape_of(8, PAIR, dtype=f32), None),
            ],
            aliases=None if earlier is None else {13: 0},
            later=later,
            spare=56,
        )

    few = num_seqs // 2
    grads, mark = back_part(0, few, ())
    grads, _ = back_part(few, num_seqs - few, chain_mlp.advance(mark), grads)
    flat_grad = grads.reshape(count, wider)
    step_columns = wider // 2
    part = shape_of(2, width // 4, wider)
    block = (2, width // 4, step_columns)

    def last_block(i):
        return (0, 0, i)

    keep, send = run(
        grad_qkv_kernel,
        wider // step_columns,
        [
            (place, None),
            (hidden_one.reshape(count, width), None),
            (flat_grad, (count, step_columns), column_block),
            (gains, None),
            (gain_sum_two, None),
            *qkv_pieces,
        ],
        [(part, block, last_block), (part, block, last_block)],
        [
            pltpu.VMEM((width, step_columns), bf16),
            pltpu.VMEM((width, 3 * width), bf16),
            pltpu.VMEM((width, PAIR), f32),
        ],
        spare=16,
    )
    send, *chain_mlp.got = together(send, *chain_mlp.got)
    chain_qkv = Chain(sum_stages(place, keep, send))
    sent = chain_mlp.advance(keep)
    sent = chain_qkv.advance(sent)
    sent = chain_mlp.advance(sent)
    large = 4 * rows
    (grad_tokens,) = run(
        stream_back_kernel,
        count // large,
        [
            (place, None),
            (flat_grad, (large, 3 * width), row_block),
            (flat_tokens, (large, width), row_block),
            (grad_stream, (large, width), row_block),
            (gains, None),
            *qkv_pieces,
        ],
        [(shape_of(count, width), (large, width), row_block)],
        [pltpu.VMEM((width, 3 * width), bf16)],
        later=sent,
        spare=12,
    )
    sent = chain_qkv.advance(grad_tokens, gate=chain_mlp, arrived=2)
    sent = chain_mlp.advance(sent)
    while chain_mlp.result is None:
        sent = chain_qkv.advance(sent)
        sent = chain_mlp.advance(sent, gate=chain_qkv, arrived=len(chain_qkv.got))
    in_sum, down_sum, out_sum = run(
        finish_three_kernel,
        1,
        [(place, None), *[(x, None) for x in chain_mlp.result]],
        [
            (shape_of(*in_weight.shape, dtype=f32), None),
            (shape_of(*down_weight.shape, dtype=f32), None),
            (shape_of(*out_weight.shape, dtype=f32), None),
        ],
        [pltpu.VMEM((bundle_rows, width), bf16)],
        later=sent,
    )
    sent = down_sum
    while chain_qkv.result is None:
        sent = chain_qkv.advance(sent)
    qkv_sum, gains_sum = run(
        finish_qkv_kernel,
        1,
        [(place, None), *[(x, None) for x in chain_qkv.result]],
        [
            (shape_of(*qkv_weight.shape, dtype=f32), None),
            (shape_of(*norm_gains.shape, dtype=f32), None),
        ],
        [pltpu.VMEM((qkv_weight.shape[0], PAIR), f32)],
    )
    return (
        layer_out.reshape(tokens.shape),
        grad_tokens.reshape(tokens.shape),
        qkv_sum,
        out_sum,
        in_sum,
        down_sum,
        gains_sum,
    )


def solution(mesh):
    in_specs = (
        P("fsdp", "seq", None),
        P("fsdp", None),
        P("fsdp", None),
        P("fsdp", None),
        P("fsdp", None),
        P("fsdp", None),
        P(None, "fsdp"),
        P("fsdp", "seq", None),
    )
    out_specs = (
        P("fsdp", "seq", None),
        P("fsdp", "seq", None),
        P("fsdp", None),
        P("fsdp", None),
        P("fsdp", None),
        P("fsdp", None),
        P(None, "fsdp"),
    )
    return jax.shard_map(local, mesh=mesh, in_specs=in_specs, out_specs=out_specs, check_vma=False)
```

```python
import math
from functools import partial

import jax
import jax.numpy as jnp
from jax import lax
from jax.experimental import pallas as pl
from jax.experimental.pallas import tpu as pltpu
from jax.sharding import PartitionSpec as P

HEAD_DIM = 64
HALF_WINDOW = 64
PAIR = 128
HEAD_ROWS = 16
MIB = 1 << 20


masked_score = -1000000000.0
norm_epsilon = 1e-05
root_half = 0.7071067811865476
normal_peak = 0.3989422804014327
f32 = jnp.float32
bf16 = jnp.bfloat16


def passed_along(block, axis, distance):
    devices = range(lax.axis_size(axis))
    route = [(i - distance, i) for i in devices if i - distance in devices]
    return lax.ppermute(block, axis, route)


def norm_parts(values):
    center = values - jnp.mean(values, -1, keepdims=True)
    factor = lax.rsqrt(jnp.mean(center * center, -1, keepdims=True) + norm_epsilon)
    return (center * factor, factor)


def norm_back(grad_normed, normed, factor):
    first = jnp.mean(grad_normed, -1, keepdims=True)
    second = jnp.mean(grad_normed * normed, -1, keepdims=True)
    return factor * (grad_normed - first - normed * second)


def dot(left, right):
    return jnp.dot(left, right, preferred_element_type=f32)


def dot_right(left, right):
    return lax.dot_general(left, right, (((1,), (1,)), ((), ())), preferred_element_type=f32)


def dot_left(left, right):
    return lax.dot_general(left, right, (((0,), (0,)), ((), ())), preferred_element_type=f32)


def half_swap(value, first_half):
    return jnp.where(first_half, pltpu.roll(value, PAIR - 32, 1), pltpu.roll(value, 32, 1))


def place_weight(place_ref, whole, own, far, near):
    rows = own.shape[0]
    half = rows // 2
    index, core = place_ref[0], place_ref[1]
    other = (1 - index) * rows
    whole[pl.ds(pl.multiple_of(index * rows, half), rows), :] = own[...]
    whole[pl.ds(pl.multiple_of(other + core * half, half), half), :] = far[:half]
    whole[pl.ds(pl.multiple_of(other + (1 - core) * half, half), half), :] = near[:half]


def place_folded(place_ref, whole, own, far, near, at):
    rows, width = own.shape
    third = rows // 6
    index, core = place_ref[0], place_ref[1]
    other = (1 - index) * rows
    whole[pl.ds(pl.multiple_of(index * rows, third), rows), :] = own[...]
    for i in range(3):
        columns = slice(i * width, (i + 1) * width)
        first = other + core * 3 * third + i * third
        whole[pl.ds(pl.multiple_of(first, third), third), :] = far[at : at + third, columns]
        first = other + (1 - core) * 3 * third + i * third
        whole[pl.ds(pl.multiple_of(first, third), third), :] = near[at : at + third, columns]


def attend_kernel(
    place_ref, before, own, after, cos_ref, sin_ref, bias_ref, gain_ref, w_own, w_far, w_near,
    h1_ref, q_ref, k_ref, v_ref, mix_ref, lse_ref, weight,
):
    @pl.when(pl.program_id(0) == 0)
    def _():
        place_weight(place_ref, weight, w_own, w_far, w_near)

    width = own.shape[2]
    rows = own.shape[1]
    span = rows + 2 * HALF_WINDOW
    stream = jnp.concatenate([before[0], own[0], after[0]], 0).astype(f32)
    normed, _ = norm_parts(stream)
    hidden = (normed * gain_ref[0:1, :].astype(f32)).astype(bf16)
    h1_ref[0] = hidden[HALF_WINDOW : HALF_WINDOW + rows]
    lane = lax.broadcasted_iota(jnp.int32, (1, PAIR), 1)
    first_half = (lane % HEAD_DIM) < HEAD_DIM // 2
    first_head = lane < HEAD_DIM
    cosine, sine = cos_ref[0], sin_ref[0]
    for start in range(0, 3 * width, 2 * PAIR):
        part = dot(hidden, weight[:, start : start + 2 * PAIR])
        for sub in range(0, 2 * PAIR, PAIR):
            value = part[:, sub : sub + PAIR]
            column = (start + sub) % width
            if start + sub < 2 * width:
                value = value * cosine + half_swap(value, first_half) * sine
            if start + sub < width:
                q_ref[0, :, column : column + PAIR] = (value * HEAD_DIM**-0.5).astype(bf16)
            elif start + sub < 2 * width:
                k_ref[0, :, column : column + PAIR] = value.astype(bf16)
            else:
                v_ref[0, :, column : column + PAIR] = value.astype(bf16)
    bias = bias_ref[0]
    bias = jnp.concatenate([bias, bias], 0)
    log_totals = jnp.zeros((rows, PAIR), f32)
    for pair in range(width // PAIR):
        columns = slice(pair * PAIR, (pair + 1) * PAIR)
        query = q_ref[0, HALF_WINDOW : HALF_WINDOW + rows, columns]
        zero = jnp.zeros_like(query)
        both = jnp.concatenate(
            [jnp.where(first_head, query, zero), jnp.where(first_head, zero, query)], 0
        )
        scores = dot_right(both, k_ref[0, :, columns]) + bias
        top = jnp.max(scores, -1, keepdims=True)
        expo = jnp.exp(scores - top)
        total = jnp.sum(expo, -1, keepdims=True)
        log_total = top + jnp.log(total)
        probs = (expo * (1.0 / total)).astype(bf16)
        mixed = dot(probs, v_ref[0, :, columns])
        mix_ref[0, :, columns] = jnp.where(first_head, mixed[:rows], mixed[rows:]).astype(bf16)
        log_totals = jnp.where(lane == 2 * pair, log_total[:rows], log_totals)
        log_totals = jnp.where(lane == 2 * pair + 1, log_total[rows:], log_totals)
    lse_ref[0] = jnp.transpose(log_totals)[:HEAD_ROWS]


def three_parts(value):
    parts = []
    for _ in range(3):
        parts.append(value.astype(bf16))
        value = value - parts[-1].astype(f32)
    return parts


def feed_kernel(
    place_ref, tok_ref, mix_ref, dy_ref, lse_ref, gain_ref,
    out_own, in_own, down_own, far_ref, near_ref,
    layer_ref, dx1_ref, do_ref, lo_ref, hi_ref, rows_ref, h2_ref, dup_ref, mid_ref, dmix_ref, gsum_ref,
    w_out, w_in, w_down,
):
    @pl.when(pl.program_id(0) == 0)
    def _():
        at = in_own.shape[0] // 2
        place_weight(place_ref, w_in, in_own, far_ref, near_ref)
        for whole, own in ((w_down, down_own), (w_out, out_own)):
            place_folded(place_ref, whole, own, far_ref, near_ref, at)
            at += own.shape[0] // 6
        gsum_ref[...] = jnp.zeros_like(gsum_ref)

    rows, width = tok_ref.shape
    ffn = w_down.shape[0]
    block = 2 * HALF_WINDOW
    after_attn = tok_ref[...].astype(f32) + dot(mix_ref[...], w_out[...])
    normed, factor = norm_parts(after_attn)
    gain = gain_ref[1:2, :].astype(f32)
    h2_ref[...] = (normed * gain).astype(bf16)
    step = 3 * PAIR
    for start in range(0, ffn, step):
        columns = slice(start, start + step)
        gates = slice(ffn + start, ffn + start + step)
        act_input = dot(h2_ref[...], w_in[:, columns])
        gate_part = dot(h2_ref[...], w_in[:, gates])
        grad_middle = dot_right(dy_ref[...], w_down[columns, :])
        share = 0.5 + 0.5 * lax.erf(act_input * root_half)
        act_value = act_input * share
        slope = share + act_input * (normal_peak * jnp.exp(-0.5 * act_input * act_input))
        mid_ref[:, columns] = (act_value * gate_part).astype(bf16)
        dup_ref[:, columns] = (grad_middle * gate_part * slope).astype(bf16)
        dup_ref[:, gates] = (grad_middle * act_value).astype(bf16)
    layer_ref[...] = (after_attn + dot(mid_ref[...], w_down[...])).astype(bf16)
    grad_hidden = dot_right(dup_ref[...], w_in[...])
    gain_terms = grad_hidden * normed
    gsum_ref[...] += jnp.sum(gain_terms.reshape(rows // 8, 8, width), 0)
    grad_stream = dy_ref[...].astype(f32) + norm_back(grad_hidden * gain, normed, factor)
    dx1_ref[...] = grad_stream
    dmix_ref[...] = grad_stream.astype(bf16)
    grad_mixed = dot_right(dmix_ref[...], w_out[...]).astype(bf16)
    do_ref[...] = grad_mixed
    products = grad_mixed.astype(f32) * mix_ref[...].astype(f32)
    high = products.astype(bf16)
    low = (products - high.astype(f32)).astype(bf16)
    head_of = lax.broadcasted_iota(jnp.int32, (width, PAIR), 0) // HEAD_DIM
    slot = lax.broadcasted_iota(jnp.int32, (width, PAIR), 1)
    pick = jnp.where(head_of == slot, 1.0, 0.0).astype(bf16)
    delta = dot(high, pick) + dot(low, pick)
    for i in range(rows // block):
        piece = grad_mixed[i * block : (i + 1) * block]
        inner_sum = jnp.transpose(delta[i * block : (i + 1) * block])[:HEAD_ROWS]
        rows_ref[i, :HEAD_ROWS] = inner_sum
        rows_ref[i, HEAD_ROWS:] = lse_ref[i]
        parts = jnp.concatenate(three_parts(lse_ref[i]) + three_parts(inner_sum), 1)
        for ref, own in ((lo_ref, piece[:HALF_WINDOW]), (hi_ref, piece[HALF_WINDOW:])):
            ref[i, :HALF_WINDOW] = own
            ref[i, HALF_WINDOW:] = parts


def pack_first_kernel(place_ref, qkv_ref, gain_ref, out_ref):
    half = qkv_ref.shape[0] // 2
    count, width = gain_ref.shape
    out_ref[:half] = qkv_ref[pl.ds(pl.multiple_of(place_ref[1] * half, half), half), :]
    out_ref[half:] = jnp.zeros_like(out_ref[half:])
    filler = jnp.zeros((out_ref.shape[0] - half - count, width), bf16)
    out_ref[half:, :width] = jnp.concatenate([gain_ref[...], filler], 0)


def pack_later_kernel(place_ref, out_w, in_w, down_w, tok_ref, later_ref, head_ref, tail_ref):
    core = place_ref[1]
    half = in_w.shape[0] // 2
    width = out_w.shape[1]
    later_ref[:half] = in_w[pl.ds(pl.multiple_of(core * half, half), half), :]
    at = half
    for ref in (down_w, out_w):
        third = ref.shape[0] // 6
        for i in range(3):
            first = pl.multiple_of((core * 3 + i) * third, third)
            later_ref[at : at + third, i * width : (i + 1) * width] = ref[pl.ds(first, third), :]
        at += third
    rows = tok_ref.shape[1]
    for i in range(tok_ref.shape[0]):
        head_ref[i] = tok_ref[i, :HALF_WINDOW]
        tail_ref[i] = tok_ref[i, rows - HALF_WINDOW :]


def part_rows(place_ref, whole, keep_ref, send_ref):
    rows = keep_ref.shape[1]
    core = place_ref[1]
    for i in range(2):
        keep_ref[i] = whole[pl.ds(pl.multiple_of((2 * i + core) * rows, 16), rows), :]
        send_ref[i] = whole[pl.ds(pl.multiple_of((2 * i + 1 - core) * rows, 16), rows), :]


def as_column(row_groups):
    ones = jnp.ones((row_groups.shape[0], PAIR), bf16)
    return sum(dot_left(part, ones) for part in three_parts(row_groups))


def grad_qkv_kernel(
    place_ref, left_ref, right_ref, gain_ref, two_ref, w_own, w_far, w_near,
    keep_ref, send_ref, whole, weight, terms,
):
    step = pl.program_id(0)

    @pl.when(step == 0)
    def _():
        place_weight(place_ref, weight, w_own, w_far, w_near)
        terms[...] = jnp.zeros_like(terms)

    grad = dot_left(left_ref[...], right_ref[...])
    whole[...] = grad.astype(bf16)
    width = whole.shape[1]
    for start in range(0, weight.shape[1], width):
        size = min(width, weight.shape[1] - start)

        @pl.when(step == start // width)
        def _():
            total = terms[...]
            for at in range(0, size, PAIR):
                total += grad[:, at : at + PAIR] * weight[:, start + at : start + at + PAIR].astype(f32)
            terms[...] = total

    @pl.when(step == pl.num_programs(0) - 1)
    def _():
        lane = lax.broadcasted_iota(jnp.int32, (1, PAIR), 1)
        pick = jnp.where(lax.broadcasted_iota(jnp.int32, (2, PAIR), 0) == 0, 1.0, 0.0).astype(bf16)
        first = jnp.sum(terms[...], -1, keepdims=True) / dot_left(gain_ref[...], pick)
        second = as_column(two_ref[...])
        columns = jnp.where(lane == 0, first, jnp.where(lane == 1, second, 0.0)).astype(bf16)
        at = width - 2 * PAIR
        whole[:, at : at + PAIR] = columns
        whole[:, at + PAIR :] = jnp.zeros_like(columns)

    part_rows(place_ref, whole, keep_ref, send_ref)


def grads_kernel(place_ref, h2_ref, dup_ref, mid_ref, dy_ref, mix_ref, dmix_ref, keep_ref, send_ref, whole):
    step = pl.program_id(0)
    width = dy_ref.shape[1]
    half = whole.shape[0] // 2
    part = width // 2
    third = mid_ref.shape[1] // 2
    grad = dot_left(h2_ref[...], dup_ref[...]).astype(bf16)
    at = pl.multiple_of(step * part, part)
    whole[pl.ds(at, part), :] = grad[:part]
    whole[pl.ds(half + at, part), :] = grad[part:]
    grad = dot_left(mid_ref[...], dy_ref[...]).astype(bf16)
    for i in range(2):
        index = 2 * step + i
        owner = index // 3
        at = pl.multiple_of(owner * half + 3 * part + (index - 3 * owner) * third, 64)
        whole[pl.ds(at, third), :] = grad[i * third : (i + 1) * third]
    grad = dot_left(mix_ref[...], dmix_ref[...]).astype(bf16)
    columns = pl.ds(pl.multiple_of(step * (width // 3), PAIR), width // 3)
    at = 3 * part + 3 * third
    whole[at : at + part, columns] = grad[:part]
    whole[half + at : half + at + part, columns] = grad[part:]

    @pl.when(step == pl.num_programs(0) - 1)
    def _():
        spare = half - at - part
        if spare:
            for start in (at + part, half + at + part):
                whole[start : start + spare] = jnp.zeros((spare, width), bf16)
        part_rows(place_ref, whole, keep_ref, send_ref)


def total_of(*values):
    total = values[0].astype(f32)
    for value in values[1:]:
        total += value.astype(f32)
    return total.astype(bf16)


def split_first_kernel(place_ref, held, got, hold_y, send_y, hold_x, send_x):
    owner, bit = place_ref[0], place_ref[2]
    width = held.shape[2] // 2
    for j in range(2):
        for to, ref in ((owner, hold_y), (1 - owner, send_y)):
            ref[j] = total_of(held[2 * to + j, :, :width], got[2 * to + j, :, :width])
        for to, ref in ((bit, hold_x), (1 - bit, send_x)):
            ref[j] = total_of(held[2 * j + to, :, width:], got[2 * j + to, :, width:])


def split_second_kernel(place_ref, hold_y, got_y, hold_x, got_x, keep, send_x, send_y):
    owner, bit = place_ref[0], place_ref[2]
    width = hold_y.shape[2]
    keep[:, :width] = total_of(hold_y[bit], got_y[bit])
    send_x[...] = total_of(hold_y[1 - bit], got_y[1 - bit])
    keep[:, width:] = total_of(hold_x[owner], got_x[owner])
    send_y[...] = total_of(hold_x[1 - owner], got_x[1 - owner])


def split_third_kernel(place_ref, held, got_left, got_right, *refs, slot):
    index = place_ref[slot]
    width = got_left.shape[2]
    for d, ref in enumerate(refs):
        ref[:, :width] = total_of(held[index ^ d, :, :width], got_left[index ^ d])
        ref[:, width:] = total_of(held[index ^ d, :, width:], got_right[index ^ d])


def sum_cut_kernel(place_ref, held, *refs, slot, arrived):
    index = place_ref[slot]
    for d, out_ref in enumerate(refs[arrived:]):
        total = held[index ^ d].astype(f32)
        for got in refs[:arrived]:
            total += got[index ^ d].astype(f32)
        out_ref[...] = total.astype(bf16)


def join_kernel(place_ref, *refs, slot):
    index = place_ref[slot]
    for d, ref in enumerate(refs[:-1]):
        refs[-1][index ^ d] = ref[...]


def attend_back_kernel(
    q_ref, k_ref, v_ref, do_ref, do_before, do_after, own_rows, rows_before, rows_after,
    bias_ref, bias_edge, cos_ref, sin_ref, *refs,
):
    out_ref, mark_ref = refs[-2:]
    mark_ref[...] = jnp.zeros_like(mark_ref)
    rows, width = do_ref.shape[1], do_ref.shape[2]
    out_ref[0, :, 3 * width :] = jnp.zeros((rows, 2 * PAIR), bf16)
    inner = slice(HALF_WINDOW, HALF_WINDOW + rows)
    lane = lax.broadcasted_iota(jnp.int32, (1, PAIR), 1)
    first_half = (lane % HEAD_DIM) < HEAD_DIM // 2
    first_head = lane < HEAD_DIM
    top_rows = lax.broadcasted_iota(jnp.int32, (PAIR, 1), 0) < HEAD_DIM
    cosine, sine = cos_ref[0, inner], sin_ref[0, inner]
    bias = jnp.concatenate([bias_ref[0], bias_ref[0]], 1)
    offsets_edge = jnp.concatenate([bias_edge[0], bias_edge[0]], 1)

    def split(value):
        zero = jnp.zeros_like(value)
        return jnp.concatenate(
            [jnp.where(first_head, value, zero), jnp.where(first_head, zero, value)], 0
        )

    after_lane = lane < HALF_WINDOW
    edge = []
    for base in (3 * PAIR, 0):
        value = jnp.zeros((HEAD_ROWS, PAIR), f32)
        for at in (base, base + PAIR, base + 2 * PAIR):
            columns = slice(at, at + PAIR)
            value += jnp.where(
                after_lane, rows_after[0, :, columns].astype(f32), rows_before[0, :, columns].astype(f32)
            )
        edge.append(value)
    edge_sum, edge_lse = edge
    own_sum, own_lse = own_rows[0, :HEAD_ROWS], own_rows[0, HEAD_ROWS:]

    def row_of(value, pair):
        at = 2 * pair
        return jnp.concatenate([value[at : at + 1, :], value[at + 1 : at + 2, :]], 1)

    def back(keys, values, query, grad_mixed, offsets, log_total, inner_sum):
        probs = jnp.exp(dot_right(keys, query) + offsets - log_total)
        grad_probs = dot_right(values, grad_mixed)
        return probs.astype(bf16), (probs * (grad_probs - inner_sum)).astype(bf16)

    def rotated_back(value):
        return value * cosine - half_swap(value, first_half) * sine

    for pair in range(width // PAIR):
        columns = slice(pair * PAIR, (pair + 1) * PAIR)
        keys, values = k_ref[0, :, columns], v_ref[0, :, columns]
        query = split(q_ref[0, inner, columns])
        grad_mixed = split(do_ref[0, :, columns])
        probs, grad_scores = back(
            keys, values, query, grad_mixed, bias,
            row_of(own_lse, pair), row_of(own_sum, pair),
        )
        query_edge = split(
            jnp.concatenate(
                [
                    q_ref[0, HALF_WINDOW + rows :, columns],
                    q_ref[0, :HALF_WINDOW, columns],
                ],
                0,
            )
        )
        grad_edge = split(jnp.concatenate([do_after[0, :, columns], do_before[0, :, columns]], 0))
        probs_edge, scores_edge = back(
            keys[inner], values[inner], query_edge, grad_edge, offsets_edge,
            row_of(edge_lse, pair), row_of(edge_sum, pair),
        )
        grad_values = dot(
            jnp.concatenate([probs[inner], probs_edge], 1),
            jnp.concatenate([grad_mixed, grad_edge], 0),
        )
        grad_keys = dot(
            jnp.concatenate([grad_scores[inner], scores_edge], 1),
            jnp.concatenate([query, query_edge], 0),
        )
        grad_query = dot_left(grad_scores, keys)
        grad_query = jnp.where(first_head, grad_query[:rows], grad_query[rows:]) * HEAD_DIM**-0.5
        out_ref[0, :, columns] = rotated_back(grad_query).astype(bf16)
        out_ref[0, :, width + pair * PAIR : width + (pair + 1) * PAIR] = rotated_back(
            grad_keys
        ).astype(bf16)
        out_ref[0, :, 2 * width + pair * PAIR : 2 * width + (pair + 1) * PAIR] = (
            grad_values.astype(bf16)
        )


def stream_back_kernel(
    place_ref, dqkv_ref, tok_ref, dx1_ref, gain_ref, w_own, w_far, w_near, out_ref, weight
):
    @pl.when(pl.program_id(0) == 0)
    def _():
        place_weight(place_ref, weight, w_own, w_far, w_near)

    grad_hidden = dot_right(dqkv_ref[...], weight[...])
    normed, factor = norm_parts(tok_ref[...].astype(f32))
    grad_normed = grad_hidden * gain_ref[0:1, :].astype(f32)
    out_ref[...] = (dx1_ref[...] + norm_back(grad_normed, normed, factor)).astype(bf16)


def join_halves(place_ref, whole, mine, other):
    rows = mine.shape[0]
    core = place_ref[1]
    whole[pl.ds(pl.multiple_of(core * rows, 16), rows), :] = mine[...]
    whole[pl.ds(pl.multiple_of((1 - core) * rows, 16), rows), :] = other[...]


def finish_qkv_kernel(place_ref, mine, other, out_ref, gain_ref, columns):
    rows = mine.shape[0]
    core = place_ref[1]
    width = out_ref.shape[1]
    for ref, at in ((mine, core * rows), (other, (1 - core) * rows)):
        at = pl.ds(pl.multiple_of(at, 16), rows)
        out_ref[at, :] = ref[:, :width].astype(f32)
        columns[at, :] = ref[:, width : width + PAIR].astype(f32)
    gain_ref[...] = columns[...].T[: gain_ref.shape[0]]


def finish_three_kernel(place_ref, mine, other, in_ref, down_ref, out_ref, whole):
    join_halves(place_ref, whole, mine, other)
    width = whole.shape[1]
    at = 0
    for i in range(in_ref.shape[1] // width):
        in_ref[:, i * width : (i + 1) * width] = whole[at : at + in_ref.shape[0]].astype(f32)
        at += in_ref.shape[0]
    for ref in (down_ref, out_ref):
        ref[...] = whole[at : at + ref.shape[0]].astype(f32)
        at += ref.shape[0]


def shape_of(*dims, dtype=bf16):
    return jax.ShapeDtypeStruct(dims, dtype)


def whole_spec(array):
    return pl.BlockSpec(array.shape, lambda i: (0,) * array.ndim)


def run(kernel, grid, inputs, outputs, scratch=(), aliases=None, later=(), spare=4):
    first = len(inputs)
    later = jax.tree.leaves(later)
    inputs = [*inputs, *[(x, pl.ANY) for x in later]]

    def body(*refs):
        kernel(*refs[:first], *refs[first + len(later) :])

    def spec(block, place):
        return pl.BlockSpec(block, place)

    specs = []
    for item in inputs:
        if item[1] is None and item[0].dtype == jnp.int32:
            specs.append(pl.BlockSpec(memory_space=pltpu.SMEM))
        elif item[1] is pl.ANY:
            specs.append(pl.BlockSpec(memory_space=pl.ANY))
        elif item[1] is None:
            specs.append(whole_spec(item[0]))
        else:
            specs.append(spec(item[1], item[2]))
    held = sum(
        math.prod(x[1] or x[0].shape) * x[0].dtype.itemsize
        for x in (*inputs, *outputs)
        if x[1] is not pl.ANY
    )
    kept = sum(math.prod(x.shape) * jnp.dtype(x.dtype).itemsize for x in scratch)
    out_specs = [whole_spec(o[0]) if o[1] is None else spec(o[1], o[2]) for o in outputs]
    return pl.pallas_call(
        body,
        grid=(grid,),
        in_specs=specs,
        out_specs=out_specs,
        out_shape=[o[0] for o in outputs],
        scratch_shapes=list(scratch),
        input_output_aliases=aliases or {},
        cost_estimate=pl.CostEstimate(flops=1, bytes_accessed=1, transcendentals=0),
        compiler_params=pltpu.CompilerParams(
            dimension_semantics=("arbitrary",),
            vmem_limit_bytes=min(56 * MIB, 2 * held + kept + spare * MIB),
        ),
    )(*[x[0] for x in inputs])


def flip_route(size, bit):
    return [(i, i ^ bit) for i in range(size)]


def swap_half(half):
    return lax.ppermute(half, "seq", flip_route(lax.axis_size("seq"), 1))


def exchange(block, distance):
    if distance == 0:
        return lax.ppermute(block, "fsdp", flip_route(2, 1))
    return lax.ppermute(block, "seq", flip_route(lax.axis_size("seq"), distance))


def together(*values):
    return lax.optimization_barrier(values)


def column_steps(rows, columns):
    return 3 if rows * columns > 400_000 and columns % (3 * PAIR) == 0 else 1


def sum_cut(place, slot, held, gots, later):
    parts, rows, columns = held.shape
    return run(
        partial(sum_cut_kernel, slot=slot, arrived=len(gots)),
        1,
        [(place, None), *[(x, None) for x in (held, *gots)]],
        [(shape_of(rows, columns), None) for _ in range(parts)],
        later=later,
    )


def split_run(kernel, place, rows, inputs, outputs, later):
    steps = 3 if rows % 48 == 0 else 1

    def item(array):
        block = (*array.shape[:-2], rows // steps, array.shape[-1])
        lead = (0,) * (len(block) - 2)
        return (array, block, lambda i: (*lead, i, 0))

    return run(kernel, steps, [(place, None), *map(item, inputs)], [item(x) for x in outputs], later=later)


def join(place, slot, parts, later):
    rows, columns = parts[0].shape
    steps = column_steps(len(parts) * rows, columns)
    (whole,) = run(
        partial(join_kernel, slot=slot),
        steps,
        [(place, None), *[(x, (rows, columns // steps), lambda i: (0, i)) for x in parts]],
        [
            (
                shape_of(len(parts), rows, columns),
                (len(parts), rows, columns // steps),
                lambda i: (0, 0, i),
            )
        ],
        later=later,
    )
    return whole.reshape(len(parts) * rows, columns)


def bit_groups():
    stages = (lax.axis_size("seq") - 1).bit_length()
    return [(0, 1), (1, 1)] + [(at, min(2, stages - at)) for at in range(2, stages, 2)]


def member(group):
    at, bits = group
    return (lax.axis_index("seq") >> at) & ((1 << bits) - 1)


def sum_stages(place, keep, send):
    (got,), later = yield [(send, 1)]
    rows, columns = keep.shape[1] // 2, keep.shape[2]
    four = (4, rows, columns)
    part = shape_of(2, rows, columns // 2)
    hold_y, send_y, hold_x, send_x = split_run(
        split_first_kernel, place, rows, [keep.reshape(four), got.reshape(four)], [part] * 4,
        later,
    )
    (got_y, got_x), later = yield [(send_y, 0), (send_x, 2)]
    block, send_x, send_y = split_run(
        split_second_kernel,
        place,
        rows,
        [hold_y, got_y, hold_x, got_x],
        [shape_of(rows, columns), *[shape_of(rows, columns // 2)] * 2],
        later,
    )
    arrived, later = yield [(send_x, 2), (send_y, 0)]
    groups = list(enumerate(bit_groups()[2:], 3))
    for step, (slot, group) in enumerate(groups):
        count = 1 << group[1]
        size = block.shape[0] // count
        if step == 0:
            block, *sends = run(
                partial(split_third_kernel, slot=slot),
                1,
                [
                    (place, None),
                    *[(x.reshape(count, size, x.shape[1]), None) for x in (block, *arrived)],
                ],
                [(shape_of(size, columns), None) for _ in range(count)],
                later=later,
            )
        else:
            shape = (count, size, columns)
            block, *sends = sum_cut(
                place, slot, block.reshape(shape), [x.reshape(shape) for x in arrived], later
            )
        arrived, later = yield [(x, (d + 1) << group[0]) for d, x in enumerate(sends)]
    (block,) = sum_cut(place, len(groups) + 3, block[None], [x[None] for x in arrived], later)
    for slot, group in reversed([(2, (1, 1)), *groups]):
        held, later = yield [(block, d << group[0]) for d in range(1, 1 << group[1])]
        block = join(place, slot, [block, *held], later)
    (other,), _ = yield [(block, 1)]
    return block, other


class Chain:
    def __init__(self, stages):
        self.stages, self.result = stages, None
        self.post(next(stages))

    def post(self, sends, gate=None, arrived=0):
        blocks = [block for block, _ in sends]
        if gate is not None:
            held = together(*blocks, *gate.got[:arrived])
            blocks = list(held[: len(blocks)])
            gate.got[:arrived] = held[len(blocks) :]
        self.sent = blocks
        self.got = [exchange(block, distance) for block, (_, distance) in zip(blocks, sends)]

    def advance(self, *later, gate=None, arrived=0):
        try:
            self.post(self.stages.send((self.got, later)), gate, arrived)
        except StopIteration as end:
            self.result = end.value
        return self.sent


def window_tables(pos, rows, head_width):
    half = head_width // 2
    freqs = 10000.0 ** (-(jnp.arange(half, dtype=f32) * 2.0 / head_width))
    angle = pos.astype(f32)[..., None] * freqs
    cosine, sine = jnp.cos(angle), jnp.sin(angle)
    cosine = jnp.concatenate([cosine] * 4, -1)
    sine = jnp.concatenate([-sine, sine, -sine, sine], -1)
    span = pos.shape[1]
    index = jnp.arange(span, dtype=jnp.int32)

    def offsets(query_pos, query_index, key_pos, key_index):
        gap = key_index - query_index
        allowed = (
            (jnp.abs(gap) <= HALF_WINDOW)
            & (key_pos >= 0)
            & (query_pos >= 0)
            & ((gap > 0) | (query_pos >= -gap))
            & ((gap <= 0) | (key_pos >= gap))
        )
        return jnp.where(allowed, 0.0, masked_score).astype(f32)

    inner = slice(HALF_WINDOW, HALF_WINDOW + rows)
    outer_pos = jnp.concatenate([pos[:, HALF_WINDOW + rows :], pos[:, :HALF_WINDOW]], 1)
    outer_index = jnp.concatenate([index[HALF_WINDOW + rows :], index[:HALF_WINDOW]])
    bias = offsets(
        pos[:, inner, None], index[None, inner, None], pos[:, None, :], index[None, None, :]
    )
    bias_t = offsets(
        pos[:, None, inner], index[None, None, inner], pos[:, :, None], index[None, :, None]
    )
    bias_edge = offsets(
        outer_pos[:, None, :],
        outer_index[None, None, :],
        pos[:, inner, None],
        index[None, inner, None],
    )
    return cosine, sine, bias, bias_t, bias_edge


def local(tokens, positions, qkv_weight, out_weight, in_weight, down_weight, norm_gains, cotangent):
    num_seqs, rows, width = tokens.shape
    span = rows + 2 * HALF_WINDOW
    count = num_seqs * rows
    ffn = 2 * down_weight.shape[0]
    seq_index, own_y = lax.axis_index("seq"), lax.axis_index("fsdp")
    place = jnp.stack(
        [own_y, seq_index % 2, *[member(group) for group in bit_groups()[1:]], 0 * own_y]
    ).astype(jnp.int32)

    gain_width = norm_gains.shape[1]
    half = qkv_weight.shape[0] // 2
    (first_half,) = run(
        pack_first_kernel,
        1,
        [(place, None), (qkv_weight, None), (norm_gains, None)],
        [(shape_of(half + 16, qkv_weight.shape[1]), None)],
        spare=56,
    )
    far_qkv = exchange(first_half, 0)
    later_rows = half + down_weight.shape[0] // 6 + out_weight.shape[0] // 6
    halo = shape_of(num_seqs, HALF_WINDOW, width)
    later_half, tok_head, tok_tail = run(
        pack_later_kernel,
        1,
        [
            (place, None),
            *[(x, None) for x in (out_weight, in_weight, down_weight)],
            (tokens, None),
        ],
        [(shape_of(later_rows, in_weight.shape[1]), None), (halo, None), (halo, None)],
        later=first_half,
        spare=56,
    )
    far_later = exchange(later_half, 0)
    tok_before = passed_along(tok_tail, "seq", 1)
    tok_after = passed_along(tok_head, "seq", -1)
    padded_pos = jnp.pad(positions, ((0, 0), (HALF_WINDOW, HALF_WINDOW)), constant_values=-1)
    key_pos = lax.dynamic_slice_in_dim(padded_pos, seq_index * rows, span, 1)
    cosine, sine, bias, bias_t, bias_edge = window_tables(key_pos, rows, HEAD_DIM)
    far_qkv, tok_before, tok_after, cosine, sine, bias, bias_t, bias_edge = together(
        far_qkv, tok_before, tok_after, cosine, sine, bias, bias_t, bias_edge
    )
    w_qkv = (qkv_weight, far_qkv, swap_half(far_qkv))
    gains_other = far_qkv[qkv_weight.shape[0] // 2 :, :gain_width][: norm_gains.shape[0]]
    gains = jnp.where(
        own_y == 0,
        jnp.concatenate([norm_gains, gains_other], 1),
        jnp.concatenate([gains_other, norm_gains], 1),
    )

    def per_seq(i):
        return (i, 0, 0)

    def row_block(i):
        return (i, 0)

    def column_block(i):
        return (0, i)

    qkv_pieces = [(piece, None) for piece in w_qkv]
    wide = (1, span, width)
    hidden_one, query, keys, values, mixed, log_total = run(
        attend_kernel,
        num_seqs,
        [
            (place, None),
            (tok_before, (1, HALF_WINDOW, width), per_seq),
            (tokens, (1, rows, width), per_seq),
            (tok_after, (1, HALF_WINDOW, width), per_seq),
            (cosine, (1, span, PAIR), per_seq),
            (sine, (1, span, PAIR), per_seq),
            (bias, (1, rows, span), per_seq),
            (gains, None),
            *qkv_pieces,
        ],
        [
            (shape_of(num_seqs, rows, width), (1, rows, width), per_seq),
            (shape_of(num_seqs, span, width), wide, per_seq),
            (shape_of(num_seqs, span, width), wide, per_seq),
            (shape_of(num_seqs, span, width), wide, per_seq),
            (shape_of(num_seqs, rows, width), (1, rows, width), per_seq),
            (shape_of(num_seqs, HEAD_ROWS, PAIR, dtype=f32), (1, HEAD_ROWS, PAIR), per_seq),
        ],
        [pltpu.VMEM((width, 3 * width), bf16)],
        spare=56,
    )
    far_later, mixed = together(far_later, mixed)
    near_later = swap_half(far_later)

    flat_tokens = tokens.reshape(count, width)
    flat_dy = cotangent.reshape(count, width)
    flat_mixed = mixed.reshape(count, width)
    step = 2 * rows
    tok_block = (step, width)
    pack = HALF_WINDOW + HEAD_ROWS
    half_block = (2, pack, width)
    (
        layer_out, grad_stream, grad_mixed, grad_lo, grad_hi, inner_sum,
        hidden_two, grad_up, middle, grad_attn, gain_sum_two,
    ) = run(
        feed_kernel,
        count // step,
        [
            (place, None),
            (flat_tokens, tok_block, row_block),
            (flat_mixed, tok_block, row_block),
            (flat_dy, tok_block, row_block),
            (log_total, (2, HEAD_ROWS, PAIR), per_seq),
            (gains, None),
            *[(x, None) for x in (out_weight, in_weight, down_weight, far_later, near_later)],
        ],
        [
            (shape_of(count, width), tok_block, row_block),
            (shape_of(count, width, dtype=f32), tok_block, row_block),
            (shape_of(count, width), tok_block, row_block),
            (shape_of(num_seqs, pack, width), half_block, per_seq),
            (shape_of(num_seqs, pack, width), half_block, per_seq),
            (shape_of(num_seqs, 2 * HEAD_ROWS, PAIR, dtype=f32), (2, 2 * HEAD_ROWS, PAIR), per_seq),
            (shape_of(count, width), tok_block, row_block),
            (shape_of(count, 2 * ffn), (step, 2 * ffn), row_block),
            (shape_of(count, ffn), (step, ffn), row_block),
            (shape_of(count, width), tok_block, row_block),
            (shape_of(8, width, dtype=f32), None),
        ],
        [
            pltpu.VMEM((width, width), bf16),
            pltpu.VMEM((width, 2 * ffn), bf16),
            pltpu.VMEM((ffn, width), bf16),
        ],
        spare=56,
    )
    do_before = passed_along(grad_hi, "seq", 1)
    do_after = passed_along(grad_lo, "seq", -1)

    size = max(lax.axis_size("seq"), PAIR)
    bundle_rows = -(-(3 * width // 2 + ffn // 2 + width // 2) // size) * size
    bundle_part = shape_of(2, bundle_rows // 2, width)
    keep, send = run(
        grads_kernel,
        3,
        [
            (place, None),
            (hidden_two, None),
            (grad_up, (count, 2 * ffn // 3), column_block),
            (middle, (count, ffn // 3), column_block),
            (flat_dy, None),
            (flat_mixed, None),
            (grad_attn, (count, width // 3), column_block),
        ],
        [(bundle_part, None), (bundle_part, None)],
        [pltpu.VMEM((2 * bundle_rows, width), bf16)],
        spare=56,
    )
    do_before, do_after, send = together(do_before, do_after, send)
    chain_mlp = Chain(sum_stages(place, keep, send))
    heads = (1, 2 * HEAD_ROWS, PAIR)
    half_part = (1, HALF_WINDOW, width)
    edge_pack = (1, HEAD_ROWS, width)

    wider = 3 * width + 2 * PAIR

    def back_part(first, many, later, earlier=None):
        def at(i):
            return (first + i, 0, 0)

        def pack_rows(i):
            return (first + i, HALF_WINDOW // HEAD_ROWS, 0)

        return run(
            attend_back_kernel,
            many,
            [
                (query, wide, at),
                (keys, wide, at),
                (values, wide, at),
                (grad_mixed.reshape(num_seqs, rows, width), (1, rows, width), at),
                (do_before, half_part, at),
                (do_after, half_part, at),
                (inner_sum, heads, at),
                (do_before, edge_pack, pack_rows),
                (do_after, edge_pack, pack_rows),
                (bias_t, (1, span, rows), at),
                (bias_edge, (1, rows, PAIR), at),
                (cosine, (1, span, PAIR), at),
                (sine, (1, span, PAIR), at),
                *([] if earlier is None else [(earlier, pl.ANY)]),
            ],
            [
                (shape_of(num_seqs, rows, wider), (1, rows, wider), at),
                (shape_of(8, PAIR, dtype=f32), None),
            ],
            aliases=None if earlier is None else {13: 0},
            later=later,
            spare=56,
        )

    few = num_seqs // 2
    grads, mark = back_part(0, few, ())
    grads, _ = back_part(few, num_seqs - few, chain_mlp.advance(mark), grads)
    flat_grad = grads.reshape(count, wider)
    step_columns = wider // 2
    part = shape_of(2, width // 4, wider)
    block = (2, width // 4, step_columns)

    def last_block(i):
        return (0, 0, i)

    keep, send = run(
        grad_qkv_kernel,
        wider // step_columns,
        [
            (place, None),
            (hidden_one.reshape(count, width), None),
            (flat_grad, (count, step_columns), column_block),
            (gains, None),
            (gain_sum_two, None),
            *qkv_pieces,
        ],
        [(part, block, last_block), (part, block, last_block)],
        [
            pltpu.VMEM((width, step_columns), bf16),
            pltpu.VMEM((width, 3 * width), bf16),
            pltpu.VMEM((width, PAIR), f32),
        ],
        spare=16,
    )
    send, *chain_mlp.got = together(send, *chain_mlp.got)
    chain_qkv = Chain(sum_stages(place, keep, send))
    sent = chain_mlp.advance(keep)
    sent = chain_qkv.advance(sent)
    sent = chain_mlp.advance(sent)
    large = 4 * rows
    (grad_tokens,) = run(
        stream_back_kernel,
        count // large,
        [
            (place, None),
            (flat_grad, (large, 3 * width), row_block),
            (flat_tokens, (large, width), row_block),
            (grad_stream, (large, width), row_block),
            (gains, None),
            *qkv_pieces,
        ],
        [(shape_of(count, width), (large, width), row_block)],
        [pltpu.VMEM((width, 3 * width), bf16)],
        later=sent,
        spare=12,
    )
    sent = chain_qkv.advance(grad_tokens, gate=chain_mlp, arrived=2)
    sent = chain_mlp.advance(sent)
    for _ in range(2 * len(bit_groups()) - 5):
        sent = chain_qkv.advance(sent)
        sent = chain_mlp.advance(sent, gate=chain_qkv, arrived=len(chain_qkv.got))
    sent = chain_qkv.advance(sent)
    sent = chain_qkv.advance(sent)
    while chain_mlp.result is None:
        chain_mlp.advance(sent)
    in_sum, down_sum, out_sum = run(
        finish_three_kernel,
        1,
        [(place, None), *[(x, None) for x in chain_mlp.result]],
        [
            (shape_of(*in_weight.shape, dtype=f32), None),
            (shape_of(*down_weight.shape, dtype=f32), None),
            (shape_of(*out_weight.shape, dtype=f32), None),
        ],
        [pltpu.VMEM((bundle_rows, width), bf16)],
        later=sent,
    )
    sent = down_sum
    while chain_qkv.result is None:
        sent = chain_qkv.advance(sent)
    qkv_sum, gains_sum = run(
        finish_qkv_kernel,
        1,
        [(place, None), *[(x, None) for x in chain_qkv.result]],
        [
            (shape_of(*qkv_weight.shape, dtype=f32), None),
            (shape_of(*norm_gains.shape, dtype=f32), None),
        ],
        [pltpu.VMEM((qkv_weight.shape[0], PAIR), f32)],
    )
    return (
        layer_out.reshape(tokens.shape),
        grad_tokens.reshape(tokens.shape),
        qkv_sum,
        out_sum,
        in_sum,
        down_sum,
        gains_sum,
    )


def solution(mesh):
    in_specs = (
        P("fsdp", "seq", None),
        P("fsdp", None),
        P("fsdp", None),
        P("fsdp", None),
        P("fsdp", None),
        P("fsdp", None),
        P(None, "fsdp"),
        P("fsdp", "seq", None),
    )
    out_specs = (
        P("fsdp", "seq", None),
        P("fsdp", "seq", None),
        P("fsdp", None),
        P("fsdp", None),
        P("fsdp", None),
        P("fsdp", None),
        P(None, "fsdp"),
    )
    return jax.shard_map(local, mesh=mesh, in_specs=in_specs, out_specs=out_specs, check_vma=False)
```
